512 devices in a mesh: gx: 32 (over x, y), gy: 16 (over z, core).
Axes of the slice: x: 4, y: 8, z: 8, core: 2. Of those that a mesh axis runs over, the one named last changes fastest.
Arguments:
- features: bfloat16 [64, 64, 128, 32], P(None, 'gx', 'gy'), may hold values from -6 to 6
- encoder_weight: bfloat16 [27, 64, 64], replicated, may hold values from -0.15625 to 0.15625
- lower_weight: bfloat16 [27, 128, 64], replicated, may hold values from -0.15625 to 0.15625
- lift_weight: bfloat16 [8, 64, 128], replicated, may hold values from -0.5 to 0.5
- decoder_weight: bfloat16 [27, 64, 128], replicated, may hold values from -0.109375 to 0.109375
- cotangent: bfloat16 [64, 64, 128, 32], P(None, 'gx', 'gy'), may hold values from -6 to 6
Outputs:
- decoded: bfloat16 [64, 64, 128, 32], P(None, 'gx', 'gy')
- input_gradient: bfloat16 [64, 64, 128, 32], P(None, 'gx', 'gy')
- encoder_gradient: float32 [27, 64, 64], replicated
- lower_gradient: float32 [27, 128, 64], replicated
- lift_gradient: float32 [8, 64, 128], replicated
- decoder_gradient: float32 [27, 64, 128], replicated
The draws below stay inside these ranges and needn't reach their ends.
All inputs are finite; a program needn't handle non-finite values.
Results may differ from the reference program's by a relative error of at most 0.014.
Values may be sent and summed in bfloat16 or wider, within the bound.
No kernel may reach another device: no remote copies, remote signals or barrier semaphores. Data moves between devices by JAX's collectives and lax.ppermute only.
A program may use at most 64 MiB of HBM per device.

```python
import jax
import jax.numpy as jnp

C_TOP = 64
C_DEEP = 128
NZ = 32
NX = 64
NY = 128


def shard_levels(own_key, extent, split, low, top_value):
    loudness = 1.0
    for dim, shards_of in split:
        heights = jax.random.uniform(jax.random.fold_in(jax.random.fold_in(own_key, 6), dim), (shards_of,), jnp.float32, low / len(split), top_value / len(split))
        loudness = loudness * jnp.repeat(jnp.exp(heights), extent[dim] // shards_of).reshape((-1,) + (1,) * (len(extent) - 1 - dim))
    return loudness


def centred(stream_key, shape, spread, most, pieces=(), kind=jnp.bfloat16):
    entries = jax.random.normal(stream_key, shape, jnp.float32) * spread
    if len(pieces) > 0:
        entries = shard_levels(stream_key, shape, pieces, -0.22, 0.18) * entries
    return jnp.clip(entries, min=-most, max=most).astype(kind)


def setup_inputs(seed: int = 0) -> dict:
    arg_keys = jax.random.split(jax.random.key(seed), 7)
    return {
        "features": centred(arg_keys[0], (C_TOP, NX, NY, NZ), 1.0, 6.0, ((1, 32), (2, 16))),
        "encoder_weight": centred(arg_keys[1], (27, C_TOP, C_TOP), (27 * C_TOP) ** -0.5, 0.15625),
        "lower_weight": centred(arg_keys[2], (27, C_DEEP, C_TOP), (27 * C_TOP) ** -0.5, 0.15625),
        "lift_weight": centred(arg_keys[3], (8, C_TOP, C_DEEP), C_DEEP ** -0.5, 0.5),
        "decoder_weight": centred(arg_keys[4], (27, C_TOP, 2 * C_TOP), (54 * C_TOP) ** -0.5, 0.109375),
        "cotangent": centred(arg_keys[5], (C_TOP, NX, NY, NZ), 1.0, 6.0, ((1, 32), (2, 16))),
    }


OFFSETS = tuple((shift_x, shift_y, shift_z) for shift_x in range(3) for shift_y in range(3) for shift_z in range(3))


def pad_volume(field):
    return jnp.pad(field.astype(jnp.float32), ((0, 0), (1, 1), (1, 1), (1, 1)))


def apply_taps(padded, weight, shape):
    size_x, size_y, size_z = shape
    total = jnp.zeros((weight.shape[1], size_x, size_y, size_z), jnp.float32)
    for tap_index, (shift_x, shift_y, shift_z) in enumerate(OFFSETS):
        window = padded[:, shift_x:shift_x + size_x, shift_y:shift_y + size_y, shift_z:shift_z + size_z]
        total = total + jnp.einsum("oc,cxyz->oxyz", weight[tap_index].astype(jnp.float32), window)
    return total


def apply_adjoint(padded, weight, shape):
    size_x, size_y, size_z = shape
    total = jnp.zeros((weight.shape[2], size_x, size_y, size_z), jnp.float32)
    for tap_index, (shift_x, shift_y, shift_z) in enumerate(OFFSETS):
        window = padded[:, 2 - shift_x:2 - shift_x + size_x, 2 - shift_y:2 - shift_y + size_y, 2 - shift_z:2 - shift_z + size_z]
        total = total + jnp.einsum("oc,oxyz->cxyz", weight[tap_index].astype(jnp.float32), window)
    return total


def tap_gradients(grad_out, padded, shape):
    size_x, size_y, size_z = shape
    grad_f = grad_out.astype(jnp.float32)
    result = []
    for shift_x, shift_y, shift_z in OFFSETS:
        window = padded[:, shift_x:shift_x + size_x, shift_y:shift_y + size_y, shift_z:shift_z + size_z]
        result.append(jnp.einsum("oxyz,cxyz->oc", grad_f, window))
    return jnp.stack(result, 0)


def silu_slope(value):
    sigma = jax.nn.sigmoid(value)
    return sigma * (1.0 + value * (1.0 - sigma))


def average_pool(field):
    chans, size_x, size_y, size_z = field.shape
    blocks = field.astype(jnp.float32).reshape(chans, size_x // 2, 2, size_y // 2, 2, size_z // 2, 2)
    return jnp.mean(blocks, axis=(2, 4, 6))


def spread_up(field):
    chans, size_x, size_y, size_z = field.shape
    wide = jnp.broadcast_to(field[:, :, None, :, None, :, None], (chans, size_x, 2, size_y, 2, size_z, 2))
    return wide.reshape(chans, 2 * size_x, 2 * size_y, 2 * size_z)


def lift_up(lower_act, lift_weight):
    chans, size_x, size_y, size_z = lower_act.shape
    taps = lift_weight.astype(jnp.float32).reshape(2, 2, 2, lift_weight.shape[1], lift_weight.shape[2])
    out = jnp.einsum("pqroc,cijk->oipjqkr", taps, lower_act.astype(jnp.float32))
    return out.reshape(lift_weight.shape[1], 2 * size_x, 2 * size_y, 2 * size_z)


def split_children(field):
    chans, size_x, size_y, size_z = field.shape
    return field.astype(jnp.float32).reshape(chans, size_x // 2, 2, size_y // 2, 2, size_z // 2, 2)


def lift_adjoint(lifted_grad, lift_weight):
    taps = lift_weight.astype(jnp.float32).reshape(2, 2, 2, lift_weight.shape[1], lift_weight.shape[2])
    return jnp.einsum("pqroc,oipjqkr->cijk", taps, split_children(lifted_grad))


def lift_outer(lifted_grad, lower_act):
    out = jnp.einsum("oipjqkr,cijk->pqroc", split_children(lifted_grad), lower_act.astype(jnp.float32))
    return out.reshape(8, out.shape[3], out.shape[4])


def reference(features, encoder_weight, lower_weight, lift_weight, decoder_weight, cotangent):
    fine_shape = (NX, NY, NZ)
    coarse_shape = (NX // 2, NY // 2, NZ // 2)
    channels = features.shape[0]
    feat_pad = pad_volume(features)
    encoder_pre = apply_taps(feat_pad, encoder_weight, fine_shape)
    encoded = jax.nn.silu(encoder_pre).astype(jnp.bfloat16)
    pooled = average_pool(encoded).astype(jnp.bfloat16)
    pool_pad = pad_volume(pooled)
    lower_pre = apply_taps(pool_pad, lower_weight, coarse_shape)
    lower_act = jax.nn.silu(lower_pre).astype(jnp.bfloat16)
    lifted = lift_up(lower_act, lift_weight).astype(jnp.bfloat16)
    joined = jnp.concatenate((encoded, lifted), 0)
    join_pad = pad_volume(joined)
    decoded = apply_taps(join_pad, decoder_weight, fine_shape).astype(jnp.bfloat16)
    joined_grad = apply_adjoint(pad_volume(cotangent), decoder_weight, fine_shape).astype(jnp.bfloat16)
    decoder_gradient = tap_gradients(cotangent, join_pad, fine_shape)
    lifted_grad = joined_grad[channels:]
    lower_grad = (lift_adjoint(lifted_grad, lift_weight) * silu_slope(lower_pre)).astype(jnp.bfloat16)
    lift_gradient = lift_outer(lifted_grad, lower_act)
    pooled_grad = apply_adjoint(pad_volume(lower_grad), lower_weight, coarse_shape).astype(jnp.bfloat16)
    lower_gradient = tap_gradients(lower_grad, pool_pad, coarse_shape)
    summed = joined_grad[:channels].astype(jnp.float32) + spread_up(pooled_grad.astype(jnp.float32)) / 8.0
    encoded_grad = (summed * silu_slope(encoder_pre)).astype(jnp.bfloat16)
    input_gradient = apply_adjoint(pad_volume(encoded_grad), encoder_weight, fine_shape).astype(jnp.bfloat16)
    encoder_gradient = tap_gradients(encoded_grad, feat_pad, fine_shape)
    return (decoded, input_gradient, encoder_gradient, lower_gradient, lift_gradient, decoder_gradient)
```

```python
import math

import jax
import jax.numpy as jnp
from jax import lax
from jax.experimental import pallas as pl
from jax.experimental.pallas import tpu as pltpu
from jax.sharding import Mesh, PartitionSpec as P

F32, BF16 = jnp.float32, jnp.bfloat16
LINK = BF16
GX, GY = ("gx",), ("gz", "gc")
TAPS9 = tuple((a, b) for a in range(3) for b in range(3))


def shifted(piece, axes, step):
    size = math.prod(lax.axis_size(axis) for axis in axes)
    pairs = [(i, i + step) for i in range(size) if 0 <= i + step < size]
    return lax.ppermute(piece, axes, pairs)


def swapped(low, high, axes):
    return shifted(high, axes, 1), shifted(low, axes, -1)


def partner(piece):
    return lax.ppermute(piece, "gc", [(0, 1), (1, 0)])


def call(kernel, outs, scratch, operands, spaces=(), flops=10**6):
    return pl.pallas_call(
        kernel,
        out_shape=[jax.ShapeDtypeStruct(s, d) for s, d in outs],
        in_specs=[
            pl.BlockSpec(memory_space=dict(spaces).get(i, pltpu.VMEM)) for i in range(len(operands))
        ],
        out_specs=[pl.BlockSpec(memory_space=pltpu.VMEM)] * len(outs),
        scratch_shapes=[s if d is None else pltpu.VMEM(s, d) for s, d in scratch],
        compiler_params=pltpu.CompilerParams(vmem_limit_bytes=40 * 2**20),
        cost_estimate=pl.CostEstimate(flops=flops, bytes_accessed=10**4, transcendentals=0),
    )(*operands)


def nn(a, b):
    return lax.dot_general(a, b, (((1,), (0,)), ((), ())), preferred_element_type=F32)


def nt(a, b):
    return lax.dot_general(a, b, (((1,), (1,)), ((), ())), preferred_element_type=F32)


def tn(a, b):
    return lax.dot_general(a, b, (((0,), (0,)), ((), ())), preferred_element_type=F32)


def nn_weight(ref):
    rows = [jnp.concatenate([ref[3 * ab + c] for c in range(3)], -1) for ab in range(9)]
    return jnp.concatenate(rows, 0)


def nt_weight(ref):
    rows = [jnp.concatenate([ref[3 * ab + c] for ab in range(9)], -1) for c in range(3)]
    return jnp.concatenate(rows, 0)


def stacked(ref, x, nx, ny, adjoint, y=0):
    pieces = []
    for a, b in TAPS9:
        i, j = (x + 2 - a, y + 2 - b) if adjoint else (x + a, y + b)
        piece = ref[i : i + nx, j : j + ny]
        pieces.append(piece.reshape(nx * ny * piece.shape[2], piece.shape[3]))
    return jnp.concatenate(pieces, -1)


def zshift(value, step, depth):
    rows = value.shape[0]
    z = lax.broadcasted_iota(jnp.int32, value.shape, 0) & (depth - 1)
    moved = pltpu.roll(value, step % rows, 0)
    return jnp.where(z == (0 if step > 0 else depth - 1), 0.0, moved)


def combined(parts, depth, adjoint):
    ch = parts.shape[1] // 3
    step = -1 if adjoint else 1
    return (
        zshift(parts[:, :ch], step, depth)
        + parts[:, ch : 2 * ch]
        + zshift(parts[:, 2 * ch :], -step, depth)
    )


def ztaps(value, depth, adjoint):
    step = -1 if adjoint else 1
    return jnp.concatenate(
        [
            zshift(value, step, depth).astype(BF16),
            value.astype(BF16),
            zshift(value, -step, depth).astype(BF16),
        ],
        -1,
    )


def assemble(ext, own, ylo, yhi, xlo, xhi):
    size_x, size_y = own.shape[:2]
    ext[1 : 1 + size_x, 1 : 1 + size_y] = own
    ext[1 : 1 + size_x, 0:1] = ylo
    ext[1 : 1 + size_x, 1 + size_y : 2 + size_y] = yhi
    ext[0:1] = xlo
    ext[1 + size_x : 2 + size_x] = xhi


def fetched(sems, *pairs):
    copies = [pltpu.make_async_copy(a, b, sems.at[k]) for k, (a, b) in enumerate(pairs)]
    for copy in copies:
        copy.start()
    for copy in copies:
        copy.wait()


def stack_kernel(first_ref, enc_ref, low_ref, dec_ref, lift_ref, *refs):
    outs, lift_out, (enc, low, dec, sems) = refs[:6], refs[6], refs[7:]
    fetched(sems, (enc_ref, enc), (low_ref, low), (dec_ref, dec), (lift_ref, lift_out))
    for ref, forward, backward in (
        (enc, nt_weight, nn_weight),
        (low, nn_weight, nt_weight),
        (dec, nt_weight, nn_weight),
    ):
        outs[0][...] = forward(ref)
        outs[1][...] = backward(ref)
        outs = outs[2:]


def pack_x_kernel(f_any, c_any, f_ref, c_ref, lo_ref, hi_ref, lo2_ref, hi2_ref, sems):
    fetched(sems, (f_any, f_ref), (c_any, c_ref))
    paired = [jnp.concatenate([f_ref[x, 0:4], f_ref[x, 4:8]], -1) for x in range(2)]
    for x, out, out2 in ((0, lo_ref, lo2_ref), (1, hi_ref, hi2_ref)):
        out[0:8] = jnp.concatenate([f_ref[x], c_ref[x]], -1)
        out[8:12] = paired[1 - x]
        out2[...] = paired[x]


def pack_y_kernel(f_ref, c_ref, xlo, xhi, xlo2, xhi2, lo_ref, hi_ref):
    for first, out in ((0, lo_ref), (5, hi_ref)):
        at = slice(first, first + 3)
        out[0] = xlo[at]
        for x in range(2):
            out[1 + x] = jnp.concatenate([f_ref[x, at], c_ref[x, at]], -1)
        out[3] = xhi[at]
        for k, far, near in ((4, xlo2[...], xlo[8:12]), (5, xhi[8:12], xhi2[...])):
            pair = [jnp.concatenate([v[..., :64], v[..., 64:]], 0)[at] for v in (far, near)]
            out[k] = jnp.concatenate(pair, -1)


def encode_kernel(
    f_ref, ylo, yhi, xlo, xhi, xlo2, xhi2, inside, w_ref, fx_ref, enc_ref, slope_ref, pool_ref, tmp
):
    fx_ref[3:5, 3:11] = f_ref[...]
    fx_ref[2, 3:11] = xlo[0:8, :, :64]
    fx_ref[5, 3:11] = xhi[0:8, :, :64]
    for x, ref, first in ((1, xlo, 8), (6, xhi, 8), (0, xlo2, 0), (7, xhi2, 0)):
        fx_ref[x, 3:7] = ref[first : first + 4, :, :64]
        fx_ref[x, 7:11] = ref[first : first + 4, :, 64:]
    for y, ref in ((0, ylo), (11, yhi)):
        at = slice(y, y + 3)
        fx_ref[2:6, at] = ref[0:4, :, :, :64]
        for x, k in ((0, 4), (6, 5)):
            fx_ref[x, at] = ref[k, :, :, :64]
            fx_ref[x + 1, at] = ref[k, :, :, 64:]
    weight = w_ref[...]
    for x in range(6):
        pre = combined(nt(stacked(fx_ref, x, 1, 12, False), weight), 32, False)
        sigma = jax.nn.sigmoid(pre)
        enc = (pre * sigma).astype(BF16)
        if x in (2, 3):
            slope = sigma * (1.0 + pre * (1.0 - sigma))
            slope_ref[pl.ds((x - 2) * 256, 256), :] = slope[64:320]
            enc_ref[x - 2] = enc[64:320].reshape(8, 32, 64)
        wide = enc.astype(F32).reshape(6, 2, 32, 64)
        part = wide[:, 0] + wide[:, 1]
        if x % 2 == 0:
            held = part
            continue
        tmp[...] = (held + part).reshape(192, 64)
        pooled = tmp[pl.ds(0, 96, stride=2), :] + tmp[pl.ds(1, 96, stride=2), :]
        pooled = pooled * (0.125 if x == 3 else 0.125 * inside[0 if x == 1 else 1])
        pool_ref[x // 2, 1:5] = pooled[16:80].astype(BF16).reshape(4, 16, 64)
        pool_ref[x // 2, 0] = (pooled[0:16] * inside[2]).astype(BF16)
        pool_ref[x // 2, 5] = (pooled[80:96] * inside[3]).astype(BF16)


def joined_grad_kernel(c_ref, *refs):
    (ylo, yhi, xlo, xhi), (w_ref, lift_ref, enc_ref) = refs[:4], refs[4:7]
    cx_ref, jg_ref, kids_ref, adj_ref, dge_ref, tmp = refs[7:]
    cx_ref[1:3, 1:9] = c_ref[...]
    cx_ref[0, 1:9] = xlo[0:8, :, 64:]
    cx_ref[3, 1:9] = xhi[0:8, :, 64:]
    cx_ref[:, 0] = ylo[0:4, 2, :, 64:]
    cx_ref[:, 9] = yhi[0:4, 0, :, 64:]
    weight = w_ref[...]
    for x in range(2):
        grad = combined(nn(stacked(cx_ref, x, 1, 8, True), weight), 32, True)
        grad = grad.astype(BF16)
        jg_ref[pl.ds(x * 256, 256), :] = grad[:, :64]
        tmp[pl.ds(x * 256, 256), :] = grad.astype(F32)
    kids = []
    for p in range(2):
        for q in range(2):
            for r in range(2):
                rows = [
                    tmp[pl.ds(p * 256 + (2 * j + q) * 32 + r, 16, stride=2), :] for j in range(4)
                ]
                kids.append(jnp.concatenate(rows, 0)[:, 64:])
    kids = jnp.concatenate(kids, -1).astype(BF16)
    kids_ref[...] = kids
    adj_ref[...] = nn(kids, lift_ref[...].reshape(512, 128))
    enc = enc_ref[...].reshape(512, 64).astype(F32)
    dge_ref[...] = tn(stacked(cx_ref, 0, 2, 8, True), ztaps(enc, 32, False))


def lower_kernel(px, core, w_ref, lift_ref, adj_ref, kids_ref, cx_ref, dge_ref, enc_ref, *refs):
    la_ref, lg_ref, lifted_ref, keep_ref, send_ref, lo_ref, hi_ref, tmp, halves = refs
    chunk = keep_ref.shape[1]

    def put(row, block):
        at = pl.ds(row % chunk, block.shape[0])
        halves[row // chunk % 2, row // (2 * chunk), at, :] = block.astype(LINK)

    pk = stacked(px, 0, 1, 4, False)
    pre = combined(nn(pk, w_ref[...]), 16, False)
    sigma = jax.nn.sigmoid(pre)
    la = (pre * sigma).astype(BF16)
    lg = (adj_ref[...] * (sigma * (1.0 + pre * (1.0 - sigma)))).astype(BF16)
    la_ref[...] = la.reshape(1, 4, 16, 128)
    lg_ref[...] = lg.reshape(1, 4, 16, 128)
    for j, y, msg in ((0, 0, lo_ref), (3, 7, hi_ref)):
        rows = slice(16 * j, 16 * j + 16)
        msg[0:16] = la[rows]
        msg[16:32] = lg[rows]
        msg[32:64] = jnp.concatenate([enc_ref[0, y], enc_ref[1, y]], -1)
    fine = nt(la, lift_ref[...].reshape(512, 128)).astype(BF16).astype(F32)
    for p in range(2):
        for q in range(2):
            for r in range(2):
                k = 4 * p + 2 * q + r
                for j in range(4):
                    tmp[pl.ds(p * 256 + (2 * j + q) * 32 + r, 16, stride=2), :] = fine[
                        16 * j : 16 * j + 16, 64 * k : 64 * k + 64
                    ]
    lifted = tmp[...]
    lifted_ref[...] = lifted.astype(BF16).reshape(2, 8, 32, 64)
    dgl = tn(stacked(cx_ref, 0, 2, 8, True), ztaps(lifted, 32, False))
    for ab in range(9):
        for c in range(3):
            cols = slice(64 * c, 64 * c + 64)
            rows = slice(64 * ab, 64 * ab + 64)
            both = jnp.concatenate([dge_ref[rows, cols], dgl[rows, cols]], -1)
            put((3 * ab + c) * 64, both)
    low = tn(pk, ztaps(lg.astype(F32), 16, True))
    for ab in range(9):
        for c in range(3):
            block = low[64 * ab : 64 * ab + 64, 128 * c : 128 * c + 128]
            put(1728 + (3 * ab + c) * 64, block)
    lift = tn(kids_ref[...], la)
    for k in range(8):
        put(3456 + 64 * k, lift[64 * k : 64 * k + 64])
    for row in (3968, 4032):
        put(row, jnp.zeros((64, 128), F32))
    mine = core[0]
    keep_ref[...] = halves[mine]
    send_ref[...] = halves[1 - mine]


def add_kernel(a_ref, b_ref, out_ref):
    out_ref[...] = (a_ref[...].astype(F32) + b_ref[...].astype(F32)).astype(LINK)


def joined_x_kernel(la_ref, lg_ref, enc_ref, ylo_ref, yhi_ref, lo_ref, hi_ref):
    for x, out in ((0, lo_ref), (1, hi_ref)):
        cols = slice(64 * x, 64 * x + 64)
        out[0:16] = ylo_ref[0:16]
        out[16:80] = la_ref[...].reshape(64, 128)
        out[80:96] = yhi_ref[0:16]
        out[96:112] = ylo_ref[16:32]
        out[112:176] = lg_ref[...].reshape(64, 128)
        out[176:192] = yhi_ref[16:32]
        enc = enc_ref[x].reshape(256, 64)
        first = jnp.concatenate([ylo_ref[32:64, cols], enc[:128]], 0)
        second = jnp.concatenate([enc[128:], yhi_ref[32:64, cols]], 0)
        out[192:352] = jnp.concatenate([first, second], -1)


def edge_y_kernel(eg_ref, lo_ref, hi_ref):
    lo_ref[...] = jnp.concatenate([eg_ref[0, 0], eg_ref[1, 0]], -1)
    hi_ref[...] = jnp.concatenate([eg_ref[0, 7], eg_ref[1, 7]], -1)


def edge_x_kernel(eg_ref, ylo_ref, yhi_ref, lo_ref, hi_ref):
    for x, out in ((0, lo_ref), (1, hi_ref)):
        cols = slice(64 * x, 64 * x + 64)
        eg = eg_ref[x].reshape(256, 64)
        first = jnp.concatenate([ylo_ref[:, cols], eg[:128]], 0)
        second = jnp.concatenate([eg[128:], yhi_ref[:, cols]], 0)
        out[...] = jnp.concatenate([first, second], -1)


def column(rows):
    return jnp.stack([rows[:, :64], rows[:, 64:]], 0).reshape(2, 1, 32, 64)


def plane(rows):
    return jnp.concatenate([rows[:, :64], rows[:, 64:]], 0).reshape(1, 10, 32, 64)


def encoder_grad_kernel(lg_ref, *refs):
    (ylo, yhi, xlo, xhi), (w_ref, slope_ref, jg_ref, fx_ref) = refs[:4], refs[4:8]
    eg_ref, grads_ref, lo_ref, hi_ref, lx, tmp = refs[8:]
    sides = [h[16:32].reshape(1, 1, 16, 128) for h in (ylo, yhi)]
    sides += [h[96:192].reshape(1, 6, 16, 128) for h in (xlo, xhi)]
    assemble(lx, lg_ref[...], *sides)
    pg = combined(nt(stacked(lx, 0, 1, 4, True), w_ref[...]), 16, True)
    pg = pg.astype(BF16).astype(F32) * 0.125
    tmp[pl.ds(0, 64, stride=2), :] = pg
    tmp[pl.ds(1, 64, stride=2), :] = pg
    wide = tmp[...].reshape(1, 4, 1, 32, 64)
    wide = jnp.broadcast_to(wide, (2, 4, 2, 32, 64)).reshape(512, 64)
    eg = ((jg_ref[...].astype(F32) + wide) * slope_ref[...]).astype(BF16)
    eg_ref[...] = eg.reshape(2, 8, 32, 64)
    edge_y_kernel(eg_ref, lo_ref, hi_ref)
    grad = tn(ztaps(eg.astype(F32), 32, True), stacked(fx_ref, 2, 2, 8, False, 2))
    for ab in range(9):
        for c in range(3):
            block = grad[64 * c : 64 * c + 64, 64 * ab : 64 * ab + 64]
            block = jnp.concatenate([block[:32], block[32:]], -1)
            grads_ref[pl.ds((3 * ab + c) * 32, 32), :] = block.astype(LINK)
    grads_ref[pl.ds(864, 160), :] = jnp.zeros((160, 128), LINK)


def decode_kernel(enc_ref, lifted_ref, *refs):
    (ylo, yhi, xlo, xhi), (lift_ref, w_ref, out_ref, jx, ty, tx) = refs[:4], refs[4:]
    sides = []
    for q, h in ((1, ylo), (0, yhi)):
        for p in range(2):
            for r in range(2):
                fine = nt(h[0:16], lift_ref[4 * p + 2 * q + r]).astype(BF16).astype(F32)
                ty[pl.ds(32 * p + r, 16, stride=2), :] = fine
        lifted = ty[...].astype(BF16).reshape(2, 1, 32, 64)
        sides.append(jnp.concatenate([column(h[32:64]), lifted], -1))
    for p, h in ((1, xlo), (0, xhi)):
        for q in range(2):
            for r in range(2):
                fine = nt(h[0:96], lift_ref[4 * p + 2 * q + r]).astype(BF16).astype(F32)
                for j in range(6):
                    y = 2 * j + q - 1
                    if 0 <= y < 10:
                        tx[pl.ds(32 * y + r, 16, stride=2), :] = fine[16 * j : 16 * j + 16]
        lifted = tx[...].astype(BF16).reshape(1, 10, 32, 64)
        sides.append(jnp.concatenate([plane(h[192:352]), lifted], -1))
    assemble(jx, jnp.concatenate([enc_ref[...], lifted_ref[...]], -1), *sides)
    weight = w_ref[...]
    for x in range(2):
        out = combined(nt(stacked(jx, x, 1, 8, False), weight), 32, False)
        out_ref[x] = out.astype(BF16).reshape(8, 32, 64)


def input_grad_kernel(eg_ref, ylo, yhi, xlo, xhi, w_ref, out_ref, ex):
    sides = [column(ylo[...]), column(yhi[...]), plane(xlo[...]), plane(xhi[...])]
    assemble(ex, eg_ref[...], *sides)
    weight = w_ref[...]
    for x in range(2):
        out = combined(nn(stacked(ex, x, 1, 8, True), weight), 32, True)
        out_ref[x] = out.astype(BF16).reshape(8, 32, 64)


def sum_x_kernel(grads_ref, enc_ref, out_ref):
    first = 0
    for ref in (grads_ref, enc_ref):
        rows = ref.shape[1]
        total = ref[0].astype(F32)
        for k in range(1, ref.shape[0]):
            total = total + ref[k].astype(F32)
        total = total.astype(LINK)
        for k in range(out_ref.shape[0]):
            out_ref[k, first : first + rows] = total
        first += rows


def sum_z_kernel(parts_ref, out_ref):
    total = parts_ref[0].astype(F32)
    for k in range(1, parts_ref.shape[0]):
        total = total + parts_ref[k].astype(F32)
    total = total.astype(LINK)
    for k in range(out_ref.shape[0]):
        out_ref[k] = total


def widen_kernel(core, own_ref, other_ref, encoder_ref, decoder_ref, lower_ref, lift_ref):
    own, other = own_ref[...].astype(F32), other_ref[...].astype(F32)
    first = core[0] == 0
    both = jnp.stack([jnp.where(first, own, other), jnp.where(first, other, own)], 1)
    chunk = own.shape[1] // 5 * 4
    sums = both[:, :, :chunk].reshape(4096, 128)
    decoder_ref[...] = sums[0:1728].reshape(27, 64, 128)
    lower_ref[...] = sums[1728:3456].reshape(27, 64, 128)
    lift_ref[...] = sums[3456:3968].reshape(8, 64, 128)
    wide = both[:, :, chunk:].reshape(1024, 128)[:864].reshape(27, 32, 128)
    encoder_ref[:, 0:32, :] = wide[..., :64]
    encoder_ref[:, 32:64, :] = wide[..., 64:]


def per_device(features, encoder_weight, lower_weight, lift_weight, decoder_weight, cotangent):
    f = jnp.transpose(features, (1, 2, 3, 0))
    c = jnp.transpose(cotangent, (1, 2, 3, 0))
    lower_t = jnp.transpose(lower_weight, (0, 2, 1))
    brick, coarse = (2, 8, 32, 64), (1, 4, 16, 128)

    size_x, size_z = lax.axis_size("gx"), lax.axis_size("gz")
    at_x, at_y = lax.axis_index("gx"), lax.axis_index(GY)
    inside = jnp.stack([at_x > 0, at_x < size_x - 1, at_y > 0, at_y < 2 * size_z - 1]).astype(F32)
    core = lax.axis_index("gc").reshape(1)

    f, c, lo, hi, lo2, hi2 = call(
        pack_x_kernel,
        [(brick, BF16)] * 2 + [((12, 32, 128), BF16)] * 2 + [((4, 32, 128), BF16)] * 2,
        [(pltpu.SemaphoreType.DMA((2,)), None)],
        [f, c],
        spaces={0: pltpu.HBM, 1: pltpu.HBM},
    )
    x_halo = swapped(lo, hi, GX)
    far_halo = [shifted(hi2, GX, 2), shifted(lo2, GX, -2)]
    edges = call(pack_y_kernel, [((6, 3, 32, 128), BF16)] * 2, [], [f, c, *x_halo, *far_halo])
    y_halo = swapped(*edges, GY)
    enc_fwd, enc_bwd, low_fwd, low_bwd, dec_fwd, dec_bwd, lift = call(
        stack_kernel,
        [
            ((192, 576), BF16),
            ((576, 192), BF16),
            ((576, 384), BF16),
            ((192, 1152), BF16),
            ((192, 1152), BF16),
            ((576, 384), BF16),
            ((8, 64, 128), BF16),
        ],
        [
            ((27, 64, 64), BF16),
            ((27, 64, 128), BF16),
            ((27, 64, 128), BF16),
            (pltpu.SemaphoreType.DMA((4,)), None),
        ],
        [edges[0], encoder_weight, lower_t, decoder_weight, lift_weight],
        spaces={k: pltpu.HBM for k in range(5)},
        flops=2 * 10**9,
    )
    fx, encoded, slope, pooled = call(
        encode_kernel,
        [((8, 14, 32, 64), BF16), (brick, BF16), ((512, 64), F32), ((3, 6, 16, 64), BF16)],
        [((192, 64), F32)],
        [f, *y_halo, *x_halo, *far_halo, inside, enc_fwd],
        spaces={7: pltpu.SMEM},
    )
    cx, jg, kids, adj, dge = call(
        joined_grad_kernel,
        [
            ((4, 10, 32, 64), BF16),
            ((512, 64), BF16),
            ((64, 512), BF16),
            ((64, 128), F32),
            ((576, 192), F32),
        ],
        [((512, 128), F32)],
        [c, *y_halo, *x_halo, dec_bwd, lift, encoded],
    )
    half = (size_x, 2048 // size_x, 128)
    la, lg, lifted, keep, send, *edges = call(
        lower_kernel,
        [(coarse, BF16), (coarse, BF16), (brick, BF16), (half, LINK), (half, LINK)]
        + [((64, 128), BF16)] * 2,
        [((512, 64), F32), ((2,) + half, LINK)],
        [pooled, core, low_fwd, lift, adj, kids, cx, dge, encoded],
        spaces={1: pltpu.SMEM},
    )
    (grads,) = call(add_kernel, [(half, LINK)], [], [keep, partner(send)])
    grads = lax.all_to_all(grads, "gx", 0, 0)
    y_halo = swapped(*edges, GY)
    edges = call(joined_x_kernel, [((352, 128), BF16)] * 2, [], [la, lg, encoded, *y_halo])
    halo = [*y_halo, *swapped(*edges, GX)]
    eg, enc_grads, *edges = call(
        encoder_grad_kernel,
        [(brick, BF16), ((1024, 128), LINK)] + [((32, 128), BF16)] * 2,
        [((3, 6, 16, 128), BF16), ((128, 64), F32)],
        [lg, *halo, low_bwd, slope, jg, fx],
    )
    enc_grads, grads = lax.optimization_barrier((enc_grads, grads))
    enc_grads = lax.all_to_all(enc_grads.reshape(2 * size_x, -1, 128), ("gx", "gc"), 0, 0)
    rows = 2560 // size_x
    (sums,) = call(sum_x_kernel, [((size_z, rows, 128), LINK)], [], [grads, enc_grads])
    sums = lax.all_to_all(sums, "gz", 0, 0)
    (sums,) = call(sum_z_kernel, [((size_x, rows, 128), LINK)], [], [sums])
    sums = lax.all_to_all(sums, "gx", 0, 0)
    encoder_gradient, decoder_gradient, lower_gradient, lift_gradient = call(
        widen_kernel,
        [((27, 64, 64), F32), ((27, 64, 128), F32), ((27, 64, 128), F32), ((8, 64, 128), F32)],
        [],
        [core, sums, partner(sums)],
        spaces={0: pltpu.SMEM},
    )
    y_halo = swapped(*edges, GY)
    edges = call(edge_x_kernel, [((160, 128), BF16)] * 2, [], [eg, *y_halo])
    eg_halo = [*y_halo, *swapped(*edges, GX)]
    (decoded,) = call(
        decode_kernel,
        [(brick, BF16)],
        [((4, 10, 32, 128), BF16), ((64, 64), F32), ((320, 64), F32)],
        [encoded, lifted, *halo, lift, dec_fwd],
    )
    (input_grad,) = call(
        input_grad_kernel,
        [(brick, BF16)],
        [((4, 10, 32, 64), BF16)],
        [eg, *eg_halo, enc_bwd],
    )
    return (
        jnp.transpose(decoded, (3, 0, 1, 2)),
        jnp.transpose(input_grad, (3, 0, 1, 2)),
        encoder_gradient,
        jnp.transpose(lower_gradient, (0, 2, 1)),
        lift_gradient,
        decoder_gradient,
    )


def solution(mesh):
    size_x, size_y = mesh.devices.shape
    chips = Mesh(mesh.devices.reshape(size_x, size_y // 2, 2), ("gx", "gz", "gc"))
    field = P(None, "gx", ("gz", "gc"), None)
    return jax.shard_map(
        per_device,
        mesh=chips,
        in_specs=(field, P(), P(), P(), P(), field),
        out_specs=(field, field, P(), P(), P(), P()),
        check_vma=False,
    )
```

```python
import math

import jax
import jax.numpy as jnp
from jax import lax
from jax.experimental import pallas as pl
from jax.experimental.pallas import tpu as pltpu
from jax.sharding import Mesh, PartitionSpec as P

F32, BF16 = jnp.float32, jnp.bfloat16
LINK = BF16
GX, GY = ("gx",), ("gz", "gc")
TAPS9 = tuple((a, b) for a in range(3) for b in range(3))


def shifted(piece, axes, step):
    size = math.prod(lax.axis_size(axis) for axis in axes)
    pairs = [(i, i + step) for i in range(size) if 0 <= i + step < size]
    return lax.ppermute(piece, axes, pairs)


def swapped(low, high, axes):
    return shifted(high, axes, 1), shifted(low, axes, -1)


def partner(piece):
    return lax.ppermute(piece, "gc", [(0, 1), (1, 0)])


def call(kernel, outs, scratch, operands, spaces=(), flops=10**6, aliases=()):
    return pl.pallas_call(
        kernel,
        out_shape=[jax.ShapeDtypeStruct(s, d) for s, d in outs],
        in_specs=[
            pl.BlockSpec(memory_space=dict(spaces).get(i, pltpu.VMEM)) for i in range(len(operands))
        ],
        out_specs=[pl.BlockSpec(memory_space=pltpu.VMEM)] * len(outs),
        scratch_shapes=[s if d is None else pltpu.VMEM(s, d) for s, d in scratch],
        input_output_aliases=dict(aliases),
        compiler_params=pltpu.CompilerParams(vmem_limit_bytes=40 * 2**20),
        cost_estimate=pl.CostEstimate(flops=flops, bytes_accessed=10**4, transcendentals=0),
    )(*operands)


def nn(a, b):
    return lax.dot_general(a, b, (((1,), (0,)), ((), ())), preferred_element_type=F32)


def nt(a, b):
    return lax.dot_general(a, b, (((1,), (1,)), ((), ())), preferred_element_type=F32)


def tn(a, b):
    return lax.dot_general(a, b, (((0,), (0,)), ((), ())), preferred_element_type=F32)


def nn_weight(ref):
    rows = [jnp.concatenate([ref[3 * ab + c] for c in range(3)], -1) for ab in range(9)]
    return jnp.concatenate(rows, 0)


def nt_weight(ref):
    rows = [jnp.concatenate([ref[3 * ab + c] for ab in range(9)], -1) for c in range(3)]
    return jnp.concatenate(rows, 0)


def stacked(ref, x, nx, ny, adjoint, y=0):
    pieces = []
    for a, b in TAPS9:
        i, j = (x + 2 - a, y + 2 - b) if adjoint else (x + a, y + b)
        piece = ref[i : i + nx, j : j + ny]
        pieces.append(piece.reshape(nx * ny * piece.shape[2], piece.shape[3]))
    return jnp.concatenate(pieces, -1)


def zshift(value, step, depth):
    rows = value.shape[0]
    z = lax.broadcasted_iota(jnp.int32, value.shape, 0) & (depth - 1)
    moved = pltpu.roll(value, step % rows, 0)
    return jnp.where(z == (0 if step > 0 else depth - 1), 0.0, moved)


def combined(parts, depth, adjoint):
    ch = parts.shape[1] // 3
    step = -1 if adjoint else 1
    return (
        zshift(parts[:, :ch], step, depth)
        + parts[:, ch : 2 * ch]
        + zshift(parts[:, 2 * ch :], -step, depth)
    )


def ztaps(value, depth, adjoint):
    step = -1 if adjoint else 1
    return jnp.concatenate(
        [
            zshift(value, step, depth).astype(BF16),
            value.astype(BF16),
            zshift(value, -step, depth).astype(BF16),
        ],
        -1,
    )


def assemble(ext, own, ylo, yhi, xlo, xhi):
    size_x, size_y = own.shape[:2]
    ext[1 : 1 + size_x, 1 : 1 + size_y] = own
    ext[1 : 1 + size_x, 0:1] = ylo
    ext[1 : 1 + size_x, 1 + size_y : 2 + size_y] = yhi
    ext[0:1] = xlo
    ext[1 + size_x : 2 + size_x] = xhi


def fetched(sems, *pairs):
    copies = [pltpu.make_async_copy(a, b, sems.at[k]) for k, (a, b) in enumerate(pairs)]
    for copy in copies:
        copy.start()
    for copy in copies:
        copy.wait()


def stack_kernel(first_ref, enc_ref, low_ref, dec_ref, lift_ref, *refs):
    outs, lift_out, (enc, low, dec, sems) = refs[:6], refs[6], refs[7:]
    fetched(sems, (enc_ref, enc), (low_ref, low), (dec_ref, dec), (lift_ref, lift_out))
    for ref, forward, backward in (
        (enc, nt_weight, nn_weight),
        (low, nn_weight, nt_weight),
        (dec, nt_weight, nn_weight),
    ):
        outs[0][...] = forward(ref)
        outs[1][...] = backward(ref)
        outs = outs[2:]


def pack_x_kernel(f_any, c_any, f_ref, c_ref, lo_ref, hi_ref, lo2_ref, hi2_ref, sems):
    fetched(sems, (f_any, f_ref), (c_any, c_ref))
    paired = [jnp.concatenate([f_ref[x, 0:4], f_ref[x, 4:8]], -1) for x in range(2)]
    for x, out, out2 in ((0, lo_ref, lo2_ref), (1, hi_ref, hi2_ref)):
        out[0:8] = jnp.concatenate([f_ref[x], c_ref[x]], -1)
        out[8:12] = paired[1 - x]
        out2[...] = paired[x]


def pack_y_kernel(f_ref, c_ref, xlo, xhi, xlo2, xhi2, lo_ref, hi_ref):
    for first, out in ((0, lo_ref), (3, hi_ref)):
        at = slice(first, first + 5)
        out[0] = xlo[at]
        for x in range(2):
            out[1 + x] = jnp.concatenate([f_ref[x, at], c_ref[x, at]], -1)
        out[3] = xhi[at]
        for k, far, near in ((4, xlo2[...], xlo[8:12]), (5, xhi[8:12], xhi2[...])):
            pair = [jnp.concatenate([v[..., :64], v[..., 64:]], 0)[at] for v in (far, near)]
            out[k] = jnp.concatenate(pair, -1)


def encode_kernel(
    f_ref, ylo, yhi, xlo, xhi, xlo2, xhi2, inside, w_ref, fx_ref, enc_ref, slope_ref, pool_ref, tmp
):
    fx_ref[3:5, 5:13] = f_ref[...]
    fx_ref[2, 5:13] = xlo[0:8, :, :64]
    fx_ref[5, 5:13] = xhi[0:8, :, :64]
    for x, ref, first in ((1, xlo, 8), (6, xhi, 8), (0, xlo2, 0), (7, xhi2, 0)):
        fx_ref[x, 5:9] = ref[first : first + 4, :, :64]
        fx_ref[x, 9:13] = ref[first : first + 4, :, 64:]
    for y, ref in ((0, ylo), (13, yhi)):
        at = slice(y, y + 5)
        fx_ref[2:6, at] = ref[0:4, :, :, :64]
        for x, k in ((0, 4), (6, 5)):
            fx_ref[x, at] = ref[k, :, :, :64]
            fx_ref[x + 1, at] = ref[k, :, :, 64:]
    weight = w_ref[...]
    for x in range(6):
        pre = combined(nt(stacked(fx_ref, x, 1, 16, False), weight), 32, False)
        sigma = jax.nn.sigmoid(pre)
        enc = (pre * sigma).astype(BF16)
        if x in (2, 3):
            slope = sigma * (1.0 + pre * (1.0 - sigma))
            slope_ref[pl.ds((x - 2) * 256, 256), :] = slope[128:384]
            enc_ref[x - 2, 1:9] = enc[128:384].reshape(8, 32, 64)
            enc_ref[x - 2, 0] = (enc[96:128].astype(F32) * inside[2]).astype(BF16)
            enc_ref[x - 2, 9] = (enc[384:416].astype(F32) * inside[3]).astype(BF16)
        wide = enc.astype(F32).reshape(8, 2, 32, 64)
        part = wide[:, 0] + wide[:, 1]
        if x % 2 == 0:
            held = part
            continue
        tmp[...] = (held + part).reshape(256, 64)
        pooled = tmp[pl.ds(0, 128, stride=2), :] + tmp[pl.ds(1, 128, stride=2), :]
        pooled = pooled * (0.125 if x == 3 else 0.125 * inside[0 if x == 1 else 1])
        pool_ref[x // 2, 2:6] = pooled[32:96].astype(BF16).reshape(4, 16, 64)
        pool_ref[x // 2, 0:2] = (pooled[0:32] * inside[2]).astype(BF16).reshape(2, 16, 64)
        pool_ref[x // 2, 6:8] = (pooled[96:128] * inside[3]).astype(BF16).reshape(2, 16, 64)


def joined_grad_kernel(c_ref, *refs):
    (ylo, yhi, xlo, xhi), (w_ref, lift_ref, enc_ref) = refs[:4], refs[4:7]
    cx_ref, jg_ref, kids_ref, adj_ref, dge_ref, tmp = refs[7:]
    cx_ref[1:3, 3:11] = c_ref[...]
    cx_ref[0, 3:11] = xlo[0:8, :, 64:]
    cx_ref[3, 3:11] = xhi[0:8, :, 64:]
    cx_ref[:, 0:3] = ylo[0:4, 2:5, :, 64:]
    cx_ref[:, 11:14] = yhi[0:4, 0:3, :, 64:]
    weight = w_ref[...]
    for x in range(2):
        grad = combined(nn(stacked(cx_ref, x, 1, 12, True), weight), 32, True)
        grad = grad.astype(BF16)
        jg_ref[pl.ds(x * 256, 256), :] = grad[64:320, :64]
        tmp[pl.ds(x * 384, 384), :] = grad.astype(F32)
    kids = []
    for p in range(2):
        for q in range(2):
            for r in range(2):
                rows = [
                    tmp[pl.ds(p * 384 + (2 * j + q) * 32 + r, 16, stride=2), :] for j in range(6)
                ]
                kids.append(jnp.concatenate(rows, 0)[:, 64:])
    kids = jnp.concatenate(kids, -1).astype(BF16)
    kids_ref[...] = kids[16:80]
    adj_ref[...] = nn(kids, lift_ref[...].reshape(512, 128))
    enc = enc_ref[:, 1:9].reshape(512, 64).astype(F32)
    dge_ref[...] = tn(stacked(cx_ref, 0, 2, 8, True, 2), ztaps(enc, 32, False))


def halver(halves):
    chunk = halves.shape[2]

    def put(row, block):
        at = pl.ds(row % chunk, block.shape[0])
        halves[row // chunk % 2, row // (2 * chunk), at, :] = block.astype(LINK)

    return put


def lower_kernel(
    px, core, inside, w_ref, lift_ref, adj_ref, kids_ref, cx_ref, dge_ref, enc_ref, *refs
):
    lg_ref, lifted_ref, keep_ref, send_ref, lo_ref, hi_ref, tmp, halves = refs
    put = halver(halves)

    def masked(value):
        first, last = value[0:16] * inside[2], value[80:96] * inside[3]
        return jnp.concatenate([first, value[16:80], last], 0).astype(BF16)

    pk = stacked(px, 0, 1, 6, False)
    pre = combined(nn(pk, w_ref[...]), 16, False)
    sigma = jax.nn.sigmoid(pre)
    la = masked(pre * sigma)
    lg = masked(adj_ref[...] * (sigma * (1.0 + pre * (1.0 - sigma))))
    lg_ref[...] = lg
    for x, msg in ((0, lo_ref), (1, hi_ref)):
        msg[0:96] = la
        msg[96:192] = lg
        enc = enc_ref[x].reshape(320, 64)
        msg[192:352] = jnp.concatenate([enc[:160], enc[160:]], -1)
    fine = nt(la, lift_ref[...].reshape(512, 128)).astype(BF16).astype(F32)
    for p in range(2):
        for q in range(2):
            for r in range(2):
                k = 4 * p + 2 * q + r
                for j in range(6):
                    y = 2 * j + q - 1
                    if 0 <= y < 10:
                        tmp[pl.ds((p * 10 + y) * 32 + r, 16, stride=2), :] = fine[
                            16 * j : 16 * j + 16, 64 * k : 64 * k + 64
                        ]
    lifted_ref[...] = tmp[...].astype(BF16).reshape(2, 10, 32, 64)
    lifted = jnp.concatenate([tmp[32:288], tmp[352:608]], 0)
    la, lg, pk = la[16:80], lg[16:80], pk[16:80]
    dgl = tn(stacked(cx_ref, 0, 2, 8, True, 2), ztaps(lifted, 32, False))
    for ab in range(9):
        for c in range(3):
            cols = slice(64 * c, 64 * c + 64)
            rows = slice(64 * ab, 64 * ab + 64)
            both = jnp.concatenate([dge_ref[rows, cols], dgl[rows, cols]], -1)
            put((3 * ab + c) * 64, both)
    low = tn(pk, ztaps(lg.astype(F32), 16, True))
    for ab in range(9):
        for c in range(3):
            block = low[64 * ab : 64 * ab + 64, 128 * c : 128 * c + 128]
            put(1728 + (3 * ab + c) * 64, block)
    lift = tn(kids_ref[...], la)
    for k in range(8):
        put(3456 + 64 * k, lift[64 * k : 64 * k + 64])
    for row in (3968, 4032):
        put(row, jnp.zeros((64, 128), F32))
    mine, chunk = core[0], halves.shape[2]
    keep_ref[:, :chunk, :] = halves[mine]
    send_ref[:, :chunk, :] = halves[1 - mine]


def add_kernel(a_ref, b_ref, out_ref):
    out_ref[...] = (a_ref[...].astype(F32) + b_ref[...].astype(F32)).astype(LINK)


def edge_y_kernel(eg_ref, lo_ref, hi_ref):
    lo_ref[...] = jnp.concatenate([eg_ref[0, 0], eg_ref[1, 0]], -1)
    hi_ref[...] = jnp.concatenate([eg_ref[0, 7], eg_ref[1, 7]], -1)


def edge_x_kernel(eg_ref, ylo_ref, yhi_ref, lo_ref, hi_ref):
    for x, out in ((0, lo_ref), (1, hi_ref)):
        cols = slice(64 * x, 64 * x + 64)
        eg = eg_ref[x].reshape(256, 64)
        first = jnp.concatenate([ylo_ref[:, cols], eg[:128]], 0)
        second = jnp.concatenate([eg[128:], yhi_ref[:, cols]], 0)
        out[...] = jnp.concatenate([first, second], -1)


def column(rows):
    return jnp.stack([rows[:, :64], rows[:, 64:]], 0).reshape(2, 1, 32, 64)


def plane(rows):
    return jnp.concatenate([rows[:, :64], rows[:, 64:]], 0).reshape(1, 10, 32, 64)


def encoder_grad_kernel(lg_ref, xlo, xhi, core, w_ref, slope_ref, jg_ref, fx_ref, *refs):
    eg_ref, keep_ref, send_ref, lo_ref, hi_ref, lx, tmp, halves = refs[2:]
    put = halver(halves)
    lx[0] = xlo[96:192].reshape(6, 16, 128)
    lx[1] = lg_ref[...].reshape(6, 16, 128)
    lx[2] = xhi[96:192].reshape(6, 16, 128)
    pg = combined(nt(stacked(lx, 0, 1, 4, True), w_ref[...]), 16, True)
    pg = pg.astype(BF16).astype(F32) * 0.125
    tmp[pl.ds(0, 64, stride=2), :] = pg
    tmp[pl.ds(1, 64, stride=2), :] = pg
    wide = tmp[...].reshape(1, 4, 1, 32, 64)
    wide = jnp.broadcast_to(wide, (2, 4, 2, 32, 64)).reshape(512, 64)
    eg = ((jg_ref[...].astype(F32) + wide) * slope_ref[...]).astype(BF16)
    eg_ref[...] = eg.reshape(2, 8, 32, 64)
    edge_y_kernel(eg_ref, lo_ref, hi_ref)
    grad = tn(ztaps(eg.astype(F32), 32, True), stacked(fx_ref, 2, 2, 8, False, 4))
    for ab in range(9):
        for c in range(3):
            block = grad[64 * c : 64 * c + 64, 64 * ab : 64 * ab + 64]
            block = jnp.concatenate([block[:32], block[32:]], -1)
            put((3 * ab + c) * 32, block[:16])
            put((3 * ab + c) * 32 + 16, block[16:])
    for row in range(864, 1024, 16):
        put(row, jnp.zeros((16, 128), F32))
    mine, chunk = core[0], keep_ref.shape[1] - halves.shape[2]
    keep_ref[:, chunk:, :] = halves[mine]
    send_ref[:, chunk:, :] = halves[1 - mine]


def decode_kernel(enc_ref, lifted_ref, xlo, xhi, lift_ref, w_ref, out_ref, jx, tx):
    jx[1:3] = jnp.concatenate([enc_ref[...], lifted_ref[...]], -1)
    for p, h in ((1, xlo), (0, xhi)):
        for q in range(2):
            for r in range(2):
                fine = nt(h[0:96], lift_ref[4 * p + 2 * q + r]).astype(BF16).astype(F32)
                for j in range(6):
                    y = 2 * j + q - 1
                    if 0 <= y < 10:
                        tx[pl.ds(32 * y + r, 16, stride=2), :] = fine[16 * j : 16 * j + 16]
        lifted = tx[...].astype(BF16).reshape(1, 10, 32, 64)
        x = 0 if p == 1 else 3
        jx[x : x + 1] = jnp.concatenate([plane(h[192:352]), lifted], -1)
    weight = w_ref[...]
    for x in range(2):
        out = combined(nt(stacked(jx, x, 1, 8, False), weight), 32, False)
        out_ref[x] = out.astype(BF16).reshape(8, 32, 64)


def input_grad_kernel(eg_ref, ylo, yhi, xlo, xhi, w_ref, out_ref, ex):
    sides = [column(ylo[...]), column(yhi[...]), plane(xlo[...]), plane(xhi[...])]
    assemble(ex, eg_ref[...], *sides)
    weight = w_ref[...]
    for x in range(2):
        out = combined(nn(stacked(ex, x, 1, 8, True), weight), 32, True)
        out_ref[x] = out.astype(BF16).reshape(8, 32, 64)


def sum_kernel(parts_ref, out_ref):
    total = parts_ref[0].astype(F32)
    for k in range(1, parts_ref.shape[0]):
        total = total + parts_ref[k].astype(F32)
    total = total.astype(LINK)
    for k in range(out_ref.shape[0]):
        out_ref[k] = total


def widen_kernel(core, own_ref, other_ref, encoder_ref, decoder_ref, lower_ref, lift_ref):
    own, other = own_ref[...].astype(F32), other_ref[...].astype(F32)
    first = core[0] == 0
    both = jnp.stack([jnp.where(first, own, other), jnp.where(first, other, own)], 1)
    chunk = own.shape[1] // 5 * 4
    sums = both[:, :, :chunk].reshape(4096, 128)
    decoder_ref[...] = sums[0:1728].reshape(27, 64, 128)
    lower_ref[...] = sums[1728:3456].reshape(27, 64, 128)
    lift_ref[...] = sums[3456:3968].reshape(8, 64, 128)
    wide = both[:, :, chunk:].reshape(1024, 128)[:864].reshape(27, 32, 128)
    encoder_ref[:, 0:32, :] = wide[..., :64]
    encoder_ref[:, 32:64, :] = wide[..., 64:]


def per_device(features, encoder_weight, lower_weight, lift_weight, decoder_weight, cotangent):
    f = jnp.transpose(features, (1, 2, 3, 0))
    c = jnp.transpose(cotangent, (1, 2, 3, 0))
    lower_t = jnp.transpose(lower_weight, (0, 2, 1))
    brick, tall = (2, 8, 32, 64), (2, 10, 32, 64)

    size_x, size_z = lax.axis_size("gx"), lax.axis_size("gz")
    at_x, at_y = lax.axis_index("gx"), lax.axis_index(GY)
    inside = jnp.stack([at_x > 0, at_x < size_x - 1, at_y > 0, at_y < 2 * size_z - 1]).astype(F32)
    core = lax.axis_index("gc").reshape(1)

    f, c, lo, hi, lo2, hi2 = call(
        pack_x_kernel,
        [(brick, BF16)] * 2 + [((12, 32, 128), BF16)] * 2 + [((4, 32, 128), BF16)] * 2,
        [(pltpu.SemaphoreType.DMA((2,)), None)],
        [f, c],
        spaces={0: pltpu.HBM, 1: pltpu.HBM},
    )
    x_halo = swapped(lo, hi, GX)
    far_halo = [shifted(hi2, GX, 2), shifted(lo2, GX, -2)]
    edges = call(pack_y_kernel, [((6, 5, 32, 128), BF16)] * 2, [], [f, c, *x_halo, *far_halo])
    y_halo = swapped(*edges, GY)
    enc_fwd, enc_bwd, low_fwd, low_bwd, dec_fwd, dec_bwd, lift = call(
        stack_kernel,
        [
            ((192, 576), BF16),
            ((576, 192), BF16),
            ((576, 384), BF16),
            ((192, 1152), BF16),
            ((192, 1152), BF16),
            ((576, 384), BF16),
            ((8, 64, 128), BF16),
        ],
        [
            ((27, 64, 64), BF16),
            ((27, 64, 128), BF16),
            ((27, 64, 128), BF16),
            (pltpu.SemaphoreType.DMA((4,)), None),
        ],
        [edges[0], encoder_weight, lower_t, decoder_weight, lift_weight],
        spaces={k: pltpu.HBM for k in range(5)},
        flops=2 * 10**9,
    )
    fx, encoded, slope, pooled = call(
        encode_kernel,
        [((8, 18, 32, 64), BF16), (tall, BF16), ((512, 64), F32), ((3, 8, 16, 64), BF16)],
        [((256, 64), F32)],
        [f, *y_halo, *x_halo, *far_halo, inside, enc_fwd],
        spaces={7: pltpu.SMEM},
    )
    cx, jg, kids, adj, dge = call(
        joined_grad_kernel,
        [
            ((4, 14, 32, 64), BF16),
            ((512, 64), BF16),
            ((64, 512), BF16),
            ((96, 128), F32),
            ((576, 192), F32),
        ],
        [((768, 128), F32)],
        [c, *y_halo, *x_halo, dec_bwd, lift, encoded],
    )
    half = (size_x, 2560 // size_x, 128)
    lg, lifted, keep, send, *edges = call(
        lower_kernel,
        [((96, 128), BF16), (tall, BF16), (half, LINK), (half, LINK)]
        + [((352, 128), BF16)] * 2,
        [((640, 64), F32), ((2, size_x, 2048 // size_x, 128), LINK)],
        [pooled, core, inside, low_fwd, lift, adj, kids, cx, dge, encoded],
        spaces={1: pltpu.SMEM, 2: pltpu.SMEM},
    )
    halo = swapped(*edges, GX)
    eg, keep, send, *edges = call(
        encoder_grad_kernel,
        [(brick, BF16), (half, LINK), (half, LINK)] + [((32, 128), BF16)] * 2,
        [
            ((3, 6, 16, 128), BF16),
            ((128, 64), F32),
            ((2, size_x, 512 // size_x, 128), LINK),
        ],
        [lg, *halo, core, low_bwd, slope, jg, fx, keep, send],
        spaces={3: pltpu.SMEM},
        aliases={8: 1, 9: 2},
    )
    (sums,) = call(add_kernel, [(half, LINK)], [], [keep, partner(send)])
    sums = lax.all_to_all(sums, "gx", 0, 0)
    (sums,) = call(sum_kernel, [((size_z,) + half[1:], LINK)], [], [sums])
    sums = lax.all_to_all(sums, "gz", 0, 0)
    (sums,) = call(sum_kernel, [(half, LINK)], [], [sums])
    sums, edges = lax.optimization_barrier((sums, edges))
    sums = lax.all_to_all(sums, "gx", 0, 0)
    y_halo = swapped(*edges, GY)
    edges = call(edge_x_kernel, [((160, 128), BF16)] * 2, [], [eg, *y_halo])
    eg_halo = [*y_halo, *swapped(*edges, GX)]
    (decoded,) = call(
        decode_kernel,
        [(brick, BF16)],
        [((4, 10, 32, 128), BF16), ((320, 64), F32)],
        [encoded, lifted, *halo, lift, dec_fwd],
    )
    (input_grad,) = call(
        input_grad_kernel,
        [(brick, BF16)],
        [((4, 10, 32, 64), BF16)],
        [eg, *eg_halo, enc_bwd],
    )
    sums, decoded, input_grad = lax.optimization_barrier((sums, decoded, input_grad))
    encoder_gradient, decoder_gradient, lower_gradient, lift_gradient = call(
        widen_kernel,
        [((27, 64, 64), F32), ((27, 64, 128), F32), ((27, 64, 128), F32), ((8, 64, 128), F32)],
        [],
        [core, sums, partner(sums)],
        spaces={0: pltpu.SMEM},
    )
    return (
        jnp.transpose(decoded, (3, 0, 1, 2)),
        jnp.transpose(input_grad, (3, 0, 1, 2)),
        encoder_gradient,
        jnp.transpose(lower_gradient, (0, 2, 1)),
        lift_gradient,
        decoder_gradient,
    )


def solution(mesh):
    size_x, size_y = mesh.devices.shape
    chips = Mesh(mesh.devices.reshape(size_x, size_y // 2, 2), ("gx", "gz", "gc"))
    field = P(None, "gx", ("gz", "gc"), None)
    return jax.shard_map(
        per_device,
        mesh=chips,
        in_specs=(field, P(), P(), P(), P(), field),
        out_specs=(field, field, P(), P(), P(), P()),
        check_vma=False,
    )
```

```python
import math

import jax
import jax.numpy as jnp
from jax import lax
from jax.experimental import pallas as pl
from jax.experimental.pallas import tpu as pltpu
from jax.sharding import Mesh, PartitionSpec as P

F32, BF16 = jnp.float32, jnp.bfloat16
LINK = BF16
GX, GY = ("gx",), ("gz", "gc")
TAPS9 = tuple((a, b) for a in range(3) for b in range(3))


def shifted(piece, axes, step):
    size = math.prod(lax.axis_size(axis) for axis in axes)
    pairs = [(i, i + step) for i in range(size) if 0 <= i + step < size]
    return lax.ppermute(piece, axes, pairs)


def swapped(low, high, axes):
    return shifted(high, axes, 1), shifted(low, axes, -1)


def partner(piece):
    return lax.ppermute(piece, "gc", [(0, 1), (1, 0)])


def call(kernel, outs, scratch, operands, spaces=(), flops=10**6, aliases=()):
    return pl.pallas_call(
        kernel,
        out_shape=[jax.ShapeDtypeStruct(s, d) for s, d in outs],
        in_specs=[
            pl.BlockSpec(memory_space=dict(spaces).get(i, pltpu.VMEM)) for i in range(len(operands))
        ],
        out_specs=[pl.BlockSpec(memory_space=pltpu.VMEM)] * len(outs),
        scratch_shapes=[s if d is None else pltpu.VMEM(s, d) for s, d in scratch],
        input_output_aliases=dict(aliases),
        compiler_params=pltpu.CompilerParams(vmem_limit_bytes=40 * 2**20),
        cost_estimate=pl.CostEstimate(flops=flops, bytes_accessed=10**4, transcendentals=0),
    )(*operands)


def nn(a, b):
    return lax.dot_general(a, b, (((1,), (0,)), ((), ())), preferred_element_type=F32)


def nt(a, b):
    return lax.dot_general(a, b, (((1,), (1,)), ((), ())), preferred_element_type=F32)


def tn(a, b):
    return lax.dot_general(a, b, (((0,), (0,)), ((), ())), preferred_element_type=F32)


def nn_weight(ref):
    rows = [jnp.concatenate([ref[3 * ab + c] for c in range(3)], -1) for ab in range(9)]
    return jnp.concatenate(rows, 0)


def nt_weight(ref):
    rows = [jnp.concatenate([ref[3 * ab + c] for ab in range(9)], -1) for c in range(3)]
    return jnp.concatenate(rows, 0)


def stacked(ref, x, nx, ny, adjoint, y=0):
    pieces = []
    for a, b in TAPS9:
        i, j = (x + 2 - a, y + 2 - b) if adjoint else (x + a, y + b)
        piece = ref[i : i + nx, j : j + ny]
        pieces.append(piece.reshape(nx * ny * piece.shape[2], piece.shape[3]))
    return jnp.concatenate(pieces, -1)


def zshift(value, step, depth):
    rows = value.shape[0]
    z = lax.broadcasted_iota(jnp.int32, value.shape, 0) & (depth - 1)
    moved = pltpu.roll(value, step % rows, 0)
    return jnp.where(z == (0 if step > 0 else depth - 1), 0.0, moved)


def combined(parts, depth, adjoint):
    ch = parts.shape[1] // 3
    step = -1 if adjoint else 1
    return (
        zshift(parts[:, :ch], step, depth)
        + parts[:, ch : 2 * ch]
        + zshift(parts[:, 2 * ch :], -step, depth)
    )


def ztaps(value, depth, adjoint):
    step = -1 if adjoint else 1
    return jnp.concatenate(
        [
            zshift(value, step, depth).astype(BF16),
            value.astype(BF16),
            zshift(value, -step, depth).astype(BF16),
        ],
        -1,
    )


def assemble(ext, own, ylo, yhi, xlo, xhi):
    size_x, size_y = own.shape[:2]
    ext[1 : 1 + size_x, 1 : 1 + size_y] = own
    ext[1 : 1 + size_x, 0:1] = ylo
    ext[1 : 1 + size_x, 1 + size_y : 2 + size_y] = yhi
    ext[0:1] = xlo
    ext[1 + size_x : 2 + size_x] = xhi


def fetched(sems, *pairs):
    copies = [pltpu.make_async_copy(a, b, sems.at[k]) for k, (a, b) in enumerate(pairs)]
    for copy in copies:
        copy.start()
    for copy in copies:
        copy.wait()


def stack_kernel(first_ref, second_ref, enc_ref, low_ref, dec_ref, lift_ref, *refs):
    outs, lift_out, (enc, low, dec, sems) = refs[:6], refs[6], refs[7:]
    fetched(sems, (enc_ref, enc), (low_ref, low), (dec_ref, dec), (lift_ref, lift_out))
    for ref, forward, backward in (
        (enc, nt_weight, nn_weight),
        (low, nn_weight, nt_weight),
        (dec, nt_weight, nn_weight),
    ):
        outs[0][...] = forward(ref)
        outs[1][...] = backward(ref)
        outs = outs[2:]


def pack_x_kernel(f_any, c_any, f_ref, c_ref, lo_ref, hi_ref, lo2_ref, hi2_ref, sems):
    fetched(sems, (f_any, f_ref), (c_any, c_ref))
    paired = [jnp.concatenate([f_ref[x, 0:4], f_ref[x, 4:8]], -1) for x in range(2)]
    for x, out, out2 in ((0, lo_ref, lo2_ref), (1, hi_ref, hi2_ref)):
        out[0:8] = jnp.concatenate([f_ref[x], c_ref[x]], -1)
        out[8:12] = paired[1 - x]
        out2[...] = paired[x]


def pack_y_kernel(f_ref, c_ref, xlo, xhi, xlo2, xhi2, after_ref, lo_ref, hi_ref):
    for first, out in ((0, lo_ref), (3, hi_ref)):
        at = slice(first, first + 5)
        out[0] = xlo[at]
        for x in range(2):
            out[1 + x] = jnp.concatenate([f_ref[x, at], c_ref[x, at]], -1)
        out[3] = xhi[at]
        for k, far, near in ((4, xlo2[...], xlo[8:12]), (5, xhi[8:12], xhi2[...])):
            pair = [jnp.concatenate([v[..., :64], v[..., 64:]], 0)[at] for v in (far, near)]
            out[k] = jnp.concatenate(pair, -1)


def encode_kernel(
    f_ref, ylo, yhi, xlo, xhi, xlo2, xhi2, inside, w_ref, fx_ref, enc_ref, slope_ref, pool_ref, tmp
):
    fx_ref[3:5, 5:13] = f_ref[...]
    fx_ref[2, 5:13] = xlo[0:8, :, :64]
    fx_ref[5, 5:13] = xhi[0:8, :, :64]
    for x, ref, first in ((1, xlo, 8), (6, xhi, 8), (0, xlo2, 0), (7, xhi2, 0)):
        fx_ref[x, 5:9] = ref[first : first + 4, :, :64]
        fx_ref[x, 9:13] = ref[first : first + 4, :, 64:]
    for y, ref in ((0, ylo), (13, yhi)):
        at = slice(y, y + 5)
        fx_ref[2:6, at] = ref[0:4, :, :, :64]
        for x, k in ((0, 4), (6, 5)):
            fx_ref[x, at] = ref[k, :, :, :64]
            fx_ref[x + 1, at] = ref[k, :, :, 64:]
    weight = w_ref[...]
    for x in range(6):
        pre = combined(nt(stacked(fx_ref, x, 1, 16, False), weight), 32, False)
        sigma = jax.nn.sigmoid(pre)
        enc = (pre * sigma).astype(BF16)
        if x in (2, 3):
            slope = sigma * (1.0 + pre * (1.0 - sigma))
            slope_ref[pl.ds((x - 2) * 256, 256), :] = slope[128:384]
            enc_ref[x - 2, 1:9] = enc[128:384].reshape(8, 32, 64)
            enc_ref[x - 2, 0] = (enc[96:128].astype(F32) * inside[2]).astype(BF16)
            enc_ref[x - 2, 9] = (enc[384:416].astype(F32) * inside[3]).astype(BF16)
        wide = enc.astype(F32).reshape(8, 2, 32, 64)
        part = wide[:, 0] + wide[:, 1]
        if x % 2 == 0:
            held = part
            continue
        tmp[...] = (held + part).reshape(256, 64)
        pooled = tmp[pl.ds(0, 128, stride=2), :] + tmp[pl.ds(1, 128, stride=2), :]
        pooled = pooled * (0.125 if x == 3 else 0.125 * inside[0 if x == 1 else 1])
        pool_ref[x // 2, 2:6] = pooled[32:96].astype(BF16).reshape(4, 16, 64)
        pool_ref[x // 2, 0:2] = (pooled[0:32] * inside[2]).astype(BF16).reshape(2, 16, 64)
        pool_ref[x // 2, 6:8] = (pooled[96:128] * inside[3]).astype(BF16).reshape(2, 16, 64)


def joined_grad_kernel(c_ref, *refs):
    (ylo, yhi, xlo, xhi), (w_ref, lift_ref) = refs[:4], refs[4:6]
    cx_ref, jg_ref, kids_ref, adj_ref, tmp = refs[6:]
    cx_ref[1:3, 3:11] = c_ref[...]
    cx_ref[0, 3:11] = xlo[0:8, :, 64:]
    cx_ref[3, 3:11] = xhi[0:8, :, 64:]
    cx_ref[:, 0:3] = ylo[0:4, 2:5, :, 64:]
    cx_ref[:, 11:14] = yhi[0:4, 0:3, :, 64:]
    weight = w_ref[...]
    for x in range(2):
        grad = combined(nn(stacked(cx_ref, x, 1, 12, True), weight), 32, True)
        grad = grad.astype(BF16)
        jg_ref[pl.ds(x * 256, 256), :] = grad[64:320, :64]
        tmp[pl.ds(x * 384, 384), :] = grad.astype(F32)
    kids = []
    for p in range(2):
        for q in range(2):
            for r in range(2):
                rows = [
                    tmp[pl.ds(p * 384 + (2 * j + q) * 32 + r, 16, stride=2), :] for j in range(6)
                ]
                kids.append(jnp.concatenate(rows, 0)[:, 64:])
    kids = jnp.concatenate(kids, -1).astype(BF16)
    kids_ref[...] = kids[16:80]
    adj_ref[...] = nn(kids, lift_ref[...].reshape(512, 128))


def halver(halves):
    chunk = halves.shape[2]

    def put(row, block):
        at = pl.ds(row % chunk, block.shape[0])
        halves[row // chunk % 2, row // (2 * chunk), at, :] = block.astype(LINK)

    return put


def lower_kernel(px, inside, w_ref, adj_ref, la_ref, lg_ref):
    def masked(value):
        first, last = value[0:16] * inside[2], value[80:96] * inside[3]
        return jnp.concatenate([first, value[16:80], last], 0).astype(BF16)

    pre = combined(nn(stacked(px, 0, 1, 6, False), w_ref[...]), 16, False)
    sigma = jax.nn.sigmoid(pre)
    la_ref[...] = masked(pre * sigma)
    lg_ref[...] = masked(adj_ref[...] * (sigma * (1.0 + pre * (1.0 - sigma))))


def grads_kernel(px, la_ref, lg_ref, core, lift_ref, kids_ref, cx_ref, enc_ref, *refs):
    lifted_ref, keep_ref, send_ref, tmp, halves = refs
    put = halver(halves)
    la, lg = la_ref[...], lg_ref[...]
    fine = nt(la, lift_ref[...].reshape(512, 128)).astype(BF16).astype(F32)
    for p in range(2):
        for q in range(2):
            for r in range(2):
                k = 4 * p + 2 * q + r
                for j in range(6):
                    y = 2 * j + q - 1
                    if 0 <= y < 10:
                        tmp[pl.ds((p * 10 + y) * 32 + r, 16, stride=2), :] = fine[
                            16 * j : 16 * j + 16, 64 * k : 64 * k + 64
                        ]
    lifted_ref[...] = tmp[...].astype(BF16).reshape(2, 10, 32, 64)
    lifted = jnp.concatenate([tmp[32:288], tmp[352:608]], 0)
    la, lg = la[16:80], lg[16:80]
    enc = enc_ref[:, 1:9].reshape(512, 64).astype(F32)
    joined = ztaps(jnp.concatenate([enc, lifted], -1), 32, False)
    dec = tn(stacked(cx_ref, 0, 2, 8, True, 2), joined)
    for ab in range(9):
        for c in range(3):
            block = dec[64 * ab : 64 * ab + 64, 128 * c : 128 * c + 128]
            put((3 * ab + c) * 64, block)
    low = tn(stacked(px, 0, 1, 4, False, 1), ztaps(lg.astype(F32), 16, True))
    for ab in range(9):
        for c in range(3):
            block = low[64 * ab : 64 * ab + 64, 128 * c : 128 * c + 128]
            put(1728 + (3 * ab + c) * 64, block)
    lift = tn(kids_ref[...], la)
    for k in range(8):
        put(3456 + 64 * k, lift[64 * k : 64 * k + 64])
    for row in (3968, 4032):
        put(row, jnp.zeros((64, 128), F32))
    mine, chunk = core[0], halves.shape[2]
    keep_ref[:, :chunk, :] = halves[mine]
    send_ref[:, :chunk, :] = halves[1 - mine]


def add_kernel(a_ref, b_ref, out_ref):
    out_ref[...] = (a_ref[...].astype(F32) + b_ref[...].astype(F32)).astype(LINK)


def edge_y_kernel(eg_ref, lo_ref, hi_ref):
    lo_ref[...] = jnp.concatenate([eg_ref[0, 0], eg_ref[1, 0]], -1)
    hi_ref[...] = jnp.concatenate([eg_ref[0, 7], eg_ref[1, 7]], -1)


def edge_x_kernel(eg_ref, enc_ref, la_ref, ylo_ref, yhi_ref, lo_ref, hi_ref):
    for x, out in ((0, lo_ref), (1, hi_ref)):
        cols = slice(64 * x, 64 * x + 64)
        eg = eg_ref[x].reshape(256, 64)
        first = jnp.concatenate([ylo_ref[:, cols], eg[:128]], 0)
        second = jnp.concatenate([eg[128:], yhi_ref[:, cols]], 0)
        out[0:160] = jnp.concatenate([first, second], -1)
        enc = enc_ref[x].reshape(320, 64)
        out[160:320] = jnp.concatenate([enc[:160], enc[160:]], -1)
        out[320:416] = la_ref[...]


def column(rows):
    return jnp.stack([rows[:, :64], rows[:, 64:]], 0).reshape(2, 1, 32, 64)


def plane(rows):
    return jnp.concatenate([rows[:, :64], rows[:, 64:]], 0).reshape(1, 10, 32, 64)


def encoder_grad_kernel(lg_ref, xlo, xhi, core, w_ref, slope_ref, jg_ref, fx_ref, *refs):
    eg_ref, keep_ref, send_ref, lo_ref, hi_ref, lx, tmp, halves = refs[2:]
    put = halver(halves)
    lx[0] = xlo[...].reshape(6, 16, 128)
    lx[1] = lg_ref[...].reshape(6, 16, 128)
    lx[2] = xhi[...].reshape(6, 16, 128)
    pg = combined(nt(stacked(lx, 0, 1, 4, True), w_ref[...]), 16, True)
    pg = pg.astype(BF16).astype(F32) * 0.125
    tmp[pl.ds(0, 64, stride=2), :] = pg
    tmp[pl.ds(1, 64, stride=2), :] = pg
    wide = tmp[...].reshape(1, 4, 1, 32, 64)
    wide = jnp.broadcast_to(wide, (2, 4, 2, 32, 64)).reshape(512, 64)
    eg = ((jg_ref[...].astype(F32) + wide) * slope_ref[...]).astype(BF16)
    eg_ref[...] = eg.reshape(2, 8, 32, 64)
    edge_y_kernel(eg_ref, lo_ref, hi_ref)
    grad = tn(ztaps(eg.astype(F32), 32, True), stacked(fx_ref, 2, 2, 8, False, 4))
    for ab in range(9):
        for c in range(3):
            block = grad[64 * c : 64 * c + 64, 64 * ab : 64 * ab + 64]
            block = jnp.concatenate([block[:32], block[32:]], -1)
            put((3 * ab + c) * 32, block[:16])
            put((3 * ab + c) * 32 + 16, block[16:])
    for row in range(864, 1024, 16):
        put(row, jnp.zeros((16, 128), F32))
    mine, chunk = core[0], keep_ref.shape[1] - halves.shape[2]
    keep_ref[:, chunk:, :] = halves[mine]
    send_ref[:, chunk:, :] = halves[1 - mine]


def decode_kernel(enc_ref, lifted_ref, xlo, xhi, lift_ref, w_ref, out_ref, jx, tx):
    jx[1:3] = jnp.concatenate([enc_ref[...], lifted_ref[...]], -1)
    for p, h in ((1, xlo), (0, xhi)):
        for q in range(2):
            for r in range(2):
                fine = nt(h[320:416], lift_ref[4 * p + 2 * q + r]).astype(BF16).astype(F32)
                for j in range(6):
                    y = 2 * j + q - 1
                    if 0 <= y < 10:
                        tx[pl.ds(32 * y + r, 16, stride=2), :] = fine[16 * j : 16 * j + 16]
        lifted = tx[...].astype(BF16).reshape(1, 10, 32, 64)
        x = 0 if p == 1 else 3
        jx[x : x + 1] = jnp.concatenate([plane(h[160:320]), lifted], -1)
    weight = w_ref[...]
    for x in range(2):
        out = combined(nt(stacked(jx, x, 1, 8, False), weight), 32, False)
        out_ref[x] = out.astype(BF16).reshape(8, 32, 64)


def input_grad_kernel(eg_ref, ylo, yhi, xlo, xhi, w_ref, out_ref, ex):
    sides = [column(ylo[...]), column(yhi[...]), plane(xlo[0:160]), plane(xhi[0:160])]
    assemble(ex, eg_ref[...], *sides)
    weight = w_ref[...]
    for x in range(2):
        out = combined(nn(stacked(ex, x, 1, 8, True), weight), 32, True)
        out_ref[x] = out.astype(BF16).reshape(8, 32, 64)


def sum_kernel(parts_ref, out_ref):
    total = parts_ref[0].astype(F32)
    for k in range(1, parts_ref.shape[0]):
        total = total + parts_ref[k].astype(F32)
    total = total.astype(LINK)
    for k in range(out_ref.shape[0]):
        out_ref[k] = total


def widen_kernel(core, own_ref, other_ref, encoder_ref, decoder_ref, lower_ref, lift_ref):
    own, other = own_ref[...].astype(F32), other_ref[...].astype(F32)
    first = core[0] == 0
    both = jnp.stack([jnp.where(first, own, other), jnp.where(first, other, own)], 1)
    chunk = own.shape[1] // 5 * 4
    sums = both[:, :, :chunk].reshape(4096, 128)
    decoder_ref[...] = sums[0:1728].reshape(27, 64, 128)
    lower_ref[...] = sums[1728:3456].reshape(27, 64, 128)
    lift_ref[...] = sums[3456:3968].reshape(8, 64, 128)
    wide = both[:, :, chunk:].reshape(1024, 128)[:864].reshape(27, 32, 128)
    encoder_ref[:, 0:32, :] = wide[..., :64]
    encoder_ref[:, 32:64, :] = wide[..., 64:]


def per_device(features, encoder_weight, lower_weight, lift_weight, decoder_weight, cotangent):
    f = jnp.transpose(features, (1, 2, 3, 0))
    c = jnp.transpose(cotangent, (1, 2, 3, 0))
    lower_t = jnp.transpose(lower_weight, (0, 2, 1))
    brick, tall = (2, 8, 32, 64), (2, 10, 32, 64)

    size_x, size_z = lax.axis_size("gx"), lax.axis_size("gz")
    at_x, at_y = lax.axis_index("gx"), lax.axis_index(GY)
    inside = jnp.stack([at_x > 0, at_x < size_x - 1, at_y > 0, at_y < 2 * size_z - 1]).astype(F32)
    core = lax.axis_index("gc").reshape(1)

    f, c, lo, hi, lo2, hi2 = call(
        pack_x_kernel,
        [(brick, BF16)] * 2 + [((12, 32, 128), BF16)] * 2 + [((4, 32, 128), BF16)] * 2,
        [(pltpu.SemaphoreType.DMA((2,)), None)],
        [f, c],
        spaces={0: pltpu.HBM, 1: pltpu.HBM},
    )
    x_halo = swapped(lo, hi, GX)
    far_halo = [shifted(hi2, GX, 2), shifted(lo2, GX, -2)]
    enc_fwd, enc_bwd, low_fwd, low_bwd, dec_fwd, dec_bwd, lift = call(
        stack_kernel,
        [
            ((192, 576), BF16),
            ((576, 192), BF16),
            ((576, 384), BF16),
            ((192, 1152), BF16),
            ((192, 1152), BF16),
            ((576, 384), BF16),
            ((8, 64, 128), BF16),
        ],
        [
            ((27, 64, 64), BF16),
            ((27, 64, 128), BF16),
            ((27, 64, 128), BF16),
            (pltpu.SemaphoreType.DMA((4,)), None),
        ],
        [*x_halo, encoder_weight, lower_t, decoder_weight, lift_weight],
        spaces={k: pltpu.HBM for k in range(6)},
        flops=2 * 10**9,
    )
    edges = call(
        pack_y_kernel,
        [((6, 5, 32, 128), BF16)] * 2,
        [],
        [f, c, *x_halo, *far_halo, enc_fwd],
        spaces={6: pltpu.HBM},
    )
    y_halo = swapped(*edges, GY)
    fx, encoded, slope, pooled = call(
        encode_kernel,
        [((8, 18, 32, 64), BF16), (tall, BF16), ((512, 64), F32), ((3, 8, 16, 64), BF16)],
        [((256, 64), F32)],
        [f, *y_halo, *x_halo, *far_halo, inside, enc_fwd],
        spaces={7: pltpu.SMEM},
    )
    cx, jg, kids, adj = call(
        joined_grad_kernel,
        [
            ((4, 14, 32, 64), BF16),
            ((512, 64), BF16),
            ((64, 512), BF16),
            ((96, 128), F32),
        ],
        [((768, 128), F32)],
        [c, *y_halo, *x_halo, dec_bwd, lift],
    )
    half = (size_x, 2560 // size_x, 128)
    la, lg = call(
        lower_kernel,
        [((96, 128), BF16)] * 2,
        [],
        [pooled, inside, low_fwd, adj],
        spaces={1: pltpu.SMEM},
    )
    halo = swapped(lg, lg, GX)
    lifted, keep, send = call(
        grads_kernel,
        [(tall, BF16), (half, LINK), (half, LINK)],
        [((640, 64), F32), ((2, size_x, 2048 // size_x, 128), LINK)],
        [pooled, la, lg, core, lift, kids, cx, encoded],
        spaces={3: pltpu.SMEM},
        flops=2 * 10**9,
    )
    eg, keep, send, *edges = call(
        encoder_grad_kernel,
        [(brick, BF16), (half, LINK), (half, LINK)] + [((32, 128), BF16)] * 2,
        [
            ((3, 6, 16, 128), BF16),
            ((128, 64), F32),
            ((2, size_x, 512 // size_x, 128), LINK),
        ],
        [lg, *halo, core, low_bwd, slope, jg, fx, keep, send],
        spaces={3: pltpu.SMEM},
        aliases={8: 1, 9: 2},
    )
    (sums,) = call(add_kernel, [(half, LINK)], [], [keep, partner(send)])
    sums, edges = lax.optimization_barrier((sums, edges))
    sums = lax.all_to_all(sums, "gx", 0, 0)
    y_halo = swapped(*edges, GY)
    (sums,) = call(sum_kernel, [((size_z,) + half[1:], LINK)], [], [sums])
    sums, y_halo = lax.optimization_barrier((sums, y_halo))
    sums = lax.all_to_all(sums, "gz", 0, 0)
    edges = call(
        edge_x_kernel, [((416, 128), BF16)] * 2, [], [eg, encoded, la, *y_halo]
    )
    halo = swapped(*edges, GX)
    (sums,) = call(sum_kernel, [(half, LINK)], [], [sums])
    sums, halo = lax.optimization_barrier((sums, halo))
    sums = lax.all_to_all(sums, "gx", 0, 0)
    (decoded,) = call(
        decode_kernel,
        [(brick, BF16)],
        [((4, 10, 32, 128), BF16), ((320, 64), F32)],
        [encoded, lifted, *halo, lift, dec_fwd],
    )
    (input_grad,) = call(
        input_grad_kernel,
        [(brick, BF16)],
        [((4, 10, 32, 64), BF16)],
        [eg, *y_halo, *halo, enc_bwd],
    )
    sums, decoded, input_grad = lax.optimization_barrier((sums, decoded, input_grad))
    encoder_gradient, decoder_gradient, lower_gradient, lift_gradient = call(
        widen_kernel,
        [((27, 64, 64), F32), ((27, 64, 128), F32), ((27, 64, 128), F32), ((8, 64, 128), F32)],
        [],
        [core, sums, partner(sums)],
        spaces={0: pltpu.SMEM},
    )
    return (
        jnp.transpose(decoded, (3, 0, 1, 2)),
        jnp.transpose(input_grad, (3, 0, 1, 2)),
        encoder_gradient,
        jnp.transpose(lower_gradient, (0, 2, 1)),
        lift_gradient,
        decoder_gradient,
    )


def solution(mesh):
    size_x, size_y = mesh.devices.shape
    chips = Mesh(mesh.devices.reshape(size_x, size_y // 2, 2), ("gx", "gz", "gc"))
    field = P(None, "gx", ("gz", "gc"), None)
    return jax.shard_map(
        per_device,
        mesh=chips,
        in_specs=(field, P(), P(), P(), P(), field),
        out_specs=(field, field, P(), P(), P(), P()),
        check_vma=False,
    )
```

```python
import math

import jax
import jax.numpy as jnp
from jax import lax
from jax.experimental import pallas as pl
from jax.experimental.pallas import tpu as pltpu
from jax.sharding import Mesh, PartitionSpec as P

F32, BF16 = jnp.float32, jnp.bfloat16
LINK = BF16
GX, GY = ("gx",), ("gz", "gc")
TAPS9 = tuple((a, b) for a in range(3) for b in range(3))


def shifted(piece, axes, step):
    size = math.prod(lax.axis_size(axis) for axis in axes)
    pairs = [(i, i + step) for i in range(size) if 0 <= i + step < size]
    return lax.ppermute(piece, axes, pairs)


def swapped(low, high, axes):
    return shifted(high, axes, 1), shifted(low, axes, -1)


def partner(piece):
    return lax.ppermute(piece, "gc", [(0, 1), (1, 0)])


def call(kernel, outs, scratch, operands, spaces=(), flops=10**6, aliases=()):
    return pl.pallas_call(
        kernel,
        out_shape=[jax.ShapeDtypeStruct(s, d) for s, d in outs],
        in_specs=[
            pl.BlockSpec(memory_space=dict(spaces).get(i, pltpu.VMEM)) for i in range(len(operands))
        ],
        out_specs=[pl.BlockSpec(memory_space=pltpu.VMEM)] * len(outs),
        scratch_shapes=[s if d is None else pltpu.VMEM(s, d) for s, d in scratch],
        input_output_aliases=dict(aliases),
        compiler_params=pltpu.CompilerParams(vmem_limit_bytes=40 * 2**20),
        cost_estimate=pl.CostEstimate(flops=flops, bytes_accessed=10**4, transcendentals=0),
    )(*operands)


def nn(a, b):
    return lax.dot_general(a, b, (((1,), (0,)), ((), ())), preferred_element_type=F32)


def nt(a, b):
    return lax.dot_general(a, b, (((1,), (1,)), ((), ())), preferred_element_type=F32)


def tn(a, b):
    return lax.dot_general(a, b, (((0,), (0,)), ((), ())), preferred_element_type=F32)


def nn_weight(ref):
    rows = [jnp.concatenate([ref[3 * ab + c] for c in range(3)], -1) for ab in range(9)]
    return jnp.concatenate(rows, 0)


def nt_weight(ref):
    rows = [jnp.concatenate([ref[3 * ab + c] for ab in range(9)], -1) for c in range(3)]
    return jnp.concatenate(rows, 0)


def stacked(ref, x, nx, ny, adjoint, y=0):
    pieces = []
    for a, b in TAPS9:
        i, j = (x + 2 - a, y + 2 - b) if adjoint else (x + a, y + b)
        piece = ref[i : i + nx, j : j + ny]
        pieces.append(piece.reshape(nx * ny * piece.shape[2], piece.shape[3]))
    return jnp.concatenate(pieces, -1)


def zshift(value, step, depth):
    rows = value.shape[0]
    z = lax.broadcasted_iota(jnp.int32, value.shape, 0) & (depth - 1)
    moved = pltpu.roll(value, step % rows, 0)
    return jnp.where(z == (0 if step > 0 else depth - 1), 0.0, moved)


def combined(parts, depth, adjoint):
    ch = parts.shape[1] // 3
    step = -1 if adjoint else 1
    return (
        zshift(parts[:, :ch], step, depth)
        + parts[:, ch : 2 * ch]
        + zshift(parts[:, 2 * ch :], -step, depth)
    )


def ztaps(value, depth, adjoint):
    step = -1 if adjoint else 1
    return jnp.concatenate(
        [
            zshift(value, step, depth).astype(BF16),
            value.astype(BF16),
            zshift(value, -step, depth).astype(BF16),
        ],
        -1,
    )


def assemble(ext, own, ylo, yhi, xlo, xhi):
    size_x, size_y = own.shape[:2]
    ext[1 : 1 + size_x, 1 : 1 + size_y] = own
    ext[1 : 1 + size_x, 0:1] = ylo
    ext[1 : 1 + size_x, 1 + size_y : 2 + size_y] = yhi
    ext[0:1] = xlo
    ext[1 + size_x : 2 + size_x] = xhi


def fetched(sems, *pairs):
    copies = [pltpu.make_async_copy(a, b, sems.at[k]) for k, (a, b) in enumerate(pairs)]
    for copy in copies:
        copy.start()
    for copy in copies:
        copy.wait()


def stack_kernel(first_ref, enc_ref, low_ref, dec_ref, lift_ref, *refs):
    outs, lift_out, (enc, low, dec, sems) = refs[:6], refs[6], refs[7:]
    fetched(sems, (enc_ref, enc), (low_ref, low), (dec_ref, dec), (lift_ref, lift_out))
    for ref, forward, backward in (
        (enc, nt_weight, nn_weight),
        (low, nn_weight, nt_weight),
        (dec, nt_weight, nn_weight),
    ):
        outs[0][...] = forward(ref)
        outs[1][...] = backward(ref)
        outs = outs[2:]


def pack_x_kernel(f_any, c_any, f_ref, c_ref, lo_ref, hi_ref, lo2_ref, hi2_ref, sems):
    fetched(sems, (f_any, f_ref), (c_any, c_ref))
    paired = [jnp.concatenate([f_ref[x, 0:4], f_ref[x, 4:8]], -1) for x in range(2)]
    for x, out, out2 in ((0, lo_ref, lo2_ref), (1, hi_ref, hi2_ref)):
        out[0:8] = jnp.concatenate([f_ref[x], c_ref[x]], -1)
        out[8:12] = paired[1 - x]
        out2[...] = paired[x]


def pack_y_kernel(f_ref, c_ref, xlo, xhi, xlo2, xhi2, lo_ref, hi_ref):
    for first, out in ((0, lo_ref), (3, hi_ref)):
        at = slice(first, first + 5)
        out[0] = xlo[at]
        for x in range(2):
            out[1 + x] = jnp.concatenate([f_ref[x, at], c_ref[x, at]], -1)
        out[3] = xhi[at]
        for k, far, near in ((4, xlo2[...], xlo[8:12]), (5, xhi[8:12], xhi2[...])):
            pair = [jnp.concatenate([v[..., :64], v[..., 64:]], 0)[at] for v in (far, near)]
            out[k] = jnp.concatenate(pair, -1)


def encode_kernel(
    f_ref, ylo, yhi, xlo, xhi, xlo2, xhi2, inside, w_ref, fx_ref, enc_ref, slope_ref, pool_ref, tmp
):
    fx_ref[3:5, 5:13] = f_ref[...]
    fx_ref[2, 5:13] = xlo[0:8, :, :64]
    fx_ref[5, 5:13] = xhi[0:8, :, :64]
    for x, ref, first in ((1, xlo, 8), (6, xhi, 8), (0, xlo2, 0), (7, xhi2, 0)):
        fx_ref[x, 5:9] = ref[first : first + 4, :, :64]
        fx_ref[x, 9:13] = ref[first : first + 4, :, 64:]
    for y, ref in ((0, ylo), (13, yhi)):
        at = slice(y, y + 5)
        fx_ref[2:6, at] = ref[0:4, :, :, :64]
        for x, k in ((0, 4), (6, 5)):
            fx_ref[x, at] = ref[k, :, :, :64]
            fx_ref[x + 1, at] = ref[k, :, :, 64:]
    weight = w_ref[...]
    for x in range(6):
        pre = combined(nt(stacked(fx_ref, x, 1, 16, False), weight), 32, False)
        sigma = jax.nn.sigmoid(pre)
        enc = (pre * sigma).astype(BF16)
        if x in (2, 3):
            slope = sigma * (1.0 + pre * (1.0 - sigma))
            slope_ref[pl.ds((x - 2) * 256, 256), :] = slope[128:384]
            enc_ref[x - 2, 1:9] = enc[128:384].reshape(8, 32, 64)
            enc_ref[x - 2, 0] = (enc[96:128].astype(F32) * inside[2]).astype(BF16)
            enc_ref[x - 2, 9] = (enc[384:416].astype(F32) * inside[3]).astype(BF16)
        wide = enc.astype(F32).reshape(8, 2, 32, 64)
        part = wide[:, 0] + wide[:, 1]
        if x % 2 == 0:
            held = part
            continue
        tmp[...] = (held + part).reshape(256, 64)
        pooled = tmp[pl.ds(0, 128, stride=2), :] + tmp[pl.ds(1, 128, stride=2), :]
        pooled = pooled * (0.125 if x == 3 else 0.125 * inside[0 if x == 1 else 1])
        pool_ref[x // 2, 2:6] = pooled[32:96].astype(BF16).reshape(4, 16, 64)
        pool_ref[x // 2, 0:2] = (pooled[0:32] * inside[2]).astype(BF16).reshape(2, 16, 64)
        pool_ref[x // 2, 6:8] = (pooled[96:128] * inside[3]).astype(BF16).reshape(2, 16, 64)


def joined_grad_kernel(c_ref, *refs):
    (ylo, yhi, xlo, xhi), (w_ref, lift_ref) = refs[:4], refs[4:6]
    cx_ref, jg_ref, kids_ref, adj_ref, tmp = refs[6:]
    cx_ref[1:3, 3:11] = c_ref[...]
    cx_ref[0, 3:11] = xlo[0:8, :, 64:]
    cx_ref[3, 3:11] = xhi[0:8, :, 64:]
    cx_ref[:, 0:3] = ylo[0:4, 2:5, :, 64:]
    cx_ref[:, 11:14] = yhi[0:4, 0:3, :, 64:]
    weight = w_ref[...]
    for x in range(2):
        grad = combined(nn(stacked(cx_ref, x, 1, 12, True), weight), 32, True)
        grad = grad.astype(BF16)
        jg_ref[pl.ds(x * 256, 256), :] = grad[64:320, :64]
        tmp[pl.ds(x * 384, 384), :] = grad.astype(F32)
    kids = []
    for p in range(2):
        for q in range(2):
            for r in range(2):
                rows = [
                    tmp[pl.ds(p * 384 + (2 * j + q) * 32 + r, 16, stride=2), :] for j in range(6)
                ]
                kids.append(jnp.concatenate(rows, 0)[:, 64:])
    kids = jnp.concatenate(kids, -1).astype(BF16)
    kids_ref[...] = kids[16:80]
    adj_ref[...] = nn(kids, lift_ref[...].reshape(512, 128))


def halver(halves):
    chunk = halves.shape[2]

    def put(row, block):
        at = pl.ds(row % chunk, block.shape[0])
        halves[row // chunk % 2, row // (2 * chunk), at, :] = block.astype(LINK)

    return put


def lower_kernel(px, inside, w_ref, adj_ref, la_ref, lg_ref):
    def masked(value):
        first, last = value[0:16] * inside[2], value[80:96] * inside[3]
        return jnp.concatenate([first, value[16:80], last], 0).astype(BF16)

    pre = combined(nn(stacked(px, 0, 1, 6, False), w_ref[...]), 16, False)
    sigma = jax.nn.sigmoid(pre)
    la_ref[...] = masked(pre * sigma)
    lg_ref[...] = masked(adj_ref[...] * (sigma * (1.0 + pre * (1.0 - sigma))))


def grads_kernel(px, la_ref, lg_ref, core, lift_ref, kids_ref, cx_ref, enc_ref, *refs):
    lifted_ref, keep_ref, send_ref, tmp, halves = refs
    put = halver(halves)
    la, lg = la_ref[...], lg_ref[...]
    fine = nt(la, lift_ref[...].reshape(512, 128)).astype(BF16).astype(F32)
    for p in range(2):
        for q in range(2):
            for r in range(2):
                k = 4 * p + 2 * q + r
                for j in range(6):
                    y = 2 * j + q - 1
                    if 0 <= y < 10:
                        tmp[pl.ds((p * 10 + y) * 32 + r, 16, stride=2), :] = fine[
                            16 * j : 16 * j + 16, 64 * k : 64 * k + 64
                        ]
    lifted_ref[...] = tmp[...].astype(BF16).reshape(2, 10, 32, 64)
    lifted = jnp.concatenate([tmp[32:288], tmp[352:608]], 0)
    la, lg = la[16:80], lg[16:80]
    enc = enc_ref[:, 1:9].reshape(512, 64).astype(F32)
    joined = ztaps(jnp.concatenate([enc, lifted], -1), 32, False)
    dec = tn(stacked(cx_ref, 0, 2, 8, True, 2), joined)
    for ab in range(9):
        for c in range(3):
            block = dec[64 * ab : 64 * ab + 64, 128 * c : 128 * c + 128]
            put((3 * ab + c) * 64, block)
    low = tn(stacked(px, 0, 1, 4, False, 1), ztaps(lg.astype(F32), 16, True))
    for ab in range(9):
        for c in range(3):
            block = low[64 * ab : 64 * ab + 64, 128 * c : 128 * c + 128]
            put(1728 + (3 * ab + c) * 64, block)
    lift = tn(kids_ref[...], la)
    for k in range(8):
        put(3456 + 64 * k, lift[64 * k : 64 * k + 64])
    for row in (3968, 4032):
        put(row, jnp.zeros((64, 128), F32))
    mine, chunk = core[0], halves.shape[2]
    keep_ref[:, :chunk, :] = halves[mine]
    send_ref[:, :chunk, :] = halves[1 - mine]


def add_kernel(a_ref, b_ref, out_ref):
    out_ref[...] = (a_ref[...].astype(F32) + b_ref[...].astype(F32)).astype(LINK)


def edge_y_kernel(eg_ref, lo_ref, hi_ref):
    lo_ref[...] = jnp.concatenate([eg_ref[0, 0], eg_ref[1, 0]], -1)
    hi_ref[...] = jnp.concatenate([eg_ref[0, 7], eg_ref[1, 7]], -1)


def edge_x_kernel(eg_ref, enc_ref, la_ref, ylo_ref, yhi_ref, lo_ref, hi_ref):
    for x, out in ((0, lo_ref), (1, hi_ref)):
        cols = slice(64 * x, 64 * x + 64)
        eg = eg_ref[x].reshape(256, 64)
        first = jnp.concatenate([ylo_ref[:, cols], eg[:128]], 0)
        second = jnp.concatenate([eg[128:], yhi_ref[:, cols]], 0)
        out[0:160] = jnp.concatenate([first, second], -1)
        enc = enc_ref[x].reshape(320, 64)
        out[160:320] = jnp.concatenate([enc[:160], enc[160:]], -1)
        out[320:416] = la_ref[...]


def column(rows):
    return jnp.stack([rows[:, :64], rows[:, 64:]], 0).reshape(2, 1, 32, 64)


def plane(rows):
    return jnp.concatenate([rows[:, :64], rows[:, 64:]], 0).reshape(1, 10, 32, 64)


def encoder_grad_kernel(lg_ref, xlo, xhi, core, w_ref, slope_ref, jg_ref, fx_ref, *refs):
    eg_ref, keep_ref, send_ref, lo_ref, hi_ref, lx, tmp, halves = refs[2:]
    put = halver(halves)
    lx[0] = xlo[...].reshape(6, 16, 128)
    lx[1] = lg_ref[...].reshape(6, 16, 128)
    lx[2] = xhi[...].reshape(6, 16, 128)
    pg = combined(nt(stacked(lx, 0, 1, 4, True), w_ref[...]), 16, True)
    pg = pg.astype(BF16).astype(F32) * 0.125
    tmp[pl.ds(0, 64, stride=2), :] = pg
    tmp[pl.ds(1, 64, stride=2), :] = pg
    wide = tmp[...].reshape(1, 4, 1, 32, 64)
    wide = jnp.broadcast_to(wide, (2, 4, 2, 32, 64)).reshape(512, 64)
    eg = ((jg_ref[...].astype(F32) + wide) * slope_ref[...]).astype(BF16)
    eg_ref[...] = eg.reshape(2, 8, 32, 64)
    edge_y_kernel(eg_ref, lo_ref, hi_ref)
    grad = tn(ztaps(eg.astype(F32), 32, True), stacked(fx_ref, 2, 2, 8, False, 4))
    for ab in range(9):
        for c in range(3):
            block = grad[64 * c : 64 * c + 64, 64 * ab : 64 * ab + 64]
            block = jnp.concatenate([block[:32], block[32:]], -1)
            put((3 * ab + c) * 32, block[:16])
            put((3 * ab + c) * 32 + 16, block[16:])
    for row in range(864, 1024, 16):
        put(row, jnp.zeros((16, 128), F32))
    mine, chunk = core[0], keep_ref.shape[1] - halves.shape[2]
    keep_ref[:, chunk:, :] = halves[mine]
    send_ref[:, chunk:, :] = halves[1 - mine]


def decode_kernel(enc_ref, lifted_ref, xlo, xhi, lift_ref, w_ref, out_ref, jx, tx):
    jx[1:3] = jnp.concatenate([enc_ref[...], lifted_ref[...]], -1)
    for p, h in ((1, xlo), (0, xhi)):
        for q in range(2):
            for r in range(2):
                fine = nt(h[320:416], lift_ref[4 * p + 2 * q + r]).astype(BF16).astype(F32)
                for j in range(6):
                    y = 2 * j + q - 1
                    if 0 <= y < 10:
                        tx[pl.ds(32 * y + r, 16, stride=2), :] = fine[16 * j : 16 * j + 16]
        lifted = tx[...].astype(BF16).reshape(1, 10, 32, 64)
        x = 0 if p == 1 else 3
        jx[x : x + 1] = jnp.concatenate([plane(h[160:320]), lifted], -1)
    weight = w_ref[...]
    for x in range(2):
        out = combined(nt(stacked(jx, x, 1, 8, False), weight), 32, False)
        out_ref[x] = out.astype(BF16).reshape(8, 32, 64)


def input_grad_kernel(eg_ref, ylo, yhi, xlo, xhi, w_ref, out_ref, ex):
    sides = [column(ylo[...]), column(yhi[...]), plane(xlo[0:160]), plane(xhi[0:160])]
    assemble(ex, eg_ref[...], *sides)
    weight = w_ref[...]
    for x in range(2):
        out = combined(nn(stacked(ex, x, 1, 8, True), weight), 32, True)
        out_ref[x] = out.astype(BF16).reshape(8, 32, 64)


def sum_kernel(parts_ref, out_ref):
    total = parts_ref[0].astype(F32)
    for k in range(1, parts_ref.shape[0]):
        total = total + parts_ref[k].astype(F32)
    total = total.astype(LINK)
    for k in range(out_ref.shape[0]):
        out_ref[k] = total


def widen_kernel(core, own_ref, other_ref, encoder_ref, decoder_ref, lower_ref, lift_ref):
    own, other = own_ref[...].astype(F32), other_ref[...].astype(F32)
    first = core[0] == 0
    both = jnp.stack([jnp.where(first, own, other), jnp.where(first, other, own)], 1)
    chunk = own.shape[1] // 5 * 4
    sums = both[:, :, :chunk].reshape(4096, 128)
    decoder_ref[...] = sums[0:1728].reshape(27, 64, 128)
    lower_ref[...] = sums[1728:3456].reshape(27, 64, 128)
    lift_ref[...] = sums[3456:3968].reshape(8, 64, 128)
    wide = both[:, :, chunk:].reshape(1024, 128)[:864].reshape(27, 32, 128)
    encoder_ref[:, 0:32, :] = wide[..., :64]
    encoder_ref[:, 32:64, :] = wide[..., 64:]


def per_device(features, encoder_weight, lower_weight, lift_weight, decoder_weight, cotangent):
    f = jnp.transpose(features, (1, 2, 3, 0))
    c = jnp.transpose(cotangent, (1, 2, 3, 0))
    lower_t = jnp.transpose(lower_weight, (0, 2, 1))
    brick, tall = (2, 8, 32, 64), (2, 10, 32, 64)

    size_x, size_z = lax.axis_size("gx"), lax.axis_size("gz")
    at_x, at_y = lax.axis_index("gx"), lax.axis_index(GY)
    inside = jnp.stack([at_x > 0, at_x < size_x - 1, at_y > 0, at_y < 2 * size_z - 1]).astype(F32)
    core = lax.axis_index("gc").reshape(1)

    f, c, lo, hi, lo2, hi2 = call(
        pack_x_kernel,
        [(brick, BF16)] * 2 + [((12, 32, 128), BF16)] * 2 + [((4, 32, 128), BF16)] * 2,
        [(pltpu.SemaphoreType.DMA((2,)), None)],
        [f, c],
        spaces={0: pltpu.HBM, 1: pltpu.HBM},
    )
    x_halo = swapped(lo, hi, GX)
    far_halo = [shifted(hi2, GX, 2), shifted(lo2, GX, -2)]
    edges = call(
        pack_y_kernel,
        [((6, 5, 32, 128), BF16)] * 2,
        [],
        [f, c, *x_halo, *far_halo],
    )
    y_halo = swapped(*edges, GY)
    enc_fwd, enc_bwd, low_fwd, low_bwd, dec_fwd, dec_bwd, lift = call(
        stack_kernel,
        [
            ((192, 576), BF16),
            ((576, 192), BF16),
            ((576, 384), BF16),
            ((192, 1152), BF16),
            ((192, 1152), BF16),
            ((576, 384), BF16),
            ((8, 64, 128), BF16),
        ],
        [
            ((27, 64, 64), BF16),
            ((27, 64, 128), BF16),
            ((27, 64, 128), BF16),
            (pltpu.SemaphoreType.DMA((4,)), None),
        ],
        [edges[0], encoder_weight, lower_t, decoder_weight, lift_weight],
        spaces={k: pltpu.HBM for k in range(5)},
        flops=2 * 10**9,
    )
    fx, encoded, slope, pooled = call(
        encode_kernel,
        [((8, 18, 32, 64), BF16), (tall, BF16), ((512, 64), F32), ((3, 8, 16, 64), BF16)],
        [((256, 64), F32)],
        [f, *y_halo, *x_halo, *far_halo, inside, enc_fwd],
        spaces={7: pltpu.SMEM},
    )
    cx, jg, kids, adj = call(
        joined_grad_kernel,
        [
            ((4, 14, 32, 64), BF16),
            ((512, 64), BF16),
            ((64, 512), BF16),
            ((96, 128), F32),
        ],
        [((768, 128), F32)],
        [c, *y_halo, *x_halo, dec_bwd, lift],
    )
    half = (size_x, 2560 // size_x, 128)
    la, lg = call(
        lower_kernel,
        [((96, 128), BF16)] * 2,
        [],
        [pooled, inside, low_fwd, adj],
        spaces={1: pltpu.SMEM},
    )
    halo = swapped(lg, lg, GX)
    lifted, keep, send = call(
        grads_kernel,
        [(tall, BF16), (half, LINK), (half, LINK)],
        [((640, 64), F32), ((2, size_x, 2048 // size_x, 128), LINK)],
        [pooled, la, lg, core, lift, kids, cx, encoded],
        spaces={3: pltpu.SMEM},
        flops=2 * 10**9,
    )
    eg, keep, send, *edges = call(
        encoder_grad_kernel,
        [(brick, BF16), (half, LINK), (half, LINK)] + [((32, 128), BF16)] * 2,
        [
            ((3, 6, 16, 128), BF16),
            ((128, 64), F32),
            ((2, size_x, 512 // size_x, 128), LINK),
        ],
        [lg, *halo, core, low_bwd, slope, jg, fx, keep, send],
        spaces={3: pltpu.SMEM},
        aliases={8: 1, 9: 2},
    )
    (sums,) = call(add_kernel, [(half, LINK)], [], [keep, partner(send)])
    sums, edges = lax.optimization_barrier((sums, edges))
    sums = lax.all_to_all(sums, "gx", 0, 0)
    y_halo = swapped(*edges, GY)
    (sums,) = call(sum_kernel, [((size_z,) + half[1:], LINK)], [], [sums])
    sums, y_halo = lax.optimization_barrier((sums, y_halo))
    sums = lax.all_to_all(sums, "gz", 0, 0)
    edges = call(
        edge_x_kernel, [((416, 128), BF16)] * 2, [], [eg, encoded, la, *y_halo]
    )
    halo = swapped(*edges, GX)
    (sums,) = call(sum_kernel, [(half, LINK)], [], [sums])
    sums, halo = lax.optimization_barrier((sums, halo))
    sums = lax.all_to_all(sums, "gx", 0, 0)
    (decoded,) = call(
        decode_kernel,
        [(brick, BF16)],
        [((4, 10, 32, 128), BF16), ((320, 64), F32)],
        [encoded, lifted, *halo, lift, dec_fwd],
    )
    (input_grad,) = call(
        input_grad_kernel,
        [(brick, BF16)],
        [((4, 10, 32, 64), BF16)],
        [eg, *y_halo, *halo, enc_bwd],
    )
    sums, decoded, input_grad = lax.optimization_barrier((sums, decoded, input_grad))
    encoder_gradient, decoder_gradient, lower_gradient, lift_gradient = call(
        widen_kernel,
        [((27, 64, 64), F32), ((27, 64, 128), F32), ((27, 64, 128), F32), ((8, 64, 128), F32)],
        [],
        [core, sums, partner(sums)],
        spaces={0: pltpu.SMEM},
    )
    return (
        jnp.transpose(decoded, (3, 0, 1, 2)),
        jnp.transpose(input_grad, (3, 0, 1, 2)),
        encoder_gradient,
        jnp.transpose(lower_gradient, (0, 2, 1)),
        lift_gradient,
        decoder_gradient,
    )


def solution(mesh):
    size_x, size_y = mesh.devices.shape
    chips = Mesh(mesh.devices.reshape(size_x, size_y // 2, 2), ("gx", "gz", "gc"))
    field = P(None, "gx", ("gz", "gc"), None)
    return jax.shard_map(
        per_device,
        mesh=chips,
        in_specs=(field, P(), P(), P(), P(), field),
        out_specs=(field, field, P(), P(), P(), P()),
        check_vma=False,
    )
```

```python
import math

import jax
import jax.numpy as jnp
from jax import lax
from jax.experimental import pallas as pl
from jax.experimental.pallas import tpu as pltpu
from jax.sharding import Mesh, PartitionSpec as P

F32, BF16 = jnp.float32, jnp.bfloat16
LINK = BF16
GX, GY = ("gx",), ("gz", "gc")
TAPS9 = tuple((a, b) for a in range(3) for b in range(3))


def shifted(piece, axes, step):
    size = math.prod(lax.axis_size(axis) for axis in axes)
    pairs = [(i, i + step) for i in range(size) if 0 <= i + step < size]
    return lax.ppermute(piece, axes, pairs)


def swapped(low, high, axes):
    return shifted(high, axes, 1), shifted(low, axes, -1)


def partner(piece):
    return lax.ppermute(piece, "gc", [(0, 1), (1, 0)])


def call(kernel, outs, scratch, operands, spaces=(), flops=10**6):
    return pl.pallas_call(
        kernel,
        out_shape=[jax.ShapeDtypeStruct(s, d) for s, d in outs],
        in_specs=[
            pl.BlockSpec(memory_space=dict(spaces).get(i, pltpu.VMEM)) for i in range(len(operands))
        ],
        out_specs=[pl.BlockSpec(memory_space=pltpu.VMEM)] * len(outs),
        scratch_shapes=[s if d is None else pltpu.VMEM(s, d) for s, d in scratch],
        compiler_params=pltpu.CompilerParams(vmem_limit_bytes=40 * 2**20),
        cost_estimate=pl.CostEstimate(flops=flops, bytes_accessed=10**4, transcendentals=0),
    )(*operands)


def nn(a, b):
    return lax.dot_general(a, b, (((1,), (0,)), ((), ())), preferred_element_type=F32)


def nt(a, b):
    return lax.dot_general(a, b, (((1,), (1,)), ((), ())), preferred_element_type=F32)


def tn(a, b):
    return lax.dot_general(a, b, (((0,), (0,)), ((), ())), preferred_element_type=F32)


def nn_weight(ref):
    rows = [jnp.concatenate([ref[3 * ab + c] for c in range(3)], -1) for ab in range(9)]
    return jnp.concatenate(rows, 0)


def nt_weight(ref):
    rows = [jnp.concatenate([ref[3 * ab + c] for ab in range(9)], -1) for c in range(3)]
    return jnp.concatenate(rows, 0)


def stacked(ref, x, nx, ny, adjoint, y=0):
    pieces = []
    for a, b in TAPS9:
        i, j = (x + 2 - a, y + 2 - b) if adjoint else (x + a, y + b)
        piece = ref[i : i + nx, j : j + ny]
        pieces.append(piece.reshape(nx * ny * piece.shape[2], piece.shape[3]))
    return jnp.concatenate(pieces, -1)


def zshift(value, step, depth):
    rows = value.shape[0]
    z = lax.broadcasted_iota(jnp.int32, value.shape, 0) & (depth - 1)
    moved = pltpu.roll(value, step % rows, 0)
    return jnp.where(z == (0 if step > 0 else depth - 1), 0.0, moved)


def combined(parts, depth, adjoint):
    ch = parts.shape[1] // 3
    step = -1 if adjoint else 1
    return (
        zshift(parts[:, :ch], step, depth)
        + parts[:, ch : 2 * ch]
        + zshift(parts[:, 2 * ch :], -step, depth)
    )


def ztaps(value, depth, adjoint):
    step = -1 if adjoint else 1
    return jnp.concatenate(
        [
            zshift(value, step, depth).astype(BF16),
            value.astype(BF16),
            zshift(value, -step, depth).astype(BF16),
        ],
        -1,
    )


def assemble(ext, own, ylo, yhi, xlo, xhi):
    size_x, size_y = own.shape[:2]
    ext[1 : 1 + size_x, 1 : 1 + size_y] = own
    ext[1 : 1 + size_x, 0:1] = ylo
    ext[1 : 1 + size_x, 1 + size_y : 2 + size_y] = yhi
    ext[0:1] = xlo
    ext[1 + size_x : 2 + size_x] = xhi


def fetched(sems, *pairs):
    copies = [pltpu.make_async_copy(a, b, sems.at[k]) for k, (a, b) in enumerate(pairs)]
    for copy in copies:
        copy.start()
    for copy in copies:
        copy.wait()


def stack_kernel(first_ref, enc_ref, low_ref, dec_ref, lift_ref, *refs):
    outs, lift_out, (enc, low, dec, sems) = refs[:6], refs[6], refs[7:]
    fetched(sems, (enc_ref, enc), (low_ref, low), (dec_ref, dec), (lift_ref, lift_out))
    for ref, forward, backward in (
        (enc, nt_weight, nn_weight),
        (low, nn_weight, nt_weight),
        (dec, nt_weight, nn_weight),
    ):
        outs[0][...] = forward(ref)
        outs[1][...] = backward(ref)
        outs = outs[2:]


def pack_x_kernel(f_any, c_any, f_ref, c_ref, lo_ref, hi_ref, lo2_ref, hi2_ref, sems):
    fetched(sems, (f_any, f_ref), (c_any, c_ref))
    paired = [jnp.concatenate([f_ref[x, 0:4], f_ref[x, 4:8]], -1) for x in range(2)]
    for x, out, out2 in ((0, lo_ref, lo2_ref), (1, hi_ref, hi2_ref)):
        out[0:8] = jnp.concatenate([f_ref[x], c_ref[x]], -1)
        out[8:12] = paired[1 - x]
        out2[...] = paired[x]


def pack_y_kernel(f_ref, c_ref, xlo, xhi, xlo2, xhi2, lo_ref, hi_ref):
    for first, out in ((0, lo_ref), (3, hi_ref)):
        at = slice(first, first + 5)
        out[0] = xlo[at]
        for x in range(2):
            out[1 + x] = jnp.concatenate([f_ref[x, at], c_ref[x, at]], -1)
        out[3] = xhi[at]
        for k, far, near in ((4, xlo2[...], xlo[8:12]), (5, xhi[8:12], xhi2[...])):
            pair = [jnp.concatenate([v[..., :64], v[..., 64:]], 0)[at] for v in (far, near)]
            out[k] = jnp.concatenate(pair, -1)


def encode_kernel(
    f_ref, ylo, yhi, xlo, xhi, xlo2, xhi2, inside, w_ref, fx_ref, enc_ref, slope_ref, pool_ref, tmp
):
    fx_ref[3:5, 5:13] = f_ref[...]
    fx_ref[2, 5:13] = xlo[0:8, :, :64]
    fx_ref[5, 5:13] = xhi[0:8, :, :64]
    for x, ref, first in ((1, xlo, 8), (6, xhi, 8), (0, xlo2, 0), (7, xhi2, 0)):
        fx_ref[x, 5:9] = ref[first : first + 4, :, :64]
        fx_ref[x, 9:13] = ref[first : first + 4, :, 64:]
    for y, ref in ((0, ylo), (13, yhi)):
        at = slice(y, y + 5)
        fx_ref[2:6, at] = ref[0:4, :, :, :64]
        for x, k in ((0, 4), (6, 5)):
            fx_ref[x, at] = ref[k, :, :, :64]
            fx_ref[x + 1, at] = ref[k, :, :, 64:]
    weight = w_ref[...]
    for x in range(6):
        pre = combined(nt(stacked(fx_ref, x, 1, 16, False), weight), 32, False)
        sigma = jax.nn.sigmoid(pre)
        enc = (pre * sigma).astype(BF16)
        slope = sigma[128:384] * (1.0 + pre[128:384] * (1.0 - sigma[128:384]))
        slope_ref[x] = slope if x in (2, 3) else slope * inside[0 if x < 2 else 1]
        if x in (2, 3):
            enc_ref[x - 2, 1:9] = enc[128:384].reshape(8, 32, 64)
            enc_ref[x - 2, 0] = (enc[96:128].astype(F32) * inside[2]).astype(BF16)
            enc_ref[x - 2, 9] = (enc[384:416].astype(F32) * inside[3]).astype(BF16)
        wide = enc.astype(F32).reshape(8, 2, 32, 64)
        part = wide[:, 0] + wide[:, 1]
        if x % 2 == 0:
            held = part
            continue
        tmp[...] = (held + part).reshape(256, 64)
        pooled = tmp[pl.ds(0, 128, stride=2), :] + tmp[pl.ds(1, 128, stride=2), :]
        pooled = pooled * (0.125 if x == 3 else 0.125 * inside[0 if x == 1 else 1])
        pool_ref[x // 2, 2:6] = pooled[32:96].astype(BF16).reshape(4, 16, 64)
        pool_ref[x // 2, 0:2] = (pooled[0:32] * inside[2]).astype(BF16).reshape(2, 16, 64)
        pool_ref[x // 2, 6:8] = (pooled[96:128] * inside[3]).astype(BF16).reshape(2, 16, 64)


def joined_grad_kernel(c_ref, *refs):
    (ylo, yhi, xlo, xhi), (w_ref, lift_ref) = refs[:4], refs[4:6]
    cx_ref, jg_ref, kids_ref, adj_ref, tmp = refs[6:]
    cx_ref[1:3, 3:11] = c_ref[...]
    cx_ref[0, 3:11] = xlo[0:8, :, 64:]
    cx_ref[3, 3:11] = xhi[0:8, :, 64:]
    cx_ref[:, 0:3] = ylo[0:4, 2:5, :, 64:]
    cx_ref[:, 11:14] = yhi[0:4, 0:3, :, 64:]
    weight = w_ref[...]
    for x in range(2):
        grad = combined(nn(stacked(cx_ref, x, 1, 12, True), weight), 32, True)
        grad = grad.astype(BF16)
        jg_ref[pl.ds(x * 256, 256), :] = grad[64:320, :64]
        tmp[pl.ds(x * 384, 384), :] = grad.astype(F32)
    kids = []
    for p in range(2):
        for q in range(2):
            for r in range(2):
                rows = [
                    tmp[pl.ds(p * 384 + (2 * j + q) * 32 + r, 16, stride=2), :] for j in range(6)
                ]
                kids.append(jnp.concatenate(rows, 0)[:, 64:])
    kids = jnp.concatenate(kids, -1).astype(BF16)
    kids_ref[...] = kids[16:80]
    adj_ref[...] = nn(kids, lift_ref[...].reshape(512, 128))


def halver(halves):
    chunk = halves.shape[2]

    def put(row, block):
        at = pl.ds(row % chunk, block.shape[0])
        halves[row // chunk % 2, row // (2 * chunk), at, :] = block.astype(LINK)

    return put


def lower_kernel(px, inside, w_ref, adj_ref, enc_ref, la_ref, lg_ref, lo_ref, hi_ref):
    def masked(value):
        first, last = value[0:16] * inside[2], value[80:96] * inside[3]
        return jnp.concatenate([first, value[16:80], last], 0).astype(BF16)

    pre = combined(nn(stacked(px, 0, 1, 6, False), w_ref[...]), 16, False)
    sigma = jax.nn.sigmoid(pre)
    la = masked(pre * sigma)
    lg = masked(adj_ref[...] * (sigma * (1.0 + pre * (1.0 - sigma))))
    la_ref[...] = la
    lg_ref[...] = lg
    for x, msg in ((0, lo_ref), (1, hi_ref)):
        msg[0:96] = la
        msg[96:192] = lg
        enc = enc_ref[x].reshape(320, 64)
        msg[192:352] = jnp.concatenate([enc[:160], enc[160:]], -1)


def doubled(coarse, tmp):
    tmp[pl.ds(0, 64, stride=2), :] = coarse
    tmp[pl.ds(1, 64, stride=2), :] = coarse
    wide = tmp[...].reshape(4, 1, 32, 64)
    return jnp.broadcast_to(wide, (4, 2, 32, 64)).reshape(256, 64)


def grads_kernel(px, la_ref, lg_ref, core, lift_ref, kids_ref, cx_ref, enc_ref, *refs):
    (w_ref, slope_ref, jg_ref, fx_ref), refs = refs[:4], refs[4:]
    lifted_ref, keep_ref, send_ref, tmp, halves, enc_halves, wide = refs
    put, put_enc = halver(halves), halver(enc_halves)
    la, lg = la_ref[...], lg_ref[...]
    fine = nt(la, lift_ref[...].reshape(512, 128)).astype(BF16).astype(F32)
    for p in range(2):
        for q in range(2):
            for r in range(2):
                k = 4 * p + 2 * q + r
                for j in range(6):
                    y = 2 * j + q - 1
                    if 0 <= y < 10:
                        tmp[pl.ds((p * 10 + y) * 32 + r, 16, stride=2), :] = fine[
                            16 * j : 16 * j + 16, 64 * k : 64 * k + 64
                        ]
    lifted_ref[...] = tmp[...].astype(BF16).reshape(2, 10, 32, 64)
    lifted = jnp.concatenate([tmp[32:288], tmp[352:608]], 0)
    la, lg = la[16:80], lg[16:80]
    enc = enc_ref[:, 1:9].reshape(512, 64).astype(F32)
    joined = ztaps(jnp.concatenate([enc, lifted], -1), 32, False)
    dec = tn(stacked(cx_ref, 0, 2, 8, True, 2), joined)
    for ab in range(9):
        for c in range(3):
            block = dec[64 * ab : 64 * ab + 64, 128 * c : 128 * c + 128]
            put((3 * ab + c) * 64, block)
    low = tn(stacked(px, 0, 1, 4, False, 1), ztaps(lg.astype(F32), 16, True))
    for ab in range(9):
        for c in range(3):
            block = low[64 * ab : 64 * ab + 64, 128 * c : 128 * c + 128]
            put(1728 + (3 * ab + c) * 64, block)
    lift = tn(kids_ref[...], la)
    for k in range(8):
        put(3456 + 64 * k, lift[64 * k : 64 * k + 64])
    for row in (3968, 4032):
        put(row, jnp.zeros((64, 128), F32))
    lg = lg_ref[...].reshape(6, 16, 128)
    source = jnp.concatenate([lg[2 - b : 6 - b].reshape(64, 128) for b in range(3)], -1)
    grad = jnp.zeros((192, 576), F32)
    for a in range(3):
        pg = combined(nt(source, w_ref[:, 384 * a : 384 * a + 384]), 16, True)
        fine = doubled(pg * 0.125, wide)
        parts = []
        for x in (2 * a, 2 * a + 1):
            own = fine if a != 1 else fine + jg_ref[256 * x - 512 : 256 * x - 256].astype(F32)
            parts.append(own * slope_ref[x])
        eg = ztaps(jnp.concatenate(parts, 0), 32, True)
        grad = grad + tn(eg, stacked(fx_ref, 2 * a, 2, 8, False, 4))
    for ab in range(9):
        for c in range(3):
            block = grad[64 * c : 64 * c + 64, 64 * ab : 64 * ab + 64]
            block = jnp.concatenate([block[:32], block[32:]], -1)
            put_enc((3 * ab + c) * 32, block[:16])
            put_enc((3 * ab + c) * 32 + 16, block[16:])
    for row in range(864, 1024, 16):
        put_enc(row, jnp.zeros((16, 128), F32))
    mine, chunk = core[0], halves.shape[2]
    keep_ref[:, :chunk, :] = halves[mine]
    send_ref[:, :chunk, :] = halves[1 - mine]
    keep_ref[:, chunk:, :] = enc_halves[mine]
    send_ref[:, chunk:, :] = enc_halves[1 - mine]


def add_kernel(a_ref, b_ref, out_ref):
    out_ref[...] = (a_ref[...].astype(F32) + b_ref[...].astype(F32)).astype(LINK)


def edge_y_kernel(eg_ref, lo_ref, hi_ref):
    lo_ref[...] = jnp.concatenate([eg_ref[0, 0], eg_ref[1, 0]], -1)
    hi_ref[...] = jnp.concatenate([eg_ref[0, 7], eg_ref[1, 7]], -1)


def edge_x_kernel(eg_ref, ylo_ref, yhi_ref, lo_ref, hi_ref):
    for x, out in ((0, lo_ref), (1, hi_ref)):
        cols = slice(64 * x, 64 * x + 64)
        eg = eg_ref[x].reshape(256, 64)
        first = jnp.concatenate([ylo_ref[:, cols], eg[:128]], 0)
        second = jnp.concatenate([eg[128:], yhi_ref[:, cols]], 0)
        out[...] = jnp.concatenate([first, second], -1)


def column(rows):
    return jnp.stack([rows[:, :64], rows[:, 64:]], 0).reshape(2, 1, 32, 64)


def plane(rows):
    return jnp.concatenate([rows[:, :64], rows[:, 64:]], 0).reshape(1, 10, 32, 64)


def encoder_grad_kernel(
    lg_ref, xlo, xhi, w_ref, slope_ref, jg_ref, eg_ref, lo_ref, hi_ref, lx, tmp
):
    lx[0] = xlo[96:192].reshape(6, 16, 128)
    lx[1] = lg_ref[...].reshape(6, 16, 128)
    lx[2] = xhi[96:192].reshape(6, 16, 128)
    pg = combined(nt(stacked(lx, 0, 1, 4, True), w_ref[...]), 16, True)
    fine = doubled(pg.astype(BF16).astype(F32) * 0.125, tmp)
    for x in range(2):
        total = jg_ref[256 * x : 256 * x + 256].astype(F32) + fine
        eg_ref[x] = (total * slope_ref[2 + x]).astype(BF16).reshape(8, 32, 64)
    edge_y_kernel(eg_ref, lo_ref, hi_ref)


def decode_kernel(enc_ref, lifted_ref, xlo, xhi, lift_ref, w_ref, out_ref, jx, tx):
    jx[1:3] = jnp.concatenate([enc_ref[...], lifted_ref[...]], -1)
    for p, h in ((1, xlo), (0, xhi)):
        for q in range(2):
            for r in range(2):
                fine = nt(h[0:96], lift_ref[4 * p + 2 * q + r]).astype(BF16).astype(F32)
                for j in range(6):
                    y = 2 * j + q - 1
                    if 0 <= y < 10:
                        tx[pl.ds(32 * y + r, 16, stride=2), :] = fine[16 * j : 16 * j + 16]
        lifted = tx[...].astype(BF16).reshape(1, 10, 32, 64)
        x = 0 if p == 1 else 3
        jx[x : x + 1] = jnp.concatenate([plane(h[192:352]), lifted], -1)
    weight = w_ref[...]
    for x in range(2):
        out = combined(nt(stacked(jx, x, 1, 8, False), weight), 32, False)
        out_ref[x] = out.astype(BF16).reshape(8, 32, 64)


def input_grad_kernel(eg_ref, ylo, yhi, xlo, xhi, w_ref, out_ref, ex):
    sides = [column(ylo[...]), column(yhi[...]), plane(xlo[...]), plane(xhi[...])]
    assemble(ex, eg_ref[...], *sides)
    weight = w_ref[...]
    for x in range(2):
        out = combined(nn(stacked(ex, x, 1, 8, True), weight), 32, True)
        out_ref[x] = out.astype(BF16).reshape(8, 32, 64)


def sum_kernel(parts_ref, out_ref):
    total = parts_ref[0].astype(F32)
    for k in range(1, parts_ref.shape[0]):
        total = total + parts_ref[k].astype(F32)
    total = total.astype(LINK)
    for k in range(out_ref.shape[0]):
        out_ref[k] = total


def widen_kernel(core, own_ref, other_ref, encoder_ref, decoder_ref, lower_ref, lift_ref):
    own, other = own_ref[...].astype(F32), other_ref[...].astype(F32)
    first = core[0] == 0
    both = jnp.stack([jnp.where(first, own, other), jnp.where(first, other, own)], 1)
    chunk = own.shape[1] // 5 * 4
    sums = both[:, :, :chunk].reshape(4096, 128)
    decoder_ref[...] = sums[0:1728].reshape(27, 64, 128)
    lower_ref[...] = sums[1728:3456].reshape(27, 64, 128)
    lift_ref[...] = sums[3456:3968].reshape(8, 64, 128)
    wide = both[:, :, chunk:].reshape(1024, 128)[:864].reshape(27, 32, 128)
    encoder_ref[:, 0:32, :] = wide[..., :64]
    encoder_ref[:, 32:64, :] = wide[..., 64:]


def per_device(features, encoder_weight, lower_weight, lift_weight, decoder_weight, cotangent):
    f = jnp.transpose(features, (1, 2, 3, 0))
    c = jnp.transpose(cotangent, (1, 2, 3, 0))
    lower_t = jnp.transpose(lower_weight, (0, 2, 1))
    brick, tall = (2, 8, 32, 64), (2, 10, 32, 64)

    size_x, size_z = lax.axis_size("gx"), lax.axis_size("gz")
    at_x, at_y = lax.axis_index("gx"), lax.axis_index(GY)
    inside = jnp.stack([at_x > 0, at_x < size_x - 1, at_y > 0, at_y < 2 * size_z - 1]).astype(F32)
    core = lax.axis_index("gc").reshape(1)

    f, c, lo, hi, lo2, hi2 = call(
        pack_x_kernel,
        [(brick, BF16)] * 2 + [((12, 32, 128), BF16)] * 2 + [((4, 32, 128), BF16)] * 2,
        [(pltpu.SemaphoreType.DMA((2,)), None)],
        [f, c],
        spaces={0: pltpu.HBM, 1: pltpu.HBM},
    )
    x_halo = swapped(lo, hi, GX)
    far_halo = [shifted(hi2, GX, 2), shifted(lo2, GX, -2)]
    edges = call(
        pack_y_kernel,
        [((6, 5, 32, 128), BF16)] * 2,
        [],
        [f, c, *x_halo, *far_halo],
    )
    y_halo = swapped(*edges, GY)
    enc_fwd, enc_bwd, low_fwd, low_bwd, dec_fwd, dec_bwd, lift = call(
        stack_kernel,
        [
            ((192, 576), BF16),
            ((576, 192), BF16),
            ((576, 384), BF16),
            ((192, 1152), BF16),
            ((192, 1152), BF16),
            ((576, 384), BF16),
            ((8, 64, 128), BF16),
        ],
        [
            ((27, 64, 64), BF16),
            ((27, 64, 128), BF16),
            ((27, 64, 128), BF16),
            (pltpu.SemaphoreType.DMA((4,)), None),
        ],
        [edges[0], encoder_weight, lower_t, decoder_weight, lift_weight],
        spaces={k: pltpu.HBM for k in range(5)},
        flops=2 * 10**9,
    )
    fx, encoded, slope, pooled = call(
        encode_kernel,
        [((8, 18, 32, 64), BF16), (tall, BF16), ((6, 256, 64), F32), ((3, 8, 16, 64), BF16)],
        [((256, 64), F32)],
        [f, *y_halo, *x_halo, *far_halo, inside, enc_fwd],
        spaces={7: pltpu.SMEM},
    )
    cx, jg, kids, adj = call(
        joined_grad_kernel,
        [
            ((4, 14, 32, 64), BF16),
            ((512, 64), BF16),
            ((64, 512), BF16),
            ((96, 128), F32),
        ],
        [((768, 128), F32)],
        [c, *y_halo, *x_halo, dec_bwd, lift],
    )
    half = (size_x, 2560 // size_x, 128)
    la, lg, *edges = call(
        lower_kernel,
        [((96, 128), BF16)] * 2 + [((352, 128), BF16)] * 2,
        [],
        [pooled, inside, low_fwd, adj, encoded],
        spaces={1: pltpu.SMEM},
    )
    lifted, keep, send = call(
        grads_kernel,
        [(tall, BF16), (half, LINK), (half, LINK)],
        [
            ((640, 64), F32),
            ((2, size_x, 2048 // size_x, 128), LINK),
            ((2, size_x, 512 // size_x, 128), LINK),
            ((128, 64), F32),
        ],
        [pooled, la, lg, core, lift, kids, cx, encoded, low_bwd, slope, jg, fx],
        spaces={3: pltpu.SMEM},
    )
    (sums,) = call(add_kernel, [(half, LINK)], [], [keep, partner(send)])
    sums, edges = lax.optimization_barrier((sums, edges))
    sums = lax.all_to_all(sums, "gx", 0, 0)
    halo = swapped(*edges, GX)
    (sums,) = call(sum_kernel, [((size_z,) + half[1:], LINK)], [], [sums])
    sums, halo = lax.optimization_barrier((sums, halo))
    sums = lax.all_to_all(sums, "gz", 0, 0)
    eg, *edges = call(
        encoder_grad_kernel,
        [(brick, BF16)] + [((32, 128), BF16)] * 2,
        [((3, 6, 16, 128), BF16), ((128, 64), F32)],
        [lg, *halo, low_bwd, slope, jg],
    )
    y_halo = swapped(*edges, GY)
    (sums,) = call(sum_kernel, [(half, LINK)], [], [sums])
    sums, y_halo = lax.optimization_barrier((sums, y_halo))
    sums = lax.all_to_all(sums, "gx", 0, 0)
    edges = call(edge_x_kernel, [((160, 128), BF16)] * 2, [], [eg, *y_halo])
    x_halo = swapped(*edges, GX)
    (decoded,) = call(
        decode_kernel,
        [(brick, BF16)],
        [((4, 10, 32, 128), BF16), ((320, 64), F32)],
        [encoded, lifted, *halo, lift, dec_fwd],
    )
    sums, x_halo, decoded = lax.optimization_barrier((sums, x_halo, decoded))
    (input_grad,) = call(
        input_grad_kernel,
        [(brick, BF16)],
        [((4, 10, 32, 64), BF16)],
        [eg, *y_halo, *x_halo, enc_bwd],
        flops=2 * 10**9,
    )
    encoder_gradient, decoder_gradient, lower_gradient, lift_gradient = call(
        widen_kernel,
        [((27, 64, 64), F32), ((27, 64, 128), F32), ((27, 64, 128), F32), ((8, 64, 128), F32)],
        [],
        [core, sums, partner(sums)],
        spaces={0: pltpu.SMEM},
    )
    return (
        jnp.transpose(decoded, (3, 0, 1, 2)),
        jnp.transpose(input_grad, (3, 0, 1, 2)),
        encoder_gradient,
        jnp.transpose(lower_gradient, (0, 2, 1)),
        lift_gradient,
        decoder_gradient,
    )


def solution(mesh):
    size_x, size_y = mesh.devices.shape
    chips = Mesh(mesh.devices.reshape(size_x, size_y // 2, 2), ("gx", "gz", "gc"))
    field = P(None, "gx", ("gz", "gc"), None)
    return jax.shard_map(
        per_device,
        mesh=chips,
        in_specs=(field, P(), P(), P(), P(), field),
        out_specs=(field, field, P(), P(), P(), P()),
        check_vma=False,
    )
```

```python
import math

import jax
import jax.numpy as jnp
from jax import lax
from jax.experimental import pallas as pl
from jax.experimental.pallas import tpu as pltpu
from jax.sharding import Mesh, PartitionSpec as P

F32, BF16 = jnp.float32, jnp.bfloat16
LINK = BF16
GX, GY = ("gx",), ("gz", "gc")
TAPS9 = tuple((a, b) for a in range(3) for b in range(3))


def shifted(piece, axes, step):
    size = math.prod(lax.axis_size(axis) for axis in axes)
    pairs = [(i, i + step) for i in range(size) if 0 <= i + step < size]
    return lax.ppermute(piece, axes, pairs)


def swapped(low, high, axes):
    return shifted(high, axes, 1), shifted(low, axes, -1)


def partner(piece):
    return lax.ppermute(piece, "gc", [(0, 1), (1, 0)])


def call(kernel, outs, scratch, operands, spaces=(), flops=10**6):
    return pl.pallas_call(
        kernel,
        out_shape=[jax.ShapeDtypeStruct(s, d) for s, d in outs],
        in_specs=[
            pl.BlockSpec(memory_space=dict(spaces).get(i, pltpu.VMEM)) for i in range(len(operands))
        ],
        out_specs=[pl.BlockSpec(memory_space=pltpu.VMEM)] * len(outs),
        scratch_shapes=[s if d is None else pltpu.VMEM(s, d) for s, d in scratch],
        compiler_params=pltpu.CompilerParams(vmem_limit_bytes=40 * 2**20),
        cost_estimate=pl.CostEstimate(flops=flops, bytes_accessed=10**4, transcendentals=0),
    )(*operands)


def nn(a, b):
    return lax.dot_general(a, b, (((1,), (0,)), ((), ())), preferred_element_type=F32)


def nt(a, b):
    return lax.dot_general(a, b, (((1,), (1,)), ((), ())), preferred_element_type=F32)


def tn(a, b):
    return lax.dot_general(a, b, (((0,), (0,)), ((), ())), preferred_element_type=F32)


def nn_weight(ref):
    rows = [jnp.concatenate([ref[3 * ab + c] for c in range(3)], -1) for ab in range(9)]
    return jnp.concatenate(rows, 0)


def nt_weight(ref):
    rows = [jnp.concatenate([ref[3 * ab + c] for ab in range(9)], -1) for c in range(3)]
    return jnp.concatenate(rows, 0)


def stacked(ref, x, nx, ny, adjoint, y=0):
    pieces = []
    for a, b in TAPS9:
        i, j = (x + 2 - a, y + 2 - b) if adjoint else (x + a, y + b)
        piece = ref[i : i + nx, j : j + ny]
        pieces.append(piece.reshape(nx * ny * piece.shape[2], piece.shape[3]))
    return jnp.concatenate(pieces, -1)


def zshift(value, step, depth):
    rows = value.shape[0]
    z = lax.broadcasted_iota(jnp.int32, value.shape, 0) & (depth - 1)
    moved = pltpu.roll(value, step % rows, 0)
    return jnp.where(z == (0 if step > 0 else depth - 1), 0.0, moved)


def combined(parts, depth, adjoint):
    ch = parts.shape[1] // 3
    step = -1 if adjoint else 1
    return (
        zshift(parts[:, :ch], step, depth)
        + parts[:, ch : 2 * ch]
        + zshift(parts[:, 2 * ch :], -step, depth)
    )


def ztaps(value, depth, adjoint):
    step = -1 if adjoint else 1
    return jnp.concatenate(
        [
            zshift(value, step, depth).astype(BF16),
            value.astype(BF16),
            zshift(value, -step, depth).astype(BF16),
        ],
        -1,
    )


def stack_kernel(first_ref, enc_ref, low_ref, dec_ref, lift_ref, *outs):
    for ref, forward, backward in (
        (enc_ref, nt_weight, nn_weight),
        (low_ref, nn_weight, nt_weight),
        (dec_ref, nt_weight, nn_weight),
    ):
        outs[0][...] = forward(ref)
        outs[1][...] = backward(ref)
        outs = outs[2:]
    outs[0][...] = lift_ref[...]


def pack_x_kernel(f_in, c_in, f_ref, c_ref, lo_ref, hi_ref, lo2_ref, hi2_ref):
    f_ref[...] = f_in[...]
    c_ref[...] = c_in[...]
    paired = [jnp.concatenate([f_in[x, 0:4], f_in[x, 4:8]], -1) for x in range(2)]
    for x, out, out2 in ((0, lo_ref, lo2_ref), (1, hi_ref, hi2_ref)):
        out[0:8] = jnp.concatenate([f_in[x], c_in[x]], -1)
        out[8:12] = paired[1 - x]
        out2[...] = paired[x]


def pack_y_kernel(f_ref, c_ref, xlo, xhi, xlo2, xhi2, lo_ref, hi_ref):
    for first, out in ((0, lo_ref), (1, hi_ref)):
        at = slice(first, first + 7)
        out[0] = xlo[at]
        for x in range(2):
            out[1 + x] = jnp.concatenate([f_ref[x, at], c_ref[x, at]], -1)
        out[3] = xhi[at]
        for k, far, near in ((4, xlo2[...], xlo[8:12]), (5, xhi[8:12], xhi2[...])):
            pair = [jnp.concatenate([v[..., :64], v[..., 64:]], 0)[at] for v in (far, near)]
            out[k] = jnp.concatenate(pair, -1)


def encode_kernel(
    f_ref, ylo, yhi, xlo, xhi, xlo2, xhi2, inside, w_ref, fx_ref, enc_ref, slope_ref, pool_ref, tmp
):
    fx_ref[3:5, 7:15] = f_ref[...]
    fx_ref[2, 7:15] = xlo[0:8, :, :64]
    fx_ref[5, 7:15] = xhi[0:8, :, :64]
    for x, ref, first in ((1, xlo, 8), (6, xhi, 8), (0, xlo2, 0), (7, xhi2, 0)):
        fx_ref[x, 7:11] = ref[first : first + 4, :, :64]
        fx_ref[x, 11:15] = ref[first : first + 4, :, 64:]
    for y, ref in ((0, ylo), (15, yhi)):
        at = slice(y, y + 7)
        fx_ref[2:6, at] = ref[0:4, :, :, :64]
        for x, k in ((0, 4), (6, 5)):
            fx_ref[x, at] = ref[k, :, :, :64]
            fx_ref[x + 1, at] = ref[k, :, :, 64:]
    weight = w_ref[...]

    def edged(value, x):
        if x < 2 or x > 3:
            value = value * inside[0 if x < 2 else 1]
        return jnp.concatenate(
            [value[0:32] * inside[2], value[32:288], value[288:320] * inside[3]], 0
        )

    for x in range(6):
        pre = combined(nt(stacked(fx_ref, x, 1, 20, False), weight), 32, False)
        sigma = jax.nn.sigmoid(pre)
        enc = (pre * sigma).astype(BF16).astype(F32)
        near, slope = pre[160:480], sigma[160:480]
        slope_ref[x] = edged(slope * (1.0 + near * (1.0 - slope)), x)
        if 0 < x < 5:
            enc_ref[x - 1] = edged(enc[160:480], x).astype(BF16).reshape(10, 32, 64)
        wide = enc.reshape(10, 2, 32, 64)
        part = wide[:, 0] + wide[:, 1]
        if x % 2 == 0:
            held = part
            continue
        tmp[...] = (held + part).reshape(320, 64)
        pooled = tmp[pl.ds(0, 160, stride=2), :] + tmp[pl.ds(1, 160, stride=2), :]
        pooled = pooled * (0.125 if x == 3 else 0.125 * inside[0 if x == 1 else 1])
        pool_ref[x // 2, 3:7] = pooled[48:112].astype(BF16).reshape(4, 16, 64)
        pool_ref[x // 2, 0:3] = (pooled[0:48] * inside[2]).astype(BF16).reshape(3, 16, 64)
        pool_ref[x // 2, 7:10] = (pooled[112:160] * inside[3]).astype(BF16).reshape(3, 16, 64)


def joined_grad_kernel(c_ref, *refs):
    (ylo, yhi, xlo, xhi), (w_ref, lift_ref) = refs[:4], refs[4:6]
    cx_ref, jg_ref, kids_ref, adj_ref, tmp = refs[6:]
    cx_ref[1:3, 5:13] = c_ref[...]
    cx_ref[0, 5:13] = xlo[0:8, :, 64:]
    cx_ref[3, 5:13] = xhi[0:8, :, 64:]
    cx_ref[:, 0:5] = ylo[0:4, 2:7, :, 64:]
    cx_ref[:, 13:18] = yhi[0:4, 0:5, :, 64:]
    weight = w_ref[...]
    for x in range(2):
        grad = combined(nn(stacked(cx_ref, x, 1, 16, True), weight), 32, True)
        grad = grad.astype(BF16)
        jg_ref[x] = grad[96:416, :64]
        tmp[pl.ds(x * 512, 512), :] = grad.astype(F32)
    kids = []
    for p in range(2):
        for q in range(2):
            for r in range(2):
                rows = [
                    tmp[pl.ds(p * 512 + (2 * j + q) * 32 + r, 16, stride=2), :] for j in range(8)
                ]
                kids.append(jnp.concatenate(rows, 0)[:, 64:])
    kids = jnp.concatenate(kids, -1).astype(BF16)
    kids_ref[...] = kids[32:96]
    adj_ref[...] = nn(kids, lift_ref[...].reshape(512, 128))


def halver(halves):
    chunk = halves.shape[2]

    def put(row, block):
        at = pl.ds(row % chunk, block.shape[0])
        halves[row // chunk % 2, row // (2 * chunk), at, :] = block.astype(LINK)

    return put


def lower_kernel(px, inside, w_ref, adj_ref, la_ref, lg_ref, msg_ref):
    def masked(value):
        first, last = value[0:32] * inside[2], value[96:128] * inside[3]
        return jnp.concatenate([first, value[32:96], last], 0).astype(BF16)

    pre = combined(nn(stacked(px, 0, 1, 8, False), w_ref[...]), 16, False)
    sigma = jax.nn.sigmoid(pre)
    la = masked(pre * sigma)
    lg = masked(adj_ref[...] * (sigma * (1.0 + pre * (1.0 - sigma))))
    la_ref[...] = la[16:112]
    lg_ref[...] = lg
    msg_ref[0:96] = la[16:112]
    msg_ref[96:224] = lg


def doubled(coarse, tmp):
    rows = coarse.shape[0]
    tmp[pl.ds(0, rows, stride=2), :] = coarse
    tmp[pl.ds(1, rows, stride=2), :] = coarse
    wide = tmp[...].reshape(rows // 16, 1, 32, 64)
    return jnp.broadcast_to(wide, (rows // 16, 2, 32, 64)).reshape(4 * rows, 64)


def grads_kernel(px, la_ref, lg_ref, core, lift_ref, kids_ref, cx_ref, enc_ref, *refs):
    (w_ref, slope_ref, jg_ref, fx_ref), refs = refs[:4], refs[4:]
    lifted_ref, keep_ref, send_ref, tmp, halves, enc_halves, wide = refs
    put, put_enc = halver(halves), halver(enc_halves)
    la, lg = la_ref[...], lg_ref[...]
    fine = nt(la, lift_ref[...].reshape(512, 128)).astype(BF16).astype(F32)
    for p in range(2):
        for q in range(2):
            for r in range(2):
                k = 4 * p + 2 * q + r
                for j in range(6):
                    y = 2 * j + q - 1
                    if 0 <= y < 10:
                        tmp[pl.ds((p * 10 + y) * 32 + r, 16, stride=2), :] = fine[
                            16 * j : 16 * j + 16, 64 * k : 64 * k + 64
                        ]
    lifted_ref[...] = tmp[...].astype(BF16).reshape(2, 10, 32, 64)
    lifted = jnp.concatenate([tmp[32:288], tmp[352:608]], 0)
    la, lg = la[16:80], lg[32:96]
    enc = enc_ref[1:3, 1:9].reshape(512, 64).astype(F32)
    joined = ztaps(jnp.concatenate([enc, lifted], -1), 32, False)
    dec = tn(stacked(cx_ref, 0, 2, 8, True, 4), joined)
    for ab in range(9):
        for c in range(3):
            block = dec[64 * ab : 64 * ab + 64, 128 * c : 128 * c + 128]
            put((3 * ab + c) * 64, block)
    low = tn(stacked(px, 0, 1, 4, False, 2), ztaps(lg.astype(F32), 16, True))
    for ab in range(9):
        for c in range(3):
            block = low[64 * ab : 64 * ab + 64, 128 * c : 128 * c + 128]
            put(1728 + (3 * ab + c) * 64, block)
    lift = tn(kids_ref[...], la)
    for k in range(8):
        put(3456 + 64 * k, lift[64 * k : 64 * k + 64])
    for row in (3968, 4032):
        put(row, jnp.zeros((64, 128), F32))
    lg = lg_ref[...].reshape(8, 16, 128)
    source = jnp.concatenate([lg[3 - b : 7 - b].reshape(64, 128) for b in range(3)], -1)
    grad = jnp.zeros((192, 576), F32)
    for a in range(3):
        pg = combined(nt(source, w_ref[:, 384 * a : 384 * a + 384]), 16, True)
        fine = doubled(pg * 0.125, wide)
        parts = []
        for x in (2 * a, 2 * a + 1):
            own = fine if a != 1 else fine + jg_ref[x - 2, 32:288].astype(F32)
            parts.append(own * slope_ref[x, 32:288])
        eg = ztaps(jnp.concatenate(parts, 0), 32, True)
        grad = grad + tn(eg, stacked(fx_ref, 2 * a, 2, 8, False, 6))
    for ab in range(9):
        for c in range(3):
            block = grad[64 * c : 64 * c + 64, 64 * ab : 64 * ab + 64]
            block = jnp.concatenate([block[:32], block[32:]], -1)
            put_enc((3 * ab + c) * 32, block[:16])
            put_enc((3 * ab + c) * 32 + 16, block[16:])
    for row in range(864, 1024, 16):
        put_enc(row, jnp.zeros((16, 128), F32))
    mine, chunk = core[0], halves.shape[2]
    keep_ref[:, :chunk, :] = halves[mine]
    send_ref[:, :chunk, :] = halves[1 - mine]
    keep_ref[:, chunk:, :] = enc_halves[mine]
    send_ref[:, chunk:, :] = enc_halves[1 - mine]


def add_kernel(a_ref, b_ref, out_ref):
    out_ref[...] = (a_ref[...].astype(F32) + b_ref[...].astype(F32)).astype(LINK)


def plane(rows):
    return jnp.concatenate([rows[:, :64], rows[:, 64:]], 0).reshape(1, 10, 32, 64)


def encoder_grad_kernel(
    lg_ref, xlo, xhi, w_ref, slope_ref, jg_ref, eg_ref, lo_ref, hi_ref, lx, tmp
):
    lx[0] = xlo[96:224].reshape(8, 16, 128)
    lx[1] = lg_ref[...].reshape(8, 16, 128)
    lx[2] = xhi[96:224].reshape(8, 16, 128)
    pg = combined(nt(stacked(lx, 0, 1, 6, True), w_ref[...]), 16, True)
    fine = doubled(pg.astype(BF16).astype(F32) * 0.125, tmp)[32:352]
    for x, msg in ((0, lo_ref), (1, hi_ref)):
        eg = ((jg_ref[x].astype(F32) + fine) * slope_ref[2 + x]).astype(BF16)
        eg_ref[x] = eg.reshape(10, 32, 64)
        msg[...] = jnp.concatenate([eg[:160], eg[160:]], -1)


def decode_kernel(enc_ref, lifted_ref, xlo, xhi, lift_ref, w_ref, out_ref, jx, tx):
    jx[1:3] = jnp.concatenate([enc_ref[1:3], lifted_ref[...]], -1)
    for p, h in ((1, xlo), (0, xhi)):
        for q in range(2):
            for r in range(2):
                fine = nt(h[0:96], lift_ref[4 * p + 2 * q + r]).astype(BF16).astype(F32)
                for j in range(6):
                    y = 2 * j + q - 1
                    if 0 <= y < 10:
                        tx[pl.ds(32 * y + r, 16, stride=2), :] = fine[16 * j : 16 * j + 16]
        lifted = tx[...].astype(BF16).reshape(1, 10, 32, 64)
        x = 0 if p == 1 else 3
        jx[x : x + 1] = jnp.concatenate([enc_ref[x : x + 1], lifted], -1)
    weight = w_ref[...]
    for x in range(2):
        out = combined(nt(stacked(jx, x, 1, 8, False), weight), 32, False)
        out_ref[x] = out.astype(BF16).reshape(8, 32, 64)


def input_grad_kernel(eg_ref, xlo, xhi, w_ref, out_ref, ex):
    ex[0:1] = plane(xlo[...])
    ex[1:3] = eg_ref[...]
    ex[3:4] = plane(xhi[...])
    weight = w_ref[...]
    for x in range(2):
        out = combined(nn(stacked(ex, x, 1, 8, True), weight), 32, True)
        out_ref[x] = out.astype(BF16).reshape(8, 32, 64)


def sum_kernel(parts_ref, out_ref):
    total = parts_ref[0].astype(F32)
    for k in range(1, parts_ref.shape[0]):
        total = total + parts_ref[k].astype(F32)
    total = total.astype(LINK)
    for k in range(out_ref.shape[0]):
        out_ref[k] = total


def widen_kernel(core, own_ref, other_ref, encoder_ref, decoder_ref, lower_ref, lift_ref):
    own, other = own_ref[...].astype(F32), other_ref[...].astype(F32)
    first = core[0] == 0
    both = jnp.stack([jnp.where(first, own, other), jnp.where(first, other, own)], 1)
    chunk = own.shape[1] // 5 * 4
    sums = both[:, :, :chunk].reshape(4096, 128)
    decoder_ref[...] = sums[0:1728].reshape(27, 64, 128)
    lower_ref[...] = sums[1728:3456].reshape(27, 64, 128)
    lift_ref[...] = sums[3456:3968].reshape(8, 64, 128)
    wide = both[:, :, chunk:].reshape(1024, 128)[:864].reshape(27, 32, 128)
    encoder_ref[:, 0:32, :] = wide[..., :64]
    encoder_ref[:, 32:64, :] = wide[..., 64:]


def per_device(features, encoder_weight, lower_weight, lift_weight, decoder_weight, cotangent):
    f = jnp.transpose(features, (1, 2, 3, 0))
    c = jnp.transpose(cotangent, (1, 2, 3, 0))
    lower_t = jnp.transpose(lower_weight, (0, 2, 1))
    brick, tall = (2, 8, 32, 64), (2, 10, 32, 64)

    size_x, size_z = lax.axis_size("gx"), lax.axis_size("gz")
    at_x, at_y = lax.axis_index("gx"), lax.axis_index(GY)
    inside = jnp.stack([at_x > 0, at_x < size_x - 1, at_y > 0, at_y < 2 * size_z - 1]).astype(F32)
    core = lax.axis_index("gc").reshape(1)

    f, c, lo, hi, lo2, hi2 = call(
        pack_x_kernel,
        [(brick, BF16)] * 2 + [((12, 32, 128), BF16)] * 2 + [((4, 32, 128), BF16)] * 2,
        [],
        [f, c],
    )
    x_halo = swapped(lo, hi, GX)
    far_halo = [shifted(hi2, GX, 2), shifted(lo2, GX, -2)]
    edges = call(
        pack_y_kernel,
        [((6, 7, 32, 128), BF16)] * 2,
        [],
        [f, c, *x_halo, *far_halo],
    )
    y_halo = swapped(*edges, GY)
    enc_fwd, enc_bwd, low_fwd, low_bwd, dec_fwd, dec_bwd, lift = call(
        stack_kernel,
        [
            ((192, 576), BF16),
            ((576, 192), BF16),
            ((576, 384), BF16),
            ((192, 1152), BF16),
            ((192, 1152), BF16),
            ((576, 384), BF16),
            ((8, 64, 128), BF16),
        ],
        [],
        [edges[0], encoder_weight, lower_t, decoder_weight, lift_weight],
        spaces={0: pltpu.HBM},
        flops=2 * 10**9,
    )
    fx, encoded, slope, pooled = call(
        encode_kernel,
        [((8, 22, 32, 64), BF16), ((4, 10, 32, 64), BF16)]
        + [((6, 320, 64), F32), ((3, 10, 16, 64), BF16)],
        [((320, 64), F32)],
        [f, *y_halo, *x_halo, *far_halo, inside, enc_fwd],
        spaces={7: pltpu.SMEM},
    )
    cx, jg, kids, adj = call(
        joined_grad_kernel,
        [
            ((4, 18, 32, 64), BF16),
            ((2, 320, 64), BF16),
            ((64, 512), BF16),
            ((128, 128), F32),
        ],
        [((1024, 128), F32)],
        [c, *y_halo, *x_halo, dec_bwd, lift],
    )
    half = (size_x, 2560 // size_x, 128)
    la, lg, edge = call(
        lower_kernel,
        [((96, 128), BF16), ((128, 128), BF16), ((224, 128), BF16)],
        [],
        [pooled, inside, low_fwd, adj],
        spaces={1: pltpu.SMEM},
    )
    lifted, keep, send = call(
        grads_kernel,
        [(tall, BF16), (half, LINK), (half, LINK)],
        [
            ((640, 64), F32),
            ((2, size_x, 2048 // size_x, 128), LINK),
            ((2, size_x, 512 // size_x, 128), LINK),
            ((128, 64), F32),
        ],
        [pooled, la, lg, core, lift, kids, cx, encoded, low_bwd, slope, jg, fx],
        spaces={3: pltpu.SMEM},
    )
    (sums,) = call(add_kernel, [(half, LINK)], [], [keep, partner(send)])
    sums, edge = lax.optimization_barrier((sums, edge))
    sums = lax.all_to_all(sums, "gx", 0, 0)
    halo = swapped(edge, edge, GX)
    (sums,) = call(sum_kernel, [((size_z,) + half[1:], LINK)], [], [sums])
    sums, halo = lax.optimization_barrier((sums, halo))
    sums = lax.all_to_all(sums, "gz", 0, 0)
    eg, *edges = call(
        encoder_grad_kernel,
        [(tall, BF16)] + [((160, 128), BF16)] * 2,
        [((3, 8, 16, 128), BF16), ((192, 64), F32)],
        [lg, *halo, low_bwd, slope, jg],
    )
    eg_halo = swapped(*edges, GX)
    (sums,) = call(sum_kernel, [(half, LINK)], [], [sums])
    sums, eg_halo = lax.optimization_barrier((sums, eg_halo))
    sums = lax.all_to_all(sums, "gx", 0, 0)
    (decoded,) = call(
        decode_kernel,
        [(brick, BF16)],
        [((4, 10, 32, 128), BF16), ((320, 64), F32)],
        [encoded, lifted, *halo, lift, dec_fwd],
    )
    (input_grad,) = call(
        input_grad_kernel,
        [(brick, BF16)],
        [((4, 10, 32, 64), BF16)],
        [eg, *eg_halo, enc_bwd],
    )
    sums, decoded, input_grad = lax.optimization_barrier((sums, decoded, input_grad))
    encoder_gradient, decoder_gradient, lower_gradient, lift_gradient = call(
        widen_kernel,
        [((27, 64, 64), F32), ((27, 64, 128), F32), ((27, 64, 128), F32), ((8, 64, 128), F32)],
        [],
        [core, sums, partner(sums)],
        spaces={0: pltpu.SMEM},
    )
    return (
        jnp.transpose(decoded, (3, 0, 1, 2)),
        jnp.transpose(input_grad, (3, 0, 1, 2)),
        encoder_gradient,
        jnp.transpose(lower_gradient, (0, 2, 1)),
        lift_gradient,
        decoder_gradient,
    )


def solution(mesh):
    size_x, size_y = mesh.devices.shape
    chips = Mesh(mesh.devices.reshape(size_x, size_y // 2, 2), ("gx", "gz", "gc"))
    field = P(None, "gx", ("gz", "gc"), None)
    return jax.shard_map(
        per_device,
        mesh=chips,
        in_specs=(field, P(), P(), P(), P(), field),
        out_specs=(field, field, P(), P(), P(), P()),
        check_vma=False,
    )
```

```python
import math

import jax
import jax.numpy as jnp
from jax import lax
from jax.experimental import pallas as pl
from jax.experimental.pallas import tpu as pltpu
from jax.sharding import Mesh, PartitionSpec as P

F32, BF16 = jnp.float32, jnp.bfloat16
LINK = BF16
GX, GY = ("gx",), ("gz", "gc")
TAPS9 = tuple((a, b) for a in range(3) for b in range(3))


def shifted(piece, axes, step):
    size = math.prod(lax.axis_size(axis) for axis in axes)
    pairs = [(i, i + step) for i in range(size) if 0 <= i + step < size]
    return lax.ppermute(piece, axes, pairs)


def swapped(low, high, axes):
    return shifted(high, axes, 1), shifted(low, axes, -1)


def partner(piece):
    return lax.ppermute(piece, "gc", [(0, 1), (1, 0)])


def call(kernel, outs, scratch, operands, spaces=(), flops=10**6, out_space=pltpu.VMEM):
    return pl.pallas_call(
        kernel,
        out_shape=[jax.ShapeDtypeStruct(s, d) for s, d in outs],
        in_specs=[
            pl.BlockSpec(memory_space=dict(spaces).get(i, pltpu.VMEM)) for i in range(len(operands))
        ],
        out_specs=[pl.BlockSpec(memory_space=out_space)] * len(outs),
        scratch_shapes=[s if d is None else pltpu.VMEM(s, d) for s, d in scratch],
        compiler_params=pltpu.CompilerParams(vmem_limit_bytes=40 * 2**20),
        cost_estimate=pl.CostEstimate(flops=flops, bytes_accessed=10**4, transcendentals=0),
    )(*operands)


def nn(a, b):
    return lax.dot_general(a, b, (((1,), (0,)), ((), ())), preferred_element_type=F32)


def nt(a, b):
    return lax.dot_general(a, b, (((1,), (1,)), ((), ())), preferred_element_type=F32)


def tn(a, b):
    return lax.dot_general(a, b, (((0,), (0,)), ((), ())), preferred_element_type=F32)


def nn_weight(ref):
    rows = [jnp.concatenate([ref[3 * ab + c] for c in range(3)], -1) for ab in range(9)]
    return jnp.concatenate(rows, 0)


def nt_weight(ref):
    rows = [jnp.concatenate([ref[3 * ab + c] for ab in range(9)], -1) for c in range(3)]
    return jnp.concatenate(rows, 0)


def stacked(ref, x, nx, ny, adjoint, y=0):
    pieces = []
    for a, b in TAPS9:
        i, j = (x + 2 - a, y + 2 - b) if adjoint else (x + a, y + b)
        piece = ref[i : i + nx, j : j + ny]
        pieces.append(piece.reshape(nx * ny * piece.shape[2], piece.shape[3]))
    return jnp.concatenate(pieces, -1)


def zshift(value, step, depth):
    rows = value.shape[0]
    z = lax.broadcasted_iota(jnp.int32, value.shape, 0) & (depth - 1)
    moved = pltpu.roll(value, step % rows, 0)
    return jnp.where(z == (0 if step > 0 else depth - 1), 0.0, moved)


def combined(parts, depth, adjoint):
    ch = parts.shape[1] // 3
    step = -1 if adjoint else 1
    return (
        zshift(parts[:, :ch], step, depth)
        + parts[:, ch : 2 * ch]
        + zshift(parts[:, 2 * ch :], -step, depth)
    )


def ztaps(value, depth, adjoint):
    step = -1 if adjoint else 1
    return jnp.concatenate(
        [
            zshift(value, step, depth).astype(BF16),
            value.astype(BF16),
            zshift(value, -step, depth).astype(BF16),
        ],
        -1,
    )


def stack_kernel(first_ref, enc_ref, low_ref, dec_ref, lift_ref, *outs):
    for ref, forward, backward in (
        (enc_ref, nt_weight, nn_weight),
        (low_ref, nn_weight, nt_weight),
        (dec_ref, nt_weight, nn_weight),
    ):
        outs[0][...] = forward(ref)
        outs[1][...] = backward(ref)
        outs = outs[2:]
    outs[0][...] = lift_ref[...]


def pack_x_kernel(f_in, c_in, f_ref, c_ref, lo_ref, hi_ref, lo2_ref, hi2_ref):
    f_ref[...] = f_in[...]
    c_ref[...] = c_in[...]
    paired = [jnp.concatenate([f_in[x, 0:4], f_in[x, 4:8]], -1) for x in range(2)]
    for x, out, out2 in ((0, lo_ref, lo2_ref), (1, hi_ref, hi2_ref)):
        out[0:8] = jnp.concatenate([f_in[x], c_in[x]], -1)
        out[8:12] = paired[1 - x]
        out2[...] = paired[x]


def pack_y_kernel(f_ref, c_ref, xlo, xhi, xlo2, xhi2, lo_ref, hi_ref):
    for first, out in ((0, lo_ref), (1, hi_ref)):
        at = slice(first, first + 7)
        out[0] = xlo[at]
        for x in range(2):
            out[1 + x] = jnp.concatenate([f_ref[x, at], c_ref[x, at]], -1)
        out[3] = xhi[at]
        for k, far, near in ((4, xlo2[...], xlo[8:12]), (5, xhi[8:12], xhi2[...])):
            pair = [jnp.concatenate([v[..., :64], v[..., 64:]], 0)[at] for v in (far, near)]
            out[k] = jnp.concatenate(pair, -1)


def encode_kernel(
    f_ref, ylo, yhi, xlo, xhi, xlo2, xhi2, inside, w_ref, fx_ref, enc_ref, slope_ref, pool_ref, tmp
):
    fx_ref[3:5, 7:15] = f_ref[...]
    fx_ref[2, 7:15] = xlo[0:8, :, :64]
    fx_ref[5, 7:15] = xhi[0:8, :, :64]
    for x, ref, first in ((1, xlo, 8), (6, xhi, 8), (0, xlo2, 0), (7, xhi2, 0)):
        fx_ref[x, 7:11] = ref[first : first + 4, :, :64]
        fx_ref[x, 11:15] = ref[first : first + 4, :, 64:]
    for y, ref in ((0, ylo), (15, yhi)):
        at = slice(y, y + 7)
        fx_ref[2:6, at] = ref[0:4, :, :, :64]
        for x, k in ((0, 4), (6, 5)):
            fx_ref[x, at] = ref[k, :, :, :64]
            fx_ref[x + 1, at] = ref[k, :, :, 64:]
    weight = w_ref[...]

    def edged(value, x):
        if x < 2 or x > 3:
            value = value * inside[0 if x < 2 else 1]
        return jnp.concatenate(
            [value[0:32] * inside[2], value[32:288], value[288:320] * inside[3]], 0
        )

    for x in range(6):
        pre = combined(nt(stacked(fx_ref, x, 1, 20, False), weight), 32, False)
        sigma = jax.nn.sigmoid(pre)
        enc = (pre * sigma).astype(BF16).astype(F32)
        near, slope = pre[160:480], sigma[160:480]
        slope_ref[x] = edged(slope * (1.0 + near * (1.0 - slope)), x)
        if 0 < x < 5:
            enc_ref[x - 1] = edged(enc[160:480], x).astype(BF16).reshape(10, 32, 64)
        wide = enc.reshape(10, 2, 32, 64)
        part = wide[:, 0] + wide[:, 1]
        if x % 2 == 0:
            held = part
            continue
        tmp[...] = (held + part).reshape(320, 64)
        pooled = tmp[pl.ds(0, 160, stride=2), :] + tmp[pl.ds(1, 160, stride=2), :]
        pooled = pooled * (0.125 if x == 3 else 0.125 * inside[0 if x == 1 else 1])
        pool_ref[x // 2, 3:7] = pooled[48:112].astype(BF16).reshape(4, 16, 64)
        pool_ref[x // 2, 0:3] = (pooled[0:48] * inside[2]).astype(BF16).reshape(3, 16, 64)
        pool_ref[x // 2, 7:10] = (pooled[112:160] * inside[3]).astype(BF16).reshape(3, 16, 64)


def joined_grad_kernel(c_ref, *refs):
    (ylo, yhi, xlo, xhi), (w_ref, lift_ref) = refs[:4], refs[4:6]
    cx_ref, jg_ref, kids_ref, adj_ref, tmp = refs[6:]
    cx_ref[1:3, 5:13] = c_ref[...]
    cx_ref[0, 5:13] = xlo[0:8, :, 64:]
    cx_ref[3, 5:13] = xhi[0:8, :, 64:]
    cx_ref[:, 0:5] = ylo[0:4, 2:7, :, 64:]
    cx_ref[:, 13:18] = yhi[0:4, 0:5, :, 64:]
    weight = w_ref[...]
    for x in range(2):
        grad = combined(nn(stacked(cx_ref, x, 1, 16, True), weight), 32, True)
        grad = grad.astype(BF16)
        jg_ref[x] = grad[96:416, :64]
        tmp[pl.ds(x * 512, 512), :] = grad.astype(F32)
    kids = []
    for p in range(2):
        for q in range(2):
            for r in range(2):
                rows = [
                    tmp[pl.ds(p * 512 + (2 * j + q) * 32 + r, 16, stride=2), :] for j in range(8)
                ]
                kids.append(jnp.concatenate(rows, 0)[:, 64:])
    kids = jnp.concatenate(kids, -1).astype(BF16)
    kids_ref[...] = kids[32:96]
    adj_ref[...] = nn(kids, lift_ref[...].reshape(512, 128))


def halver(halves):
    chunk = halves.shape[2]

    def put(row, block):
        at = pl.ds(row % chunk, block.shape[0])
        halves[row // chunk % 2, row // (2 * chunk), at, :] = block.astype(LINK)

    return put


def lower_kernel(px, inside, w_ref, adj_ref, la_ref, lg_ref, msg_ref):
    def masked(value):
        first, last = value[0:32] * inside[2], value[96:128] * inside[3]
        return jnp.concatenate([first, value[32:96], last], 0).astype(BF16)

    pre = combined(nn(stacked(px, 0, 1, 8, False), w_ref[...]), 16, False)
    sigma = jax.nn.sigmoid(pre)
    la = masked(pre * sigma)
    lg = masked(adj_ref[...] * (sigma * (1.0 + pre * (1.0 - sigma))))
    la_ref[...] = la[16:112]
    lg_ref[...] = lg
    msg_ref[0:96] = la[16:112]
    msg_ref[96:224] = lg


def doubled(coarse, tmp):
    rows = coarse.shape[0]
    tmp[pl.ds(0, rows, stride=2), :] = coarse
    tmp[pl.ds(1, rows, stride=2), :] = coarse
    wide = tmp[...].reshape(rows // 16, 1, 32, 64)
    return jnp.broadcast_to(wide, (rows // 16, 2, 32, 64)).reshape(4 * rows, 64)


def grads_kernel(px, la_ref, lg_ref, core, lift_ref, kids_ref, cx_ref, enc_ref, *refs):
    (w_ref, slope_ref, jg_ref, fx_ref), refs = refs[:4], refs[4:]
    lifted_ref, keep_ref, send_ref, tmp, halves, enc_halves, wide = refs
    put, put_enc = halver(halves), halver(enc_halves)
    la, lg = la_ref[...], lg_ref[...]
    fine = nt(la, lift_ref[...].reshape(512, 128)).astype(BF16).astype(F32)
    for p in range(2):
        for q in range(2):
            for r in range(2):
                k = 4 * p + 2 * q + r
                for j in range(6):
                    y = 2 * j + q - 1
                    if 0 <= y < 10:
                        tmp[pl.ds((p * 10 + y) * 32 + r, 16, stride=2), :] = fine[
                            16 * j : 16 * j + 16, 64 * k : 64 * k + 64
                        ]
    lifted_ref[...] = tmp[...].astype(BF16).reshape(2, 10, 32, 64)
    lifted = jnp.concatenate([tmp[32:288], tmp[352:608]], 0)
    la, lg = la[16:80], lg[32:96]
    enc = enc_ref[1:3, 1:9].reshape(512, 64).astype(F32)
    joined = ztaps(jnp.concatenate([enc, lifted], -1), 32, False)
    dec = tn(stacked(cx_ref, 0, 2, 8, True, 4), joined)
    for ab in range(9):
        for c in range(3):
            block = dec[64 * ab : 64 * ab + 64, 128 * c : 128 * c + 128]
            put((3 * ab + c) * 64, block)
    low = tn(stacked(px, 0, 1, 4, False, 2), ztaps(lg.astype(F32), 16, True))
    for ab in range(9):
        for c in range(3):
            block = low[64 * ab : 64 * ab + 64, 128 * c : 128 * c + 128]
            put(1728 + (3 * ab + c) * 64, block)
    lift = tn(kids_ref[...], la)
    for k in range(8):
        put(3456 + 64 * k, lift[64 * k : 64 * k + 64])
    for row in (3968, 4032):
        put(row, jnp.zeros((64, 128), F32))
    lg = lg_ref[...].reshape(8, 16, 128)
    source = jnp.concatenate([lg[3 - b : 7 - b].reshape(64, 128) for b in range(3)], -1)
    grad = jnp.zeros((192, 576), F32)
    for a in range(3):
        pg = combined(nt(source, w_ref[:, 384 * a : 384 * a + 384]), 16, True)
        fine = doubled(pg * 0.125, wide)
        parts = []
        for x in (2 * a, 2 * a + 1):
            own = fine if a != 1 else fine + jg_ref[x - 2, 32:288].astype(F32)
            parts.append(own * slope_ref[x, 32:288])
        eg = ztaps(jnp.concatenate(parts, 0), 32, True)
        grad = grad + tn(eg, stacked(fx_ref, 2 * a, 2, 8, False, 6))
    for ab in range(9):
        for c in range(3):
            block = grad[64 * c : 64 * c + 64, 64 * ab : 64 * ab + 64]
            block = jnp.concatenate([block[:32], block[32:]], -1)
            put_enc((3 * ab + c) * 32, block[:16])
            put_enc((3 * ab + c) * 32 + 16, block[16:])
    for row in range(864, 1024, 16):
        put_enc(row, jnp.zeros((16, 128), F32))
    mine, chunk = core[0], halves.shape[2]
    keep_ref[:, :chunk, :] = halves[mine]
    send_ref[:, :chunk, :] = halves[1 - mine]
    keep_ref[:, chunk:, :] = enc_halves[mine]
    send_ref[:, chunk:, :] = enc_halves[1 - mine]


def add_kernel(a_ref, b_ref, out_ref):
    out_ref[...] = (a_ref[...].astype(F32) + b_ref[...].astype(F32)).astype(LINK)


def plane(rows):
    return jnp.concatenate([rows[:, :64], rows[:, 64:]], 0).reshape(1, 10, 32, 64)


def encoder_grad_kernel(
    lg_ref, xlo, xhi, w_ref, slope_ref, jg_ref, eg_ref, lo_ref, hi_ref, lx, tmp
):
    lx[0] = xlo[96:224].reshape(8, 16, 128)
    lx[1] = lg_ref[...].reshape(8, 16, 128)
    lx[2] = xhi[96:224].reshape(8, 16, 128)
    pg = combined(nt(stacked(lx, 0, 1, 6, True), w_ref[...]), 16, True)
    fine = doubled(pg.astype(BF16).astype(F32) * 0.125, tmp)[32:352]
    for x, msg in ((0, lo_ref), (1, hi_ref)):
        eg = ((jg_ref[x].astype(F32) + fine) * slope_ref[2 + x]).astype(BF16)
        eg_ref[x] = eg.reshape(10, 32, 64)
        msg[...] = jnp.concatenate([eg[:160], eg[160:]], -1)


def decode_kernel(enc_ref, lifted_ref, xlo, xhi, lift_ref, w_ref, out_ref, jx, tx):
    jx[1:3] = jnp.concatenate([enc_ref[1:3], lifted_ref[...]], -1)
    for p, h in ((1, xlo), (0, xhi)):
        for q in range(2):
            for r in range(2):
                fine = nt(h[0:96], lift_ref[4 * p + 2 * q + r]).astype(BF16).astype(F32)
                for j in range(6):
                    y = 2 * j + q - 1
                    if 0 <= y < 10:
                        tx[pl.ds(32 * y + r, 16, stride=2), :] = fine[16 * j : 16 * j + 16]
        lifted = tx[...].astype(BF16).reshape(1, 10, 32, 64)
        x = 0 if p == 1 else 3
        jx[x : x + 1] = jnp.concatenate([enc_ref[x : x + 1], lifted], -1)
    weight = w_ref[...]
    for x in range(2):
        out = combined(nt(stacked(jx, x, 1, 8, False), weight), 32, False)
        out_ref[x] = out.astype(BF16).reshape(8, 32, 64)


def input_grad_kernel(eg_ref, xlo, xhi, w_ref, out_ref, ex):
    ex[0:1] = plane(xlo[...])
    ex[1:3] = eg_ref[...]
    ex[3:4] = plane(xhi[...])
    weight = w_ref[...]
    for x in range(2):
        out = combined(nn(stacked(ex, x, 1, 8, True), weight), 32, True)
        out_ref[x] = out.astype(BF16).reshape(8, 32, 64)


def sum_kernel(parts_ref, out_ref):
    total = parts_ref[0].astype(F32)
    for k in range(1, parts_ref.shape[0]):
        total = total + parts_ref[k].astype(F32)
    total = total.astype(LINK)
    for k in range(out_ref.shape[0]):
        out_ref[k] = total


def widen_kernel(core, own_ref, other_ref, *refs):
    outs, (encoder, decoder, lower, lift), sems = refs[:4], refs[4:8], refs[8]
    own, other = own_ref[...].astype(F32), other_ref[...].astype(F32)
    first = core[0] == 0
    both = jnp.stack([jnp.where(first, own, other), jnp.where(first, other, own)], 1)
    chunk = own.shape[1] // 5 * 4
    sums = both[:, :, :chunk].reshape(4096, 128)
    wide = both[:, :, chunk:].reshape(1024, 128)[:864].reshape(27, 32, 128)
    copies = [
        pltpu.make_async_copy(a, b, sems.at[k])
        for k, (a, b) in enumerate(zip((encoder, decoder, lower, lift), outs))
    ]
    decoder[...] = sums[0:1728].reshape(27, 64, 128)
    copies[1].start()
    lower[...] = sums[1728:3456].reshape(27, 64, 128)
    copies[2].start()
    lift[...] = sums[3456:3968].reshape(8, 64, 128)
    copies[3].start()
    encoder[:, 0:32, :] = wide[..., :64]
    encoder[:, 32:64, :] = wide[..., 64:]
    copies[0].start()
    for copy in copies:
        copy.wait()


def per_device(features, encoder_weight, lower_weight, lift_weight, decoder_weight, cotangent):
    f = jnp.transpose(features, (1, 2, 3, 0))
    c = jnp.transpose(cotangent, (1, 2, 3, 0))
    lower_t = jnp.transpose(lower_weight, (0, 2, 1))
    brick, tall = (2, 8, 32, 64), (2, 10, 32, 64)

    size_x, size_z = lax.axis_size("gx"), lax.axis_size("gz")
    at_x, at_y = lax.axis_index("gx"), lax.axis_index(GY)
    inside = jnp.stack([at_x > 0, at_x < size_x - 1, at_y > 0, at_y < 2 * size_z - 1]).astype(F32)
    core = lax.axis_index("gc").reshape(1)

    f, c, lo, hi, lo2, hi2 = call(
        pack_x_kernel,
        [(brick, BF16)] * 2 + [((12, 32, 128), BF16)] * 2 + [((4, 32, 128), BF16)] * 2,
        [],
        [f, c],
    )
    x_halo = swapped(lo, hi, GX)
    far_halo = [shifted(hi2, GX, 2), shifted(lo2, GX, -2)]
    edges = call(
        pack_y_kernel,
        [((6, 7, 32, 128), BF16)] * 2,
        [],
        [f, c, *x_halo, *far_halo],
    )
    y_halo = swapped(*edges, GY)
    enc_fwd, enc_bwd, low_fwd, low_bwd, dec_fwd, dec_bwd, lift = call(
        stack_kernel,
        [
            ((192, 576), BF16),
            ((576, 192), BF16),
            ((576, 384), BF16),
            ((192, 1152), BF16),
            ((192, 1152), BF16),
            ((576, 384), BF16),
            ((8, 64, 128), BF16),
        ],
        [],
        [edges[0], encoder_weight, lower_t, decoder_weight, lift_weight],
        spaces={0: pltpu.HBM},
        flops=2 * 10**9,
    )
    fx, encoded, slope, pooled = call(
        encode_kernel,
        [((8, 22, 32, 64), BF16), ((4, 10, 32, 64), BF16)]
        + [((6, 320, 64), F32), ((3, 10, 16, 64), BF16)],
        [((320, 64), F32)],
        [f, *y_halo, *x_halo, *far_halo, inside, enc_fwd],
        spaces={7: pltpu.SMEM},
    )
    cx, jg, kids, adj = call(
        joined_grad_kernel,
        [
            ((4, 18, 32, 64), BF16),
            ((2, 320, 64), BF16),
            ((64, 512), BF16),
            ((128, 128), F32),
        ],
        [((1024, 128), F32)],
        [c, *y_halo, *x_halo, dec_bwd, lift],
    )
    half = (size_x, 2560 // size_x, 128)
    la, lg, edge = call(
        lower_kernel,
        [((96, 128), BF16), ((128, 128), BF16), ((224, 128), BF16)],
        [],
        [pooled, inside, low_fwd, adj],
        spaces={1: pltpu.SMEM},
    )
    lifted, keep, send = call(
        grads_kernel,
        [(tall, BF16), (half, LINK), (half, LINK)],
        [
            ((640, 64), F32),
            ((2, size_x, 2048 // size_x, 128), LINK),
            ((2, size_x, 512 // size_x, 128), LINK),
            ((128, 64), F32),
        ],
        [pooled, la, lg, core, lift, kids, cx, encoded, low_bwd, slope, jg, fx],
        spaces={3: pltpu.SMEM},
    )
    (sums,) = call(add_kernel, [(half, LINK)], [], [keep, partner(send)])
    sums, edge = lax.optimization_barrier((sums, edge))
    sums = lax.all_to_all(sums, "gx", 0, 0)
    halo = swapped(edge, edge, GX)
    (sums,) = call(sum_kernel, [((size_z,) + half[1:], LINK)], [], [sums])
    sums, halo = lax.optimization_barrier((sums, halo))
    sums = lax.all_to_all(sums, "gz", 0, 0)
    eg, *edges = call(
        encoder_grad_kernel,
        [(tall, BF16)] + [((160, 128), BF16)] * 2,
        [((3, 8, 16, 128), BF16), ((192, 64), F32)],
        [lg, *halo, low_bwd, slope, jg],
        flops=2 * 10**9,
    )
    (sums,) = call(sum_kernel, [(half, LINK)], [], [sums])
    sums, edges = lax.optimization_barrier((sums, edges))
    sums = lax.all_to_all(sums, "gx", 0, 0)
    eg_halo = swapped(*edges, GX)
    (decoded,) = call(
        decode_kernel,
        [(brick, BF16)],
        [((4, 10, 32, 128), BF16), ((320, 64), F32)],
        [encoded, lifted, *halo, lift, dec_fwd],
    )
    sums, eg_halo, decoded = lax.optimization_barrier((sums, eg_halo, decoded))
    (input_grad,) = call(
        input_grad_kernel,
        [(brick, BF16)],
        [((4, 10, 32, 64), BF16)],
        [eg, *eg_halo, enc_bwd],
        flops=2 * 10**9,
    )
    shapes = [((27, 64, 64), F32), ((27, 64, 128), F32), ((27, 64, 128), F32), ((8, 64, 128), F32)]
    encoder_gradient, decoder_gradient, lower_gradient, lift_gradient = call(
        widen_kernel,
        shapes,
        shapes + [(pltpu.SemaphoreType.DMA((4,)), None)],
        [core, sums, partner(sums)],
        spaces={0: pltpu.SMEM},
        out_space=pltpu.HBM,
    )
    return (
        jnp.transpose(decoded, (3, 0, 1, 2)),
        jnp.transpose(input_grad, (3, 0, 1, 2)),
        encoder_gradient,
        jnp.transpose(lower_gradient, (0, 2, 1)),
        lift_gradient,
        decoder_gradient,
    )


def solution(mesh):
    size_x, size_y = mesh.devices.shape
    chips = Mesh(mesh.devices.reshape(size_x, size_y // 2, 2), ("gx", "gz", "gc"))
    field = P(None, "gx", ("gz", "gc"), None)
    return jax.shard_map(
        per_device,
        mesh=chips,
        in_specs=(field, P(), P(), P(), P(), field),
        out_specs=(field, field, P(), P(), P(), P()),
        check_vma=False,
    )
```

```python
import math

import jax
import jax.numpy as jnp
from jax import lax
from jax.experimental import pallas as pl
from jax.experimental.pallas import tpu as pltpu
from jax.sharding import Mesh, PartitionSpec as P

F32, BF16 = jnp.float32, jnp.bfloat16
LINK = BF16
GX, GY = ("gx",), ("gz", "gc")
TAPS9 = tuple((a, b) for a in range(3) for b in range(3))


def shifted(piece, axes, step):
    size = math.prod(lax.axis_size(axis) for axis in axes)
    pairs = [(i, i + step) for i in range(size) if 0 <= i + step < size]
    return lax.ppermute(piece, axes, pairs)


def swapped(low, high, axes):
    return shifted(high, axes, 1), shifted(low, axes, -1)


def partner(piece):
    return lax.ppermute(piece, "gc", [(0, 1), (1, 0)])


def call(kernel, outs, scratch, operands, spaces=(), flops=10**6):
    return pl.pallas_call(
        kernel,
        out_shape=[jax.ShapeDtypeStruct(s, d) for s, d in outs],
        in_specs=[
            pl.BlockSpec(memory_space=dict(spaces).get(i, pltpu.VMEM)) for i in range(len(operands))
        ],
        out_specs=[pl.BlockSpec(memory_space=pltpu.VMEM)] * len(outs),
        scratch_shapes=[s if d is None else pltpu.VMEM(s, d) for s, d in scratch],
        compiler_params=pltpu.CompilerParams(vmem_limit_bytes=40 * 2**20),
        cost_estimate=pl.CostEstimate(flops=flops, bytes_accessed=10**4, transcendentals=0),
    )(*operands)


def nn(a, b):
    return lax.dot_general(a, b, (((1,), (0,)), ((), ())), preferred_element_type=F32)


def nt(a, b):
    return lax.dot_general(a, b, (((1,), (1,)), ((), ())), preferred_element_type=F32)


def tn(a, b):
    return lax.dot_general(a, b, (((0,), (0,)), ((), ())), preferred_element_type=F32)


def nn_weight(ref):
    rows = [jnp.concatenate([ref[3 * ab + c] for c in range(3)], -1) for ab in range(9)]
    return jnp.concatenate(rows, 0)


def nt_weight(ref):
    rows = [jnp.concatenate([ref[3 * ab + c] for ab in range(9)], -1) for c in range(3)]
    return jnp.concatenate(rows, 0)


def stacked(ref, x, nx, ny, adjoint, y=0):
    pieces = []
    for a, b in TAPS9:
        i, j = (x + 2 - a, y + 2 - b) if adjoint else (x + a, y + b)
        piece = ref[i : i + nx, j : j + ny]
        pieces.append(piece.reshape(nx * ny * piece.shape[2], piece.shape[3]))
    return jnp.concatenate(pieces, -1)


def zshift(value, step, depth):
    rows = value.shape[0]
    z = lax.broadcasted_iota(jnp.int32, value.shape, 0) & (depth - 1)
    moved = pltpu.roll(value, step % rows, 0)
    return jnp.where(z == (0 if step > 0 else depth - 1), 0.0, moved)


def combined(parts, depth, adjoint):
    ch = parts.shape[1] // 3
    step = -1 if adjoint else 1
    return (
        zshift(parts[:, :ch], step, depth)
        + parts[:, ch : 2 * ch]
        + zshift(parts[:, 2 * ch :], -step, depth)
    )


def ztaps(value, depth, adjoint):
    step = -1 if adjoint else 1
    return jnp.concatenate(
        [
            zshift(value, step, depth).astype(BF16),
            value.astype(BF16),
            zshift(value, -step, depth).astype(BF16),
        ],
        -1,
    )


def stack_kernel(first_ref, enc_ref, low_ref, dec_ref, lift_ref, *outs):
    for ref, forward, backward in (
        (enc_ref, nt_weight, nn_weight),
        (low_ref, nn_weight, nt_weight),
        (dec_ref, nt_weight, nn_weight),
    ):
        outs[0][...] = forward(ref)
        outs[1][...] = backward(ref)
        outs = outs[2:]
    outs[0][...] = lift_ref[...]


def pack_x_kernel(f_in, c_in, f_ref, c_ref, lo_ref, hi_ref, lo2_ref, hi2_ref):
    f_ref[...] = f_in[...]
    c_ref[...] = c_in[...]
    paired = [jnp.concatenate([f_in[x, 0:4], f_in[x, 4:8]], -1) for x in range(2)]
    for x, out, out2 in ((0, lo_ref, lo2_ref), (1, hi_ref, hi2_ref)):
        out[0:8] = jnp.concatenate([f_in[x], c_in[x]], -1)
        out[8:12] = paired[1 - x]
        out2[...] = paired[x]


def pack_y_kernel(f_ref, c_ref, xlo, xhi, xlo2, xhi2, lo_ref, hi_ref):
    for first, out in ((0, lo_ref), (1, hi_ref)):
        at = slice(first, first + 7)
        out[0] = xlo[at]
        for x in range(2):
            out[1 + x] = jnp.concatenate([f_ref[x, at], c_ref[x, at]], -1)
        out[3] = xhi[at]
        for k, far, near in ((4, xlo2[...], xlo[8:12]), (5, xhi[8:12], xhi2[...])):
            pair = [jnp.concatenate([v[..., :64], v[..., 64:]], 0)[at] for v in (far, near)]
            out[k] = jnp.concatenate(pair, -1)


def encode_kernel(
    f_ref, ylo, yhi, xlo, xhi, xlo2, xhi2, inside, w_ref, fx_ref, enc_ref, slope_ref, pool_ref, tmp
):
    fx_ref[3:5, 7:15] = f_ref[...]
    fx_ref[2, 7:15] = xlo[0:8, :, :64]
    fx_ref[5, 7:15] = xhi[0:8, :, :64]
    for x, ref, first in ((1, xlo, 8), (6, xhi, 8), (0, xlo2, 0), (7, xhi2, 0)):
        fx_ref[x, 7:11] = ref[first : first + 4, :, :64]
        fx_ref[x, 11:15] = ref[first : first + 4, :, 64:]
    for y, ref in ((0, ylo), (15, yhi)):
        at = slice(y, y + 7)
        fx_ref[2:6, at] = ref[0:4, :, :, :64]
        for x, k in ((0, 4), (6, 5)):
            fx_ref[x, at] = ref[k, :, :, :64]
            fx_ref[x + 1, at] = ref[k, :, :, 64:]
    weight = w_ref[...]

    def edged(value, x):
        if x < 2 or x > 3:
            value = value * inside[0 if x < 2 else 1]
        return jnp.concatenate(
            [value[0:32] * inside[2], value[32:288], value[288:320] * inside[3]], 0
        )

    for x in range(6):
        pre = combined(nt(stacked(fx_ref, x, 1, 20, False), weight), 32, False)
        sigma = jax.nn.sigmoid(pre)
        enc = (pre * sigma).astype(BF16).astype(F32)
        near, slope = pre[160:480], sigma[160:480]
        slope_ref[x] = edged(slope * (1.0 + near * (1.0 - slope)), x)
        if 0 < x < 5:
            enc_ref[x - 1] = edged(enc[160:480], x).astype(BF16).reshape(10, 32, 64)
        wide = enc.reshape(10, 2, 32, 64)
        part = wide[:, 0] + wide[:, 1]
        if x % 2 == 0:
            held = part
            continue
        tmp[...] = (held + part).reshape(320, 64)
        pooled = tmp[pl.ds(0, 160, stride=2), :] + tmp[pl.ds(1, 160, stride=2), :]
        pooled = pooled * (0.125 if x == 3 else 0.125 * inside[0 if x == 1 else 1])
        pool_ref[x // 2, 3:7] = pooled[48:112].astype(BF16).reshape(4, 16, 64)
        pool_ref[x // 2, 0:3] = (pooled[0:48] * inside[2]).astype(BF16).reshape(3, 16, 64)
        pool_ref[x // 2, 7:10] = (pooled[112:160] * inside[3]).astype(BF16).reshape(3, 16, 64)


def joined_grad_kernel(
    c_ref, ylo, yhi, xlo, xhi, w_ref, lift_ref, cx_ref, jg_ref, kids_ref, adj_ref, tmp
):
    cx_ref[1:3, 5:13] = c_ref[...]
    cx_ref[0, 5:13] = xlo[0:8, :, 64:]
    cx_ref[3, 5:13] = xhi[0:8, :, 64:]
    cx_ref[:, 0:5] = ylo[0:4, 2:7, :, 64:]
    cx_ref[:, 13:18] = yhi[0:4, 0:5, :, 64:]
    weight = w_ref[...]
    for x in range(2):
        grad = combined(nn(stacked(cx_ref, x, 1, 16, True), weight), 32, True)
        grad = grad.astype(BF16)
        jg_ref[x] = grad[96:416, :64]
        tmp[pl.ds(x * 512, 512), :] = grad.astype(F32)
    kids = []
    for p in range(2):
        for q in range(2):
            for r in range(2):
                rows = [
                    tmp[pl.ds(p * 512 + (2 * j + q) * 32 + r, 16, stride=2), :] for j in range(8)
                ]
                kids.append(jnp.concatenate(rows, 0)[:, 64:])
    kids = jnp.concatenate(kids, -1).astype(BF16)
    kids_ref[...] = kids[32:96]
    adj_ref[...] = nn(kids, lift_ref[...].reshape(512, 128))


def halver(halves):
    chunk = halves.shape[2]

    def put(row, block):
        at = pl.ds(row % chunk, block.shape[0])
        halves[row // chunk % 2, row // (2 * chunk), at, :] = block.astype(LINK)

    return put


def lower_kernel(px, inside, w_ref, adj_ref, la_ref, lg_ref, msg_ref):
    def masked(value):
        first, last = value[0:32] * inside[2], value[96:128] * inside[3]
        return jnp.concatenate([first, value[32:96], last], 0).astype(BF16)

    pre = combined(nn(stacked(px, 0, 1, 8, False), w_ref[...]), 16, False)
    sigma = jax.nn.sigmoid(pre)
    la = masked(pre * sigma)
    lg = masked(adj_ref[...] * (sigma * (1.0 + pre * (1.0 - sigma))))
    la_ref[...] = la[16:112]
    lg_ref[...] = lg
    msg_ref[0:96] = la[16:112]
    msg_ref[96:224] = lg


def doubled(coarse, tmp):
    rows = coarse.shape[0]
    tmp[pl.ds(0, rows, stride=2), :] = coarse
    tmp[pl.ds(1, rows, stride=2), :] = coarse
    wide = tmp[...].reshape(rows // 16, 1, 32, 64)
    return jnp.broadcast_to(wide, (rows // 16, 2, 32, 64)).reshape(4 * rows, 64)


def grads_kernel(px, la_ref, lg_ref, core, lift_ref, kids_ref, cx_ref, enc_ref, *refs):
    (w_ref, slope_ref, jg_ref, fx_ref), refs = refs[:4], refs[4:]
    lifted_ref, keep_ref, send_ref, tmp, halves, enc_halves, wide = refs
    put, put_enc = halver(halves), halver(enc_halves)
    la, lg = la_ref[...], lg_ref[...]
    fine = nt(la, lift_ref[...].reshape(512, 128)).astype(BF16).astype(F32)
    for p in range(2):
        for q in range(2):
            for r in range(2):
                k = 4 * p + 2 * q + r
                for j in range(6):
                    y = 2 * j + q - 1
                    if 0 <= y < 10:
                        tmp[pl.ds((p * 10 + y) * 32 + r, 16, stride=2), :] = fine[
                            16 * j : 16 * j + 16, 64 * k : 64 * k + 64
                        ]
    lifted_ref[...] = tmp[...].astype(BF16).reshape(2, 10, 32, 64)
    lifted = jnp.concatenate([tmp[32:288], tmp[352:608]], 0)
    la, lg = la[16:80], lg[32:96]
    enc = enc_ref[1:3, 1:9].reshape(512, 64).astype(F32)
    joined = ztaps(jnp.concatenate([enc, lifted], -1), 32, False)
    dec = tn(stacked(cx_ref, 0, 2, 8, True, 4), joined)
    for ab in range(9):
        for c in range(3):
            block = dec[64 * ab : 64 * ab + 64, 128 * c : 128 * c + 128]
            put((3 * ab + c) * 64, block)
    low = tn(stacked(px, 0, 1, 4, False, 2), ztaps(lg.astype(F32), 16, True))
    for ab in range(9):
        for c in range(3):
            block = low[64 * ab : 64 * ab + 64, 128 * c : 128 * c + 128]
            put(1728 + (3 * ab + c) * 64, block)
    lift = tn(kids_ref[...], la)
    for k in range(8):
        put(3456 + 64 * k, lift[64 * k : 64 * k + 64])
    for row in (3968, 4032):
        put(row, jnp.zeros((64, 128), F32))
    lg = lg_ref[...].reshape(8, 16, 128)
    source = jnp.concatenate([lg[3 - b : 7 - b].reshape(64, 128) for b in range(3)], -1)
    grad = jnp.zeros((192, 576), F32)
    for a in range(3):
        pg = combined(nt(source, w_ref[:, 384 * a : 384 * a + 384]), 16, True)
        fine = doubled(pg * 0.125, wide)
        parts = []
        for x in (2 * a, 2 * a + 1):
            own = fine if a != 1 else fine + jg_ref[x - 2, 32:288].astype(F32)
            parts.append(own * slope_ref[x, 32:288])
        eg = ztaps(jnp.concatenate(parts, 0), 32, True)
        grad = grad + tn(eg, stacked(fx_ref, 2 * a, 2, 8, False, 6))
    for ab in range(9):
        for c in range(3):
            block = grad[64 * c : 64 * c + 64, 64 * ab : 64 * ab + 64]
            block = jnp.concatenate([block[:32], block[32:]], -1)
            put_enc((3 * ab + c) * 32, block[:16])
            put_enc((3 * ab + c) * 32 + 16, block[16:])
    for row in range(864, 1024, 16):
        put_enc(row, jnp.zeros((16, 128), F32))
    mine, chunk = core[0], halves.shape[2]
    keep_ref[:, :chunk, :] = halves[mine]
    send_ref[:, :chunk, :] = halves[1 - mine]
    keep_ref[:, chunk:, :] = enc_halves[mine]
    send_ref[:, chunk:, :] = enc_halves[1 - mine]


def middle_kernel(f_ref, c_ref, *refs):
    (ylo, yhi, xlo, xhi, xlo2, xhi2, inside, core), refs = refs[:8], refs[8:]
    (enc_w, dec_w, low_w, low_wt, lift), refs = refs[:5], refs[5:]
    (enc, slope, jg, lg, msg, lifted, keep, send), refs = refs[:8], refs[8:]
    (fx, cx, pool, kids, adj, la, tmp, kid_tmp, lift_tmp, halves, enc_halves, wide) = refs
    joined_grad_kernel(c_ref, ylo, yhi, xlo, xhi, dec_w, lift, cx, jg, kids, adj, kid_tmp)
    encode_kernel(
        f_ref, ylo, yhi, xlo, xhi, xlo2, xhi2, inside, enc_w, fx, enc, slope, pool, tmp
    )
    lower_kernel(pool, inside, low_w, adj, la, lg, msg)
    grads_kernel(
        *(pool, la, lg, core, lift, kids, cx, enc, low_wt, slope, jg, fx),
        *(lifted, keep, send, lift_tmp, halves, enc_halves, wide),
    )


def add_kernel(a_ref, b_ref, out_ref):
    out_ref[...] = (a_ref[...].astype(F32) + b_ref[...].astype(F32)).astype(LINK)


def plane(rows):
    return jnp.concatenate([rows[:, :64], rows[:, 64:]], 0).reshape(1, 10, 32, 64)


def encoder_grad_kernel(
    lg_ref, xlo, xhi, w_ref, slope_ref, jg_ref, eg_ref, lo_ref, hi_ref, lx, tmp
):
    lx[0] = xlo[96:224].reshape(8, 16, 128)
    lx[1] = lg_ref[...].reshape(8, 16, 128)
    lx[2] = xhi[96:224].reshape(8, 16, 128)
    pg = combined(nt(stacked(lx, 0, 1, 6, True), w_ref[...]), 16, True)
    fine = doubled(pg.astype(BF16).astype(F32) * 0.125, tmp)[32:352]
    for x, msg in ((0, lo_ref), (1, hi_ref)):
        eg = ((jg_ref[x].astype(F32) + fine) * slope_ref[2 + x]).astype(BF16)
        eg_ref[x] = eg.reshape(10, 32, 64)
        msg[...] = jnp.concatenate([eg[:160], eg[160:]], -1)


def decode_kernel(enc_ref, lifted_ref, xlo, xhi, lift_ref, w_ref, out_ref, jx, tx):
    jx[1:3] = jnp.concatenate([enc_ref[1:3], lifted_ref[...]], -1)
    for p, h in ((1, xlo), (0, xhi)):
        for q in range(2):
            for r in range(2):
                fine = nt(h[0:96], lift_ref[4 * p + 2 * q + r]).astype(BF16).astype(F32)
                for j in range(6):
                    y = 2 * j + q - 1
                    if 0 <= y < 10:
                        tx[pl.ds(32 * y + r, 16, stride=2), :] = fine[16 * j : 16 * j + 16]
        lifted = tx[...].astype(BF16).reshape(1, 10, 32, 64)
        x = 0 if p == 1 else 3
        jx[x : x + 1] = jnp.concatenate([enc_ref[x : x + 1], lifted], -1)
    weight = w_ref[...]
    for x in range(2):
        out = combined(nt(stacked(jx, x, 1, 8, False), weight), 32, False)
        out_ref[x] = out.astype(BF16).reshape(8, 32, 64)


def input_grad_kernel(eg_ref, xlo, xhi, w_ref, out_ref, ex):
    ex[0:1] = plane(xlo[...])
    ex[1:3] = eg_ref[...]
    ex[3:4] = plane(xhi[...])
    weight = w_ref[...]
    for x in range(2):
        out = combined(nn(stacked(ex, x, 1, 8, True), weight), 32, True)
        out_ref[x] = out.astype(BF16).reshape(8, 32, 64)


def sum_kernel(parts_ref, out_ref):
    total = parts_ref[0].astype(F32)
    for k in range(1, parts_ref.shape[0]):
        total = total + parts_ref[k].astype(F32)
    total = total.astype(LINK)
    for k in range(out_ref.shape[0]):
        out_ref[k] = total


def widen_kernel(core, own_ref, other_ref, encoder_ref, decoder_ref, lower_ref, lift_ref):
    own, other = own_ref[...].astype(F32), other_ref[...].astype(F32)
    first = core[0] == 0
    both = jnp.stack([jnp.where(first, own, other), jnp.where(first, other, own)], 1)
    chunk = own.shape[1] // 5 * 4
    sums = both[:, :, :chunk].reshape(4096, 128)
    decoder_ref[...] = sums[0:1728].reshape(27, 64, 128)
    lower_ref[...] = sums[1728:3456].reshape(27, 64, 128)
    lift_ref[...] = sums[3456:3968].reshape(8, 64, 128)
    wide = both[:, :, chunk:].reshape(1024, 128)[:864].reshape(27, 32, 128)
    encoder_ref[:, 0:32, :] = wide[..., :64]
    encoder_ref[:, 32:64, :] = wide[..., 64:]


def per_device(features, encoder_weight, lower_weight, lift_weight, decoder_weight, cotangent):
    f = jnp.transpose(features, (1, 2, 3, 0))
    c = jnp.transpose(cotangent, (1, 2, 3, 0))
    lower_t = jnp.transpose(lower_weight, (0, 2, 1))
    brick, tall = (2, 8, 32, 64), (2, 10, 32, 64)

    size_x, size_z = lax.axis_size("gx"), lax.axis_size("gz")
    at_x, at_y = lax.axis_index("gx"), lax.axis_index(GY)
    inside = jnp.stack([at_x > 0, at_x < size_x - 1, at_y > 0, at_y < 2 * size_z - 1]).astype(F32)
    core = lax.axis_index("gc").reshape(1)

    f, c, lo, hi, lo2, hi2 = call(
        pack_x_kernel,
        [(brick, BF16)] * 2 + [((12, 32, 128), BF16)] * 2 + [((4, 32, 128), BF16)] * 2,
        [],
        [f, c],
    )
    x_halo = swapped(lo, hi, GX)
    far_halo = [shifted(hi2, GX, 2), shifted(lo2, GX, -2)]
    edges = call(
        pack_y_kernel,
        [((6, 7, 32, 128), BF16)] * 2,
        [],
        [f, c, *x_halo, *far_halo],
    )
    y_halo = swapped(*edges, GY)
    enc_fwd, enc_bwd, low_fwd, low_bwd, dec_fwd, dec_bwd, lift = call(
        stack_kernel,
        [
            ((192, 576), BF16),
            ((576, 192), BF16),
            ((576, 384), BF16),
            ((192, 1152), BF16),
            ((192, 1152), BF16),
            ((576, 384), BF16),
            ((8, 64, 128), BF16),
        ],
        [],
        [edges[0], encoder_weight, lower_t, decoder_weight, lift_weight],
        spaces={0: pltpu.HBM},
        flops=2 * 10**9,
    )
    half = (size_x, 2560 // size_x, 128)
    encoded, slope, jg, lg, edge, lifted, keep, send = call(
        middle_kernel,
        [((4, 10, 32, 64), BF16), ((6, 320, 64), F32), ((2, 320, 64), BF16)]
        + [((128, 128), BF16), ((224, 128), BF16), (tall, BF16), (half, LINK), (half, LINK)],
        [
            ((8, 22, 32, 64), BF16),
            ((4, 18, 32, 64), BF16),
            ((3, 10, 16, 64), BF16),
            ((64, 512), BF16),
            ((128, 128), F32),
            ((96, 128), BF16),
            ((320, 64), F32),
            ((1024, 128), F32),
            ((640, 64), F32),
            ((2, size_x, 2048 // size_x, 128), LINK),
            ((2, size_x, 512 // size_x, 128), LINK),
            ((128, 64), F32),
        ],
        [f, c, *y_halo, *x_halo, *far_halo, inside, core]
        + [enc_fwd, dec_bwd, low_fwd, low_bwd, lift],
        spaces={8: pltpu.SMEM, 9: pltpu.SMEM},
    )
    (sums,) = call(add_kernel, [(half, LINK)], [], [keep, partner(send)])
    sums = lax.all_to_all(sums, "gx", 0, 0)
    (sums,) = call(sum_kernel, [((size_z,) + half[1:], LINK)], [], [sums])
    sums, edge = lax.optimization_barrier((sums, edge))
    sums = lax.all_to_all(sums, "gz", 0, 0)
    halo = swapped(edge, edge, GX)
    (sums,) = call(sum_kernel, [(half, LINK)], [], [sums])
    sums, halo = lax.optimization_barrier((sums, halo))
    sums = lax.all_to_all(sums, "gx", 0, 0)
    eg, *edges = call(
        encoder_grad_kernel,
        [(tall, BF16)] + [((160, 128), BF16)] * 2,
        [((3, 8, 16, 128), BF16), ((192, 64), F32)],
        [lg, *halo, low_bwd, slope, jg],
    )
    eg_halo = swapped(*edges, GX)
    (decoded,) = call(
        decode_kernel,
        [(brick, BF16)],
        [((4, 10, 32, 128), BF16), ((320, 64), F32)],
        [encoded, lifted, *halo, lift, dec_fwd],
    )
    sums, eg_halo, decoded = lax.optimization_barrier((sums, eg_halo, decoded))
    (input_grad,) = call(
        input_grad_kernel,
        [(brick, BF16)],
        [((4, 10, 32, 64), BF16)],
        [eg, *eg_halo, enc_bwd],
        flops=2 * 10**9,
    )
    encoder_gradient, decoder_gradient, lower_gradient, lift_gradient = call(
        widen_kernel,
        [((27, 64, 64), F32), ((27, 64, 128), F32), ((27, 64, 128), F32), ((8, 64, 128), F32)],
        [],
        [core, sums, partner(sums)],
        spaces={0: pltpu.SMEM},
    )
    return (
        jnp.transpose(decoded, (3, 0, 1, 2)),
        jnp.transpose(input_grad, (3, 0, 1, 2)),
        encoder_gradient,
        jnp.transpose(lower_gradient, (0, 2, 1)),
        lift_gradient,
        decoder_gradient,
    )


def solution(mesh):
    size_x, size_y = mesh.devices.shape
    chips = Mesh(mesh.devices.reshape(size_x, size_y // 2, 2), ("gx", "gz", "gc"))
    field = P(None, "gx", ("gz", "gc"), None)
    return jax.shard_map(
        per_device,
        mesh=chips,
        in_specs=(field, P(), P(), P(), P(), field),
        out_specs=(field, field, P(), P(), P(), P()),
        check_vma=False,
    )
```

```python
import math

import jax
import jax.numpy as jnp
from jax import lax
from jax.experimental import pallas as pl
from jax.experimental.pallas import tpu as pltpu
from jax.sharding import Mesh, PartitionSpec as P

F32, BF16 = jnp.float32, jnp.bfloat16
LINK = BF16
GX, GY = ("gx",), ("gz", "gc")
TAPS9 = tuple((a, b) for a in range(3) for b in range(3))


def shifted(piece, axes, step):
    size = math.prod(lax.axis_size(axis) for axis in axes)
    pairs = [(i, i + step) for i in range(size) if 0 <= i + step < size]
    return lax.ppermute(piece, axes, pairs)


def swapped(low, high, axes):
    return shifted(high, axes, 1), shifted(low, axes, -1)


def partner(piece):
    return lax.ppermute(piece, "gc", [(0, 1), (1, 0)])


def exchanged(blocks, wide):
    size_x, size_z = lax.axis_size("gx"), lax.axis_size("gz")
    size_y = size_z
    assert size_x % size_y == 0

    def place(x, y, z, core):
        return ((x * size_y + y) * size_z + z) * 2 + core

    xs, ys, zs = range(size_x // size_y), range(size_y), range(size_z)
    if wide:
        groups = [[place(x, y, z, 0) for x in xs for y in ys] for z in zs]
        groups += [[place(x, y, z, 1) for x in xs for z in zs] for y in ys]
    else:
        groups = [[place(x, y, z, 0) for z in zs] for x in xs for y in ys]
        groups += [[place(x, y, z, 1) for y in ys] for x in xs for z in zs]
    return lax.all_to_all(blocks, ("gx", "gz", "gc"), 0, 0, axis_index_groups=groups)


def call(kernel, outs, scratch, operands, spaces=(), flops=10**6):
    return pl.pallas_call(
        kernel,
        out_shape=[jax.ShapeDtypeStruct(s, d) for s, d in outs],
        in_specs=[
            pl.BlockSpec(memory_space=dict(spaces).get(i, pltpu.VMEM)) for i in range(len(operands))
        ],
        out_specs=[pl.BlockSpec(memory_space=pltpu.VMEM)] * len(outs),
        scratch_shapes=[s if d is None else pltpu.VMEM(s, d) for s, d in scratch],
        compiler_params=pltpu.CompilerParams(vmem_limit_bytes=40 * 2**20),
        cost_estimate=pl.CostEstimate(flops=flops, bytes_accessed=10**4, transcendentals=0),
    )(*operands)


def nn(a, b):
    return lax.dot_general(a, b, (((1,), (0,)), ((), ())), preferred_element_type=F32)


def nt(a, b):
    return lax.dot_general(a, b, (((1,), (1,)), ((), ())), preferred_element_type=F32)


def tn(a, b):
    return lax.dot_general(a, b, (((0,), (0,)), ((), ())), preferred_element_type=F32)


def nn_weight(ref):
    rows = [jnp.concatenate([ref[3 * ab + c] for c in range(3)], -1) for ab in range(9)]
    return jnp.concatenate(rows, 0)


def nt_weight(ref):
    rows = [jnp.concatenate([ref[3 * ab + c] for ab in range(9)], -1) for c in range(3)]
    return jnp.concatenate(rows, 0)


def stacked(ref, x, nx, ny, adjoint, y=0):
    pieces = []
    for a, b in TAPS9:
        i, j = (x + 2 - a, y + 2 - b) if adjoint else (x + a, y + b)
        piece = ref[i : i + nx, j : j + ny]
        pieces.append(piece.reshape(nx * ny * piece.shape[2], piece.shape[3]))
    return jnp.concatenate(pieces, -1)


def zshift(value, step, depth):
    rows = value.shape[0]
    z = lax.broadcasted_iota(jnp.int32, value.shape, 0) & (depth - 1)
    moved = pltpu.roll(value, step % rows, 0)
    return jnp.where(z == (0 if step > 0 else depth - 1), 0.0, moved)


def combined(parts, depth, adjoint):
    ch = parts.shape[1] // 3
    step = -1 if adjoint else 1
    return (
        zshift(parts[:, :ch], step, depth)
        + parts[:, ch : 2 * ch]
        + zshift(parts[:, 2 * ch :], -step, depth)
    )


def ztaps(value, depth, adjoint):
    step = -1 if adjoint else 1
    return jnp.concatenate(
        [
            zshift(value, step, depth).astype(BF16),
            value.astype(BF16),
            zshift(value, -step, depth).astype(BF16),
        ],
        -1,
    )


def stack_kernel(first_ref, enc_ref, low_ref, dec_ref, lift_ref, *outs):
    for ref, forward, backward in (
        (enc_ref, nt_weight, nn_weight),
        (low_ref, nn_weight, nt_weight),
        (dec_ref, nt_weight, nn_weight),
    ):
        outs[0][...] = forward(ref)
        outs[1][...] = backward(ref)
        outs = outs[2:]
    outs[0][...] = lift_ref[...]


def pack_x_kernel(f_in, c_in, f_ref, c_ref, lo_ref, hi_ref, lo2_ref, hi2_ref):
    f_ref[...] = f_in[...]
    c_ref[...] = c_in[...]
    paired = [jnp.concatenate([f_in[x, 0:4], f_in[x, 4:8]], -1) for x in range(2)]
    for x, out, out2 in ((0, lo_ref, lo2_ref), (1, hi_ref, hi2_ref)):
        out[0:8] = jnp.concatenate([f_in[x], c_in[x]], -1)
        out[8:12] = paired[1 - x]
        out2[...] = paired[x]


def pack_y_kernel(f_ref, c_ref, xlo, xhi, xlo2, xhi2, lo_ref, hi_ref):
    for first, out in ((0, lo_ref), (1, hi_ref)):
        at = slice(first, first + 7)
        out[0] = xlo[at]
        for x in range(2):
            out[1 + x] = jnp.concatenate([f_ref[x, at], c_ref[x, at]], -1)
        out[3] = xhi[at]
        for k, far, near in ((4, xlo2[...], xlo[8:12]), (5, xhi[8:12], xhi2[...])):
            pair = [jnp.concatenate([v[..., :64], v[..., 64:]], 0)[at] for v in (far, near)]
            out[k] = jnp.concatenate(pair, -1)


def encode_kernel(
    f_ref, ylo, yhi, xlo, xhi, xlo2, xhi2, inside, w_ref, fx_ref, enc_ref, slope_ref, pool_ref, tmp
):
    fx_ref[3:5, 7:15] = f_ref[...]
    fx_ref[2, 7:15] = xlo[0:8, :, :64]
    fx_ref[5, 7:15] = xhi[0:8, :, :64]
    for x, ref, first in ((1, xlo, 8), (6, xhi, 8), (0, xlo2, 0), (7, xhi2, 0)):
        fx_ref[x, 7:11] = ref[first : first + 4, :, :64]
        fx_ref[x, 11:15] = ref[first : first + 4, :, 64:]
    for y, ref in ((0, ylo), (15, yhi)):
        at = slice(y, y + 7)
        fx_ref[2:6, at] = ref[0:4, :, :, :64]
        for x, k in ((0, 4), (6, 5)):
            fx_ref[x, at] = ref[k, :, :, :64]
            fx_ref[x + 1, at] = ref[k, :, :, 64:]
    weight = w_ref[...]

    def edged(value, x):
        if x < 2 or x > 3:
            value = value * inside[0 if x < 2 else 1]
        return jnp.concatenate(
            [value[0:32] * inside[2], value[32:288], value[288:320] * inside[3]], 0
        )

    for x in range(6):
        pre = combined(nt(stacked(fx_ref, x, 1, 20, False), weight), 32, False)
        sigma = jax.nn.sigmoid(pre)
        enc = (pre * sigma).astype(BF16).astype(F32)
        near, slope = pre[160:480], sigma[160:480]
        slope_ref[x] = edged(slope * (1.0 + near * (1.0 - slope)), x)
        if 0 < x < 5:
            enc_ref[x - 1] = edged(enc[160:480], x).astype(BF16).reshape(10, 32, 64)
        wide = enc.reshape(10, 2, 32, 64)
        part = wide[:, 0] + wide[:, 1]
        if x % 2 == 0:
            held = part
            continue
        tmp[...] = (held + part).reshape(320, 64)
        pooled = tmp[pl.ds(0, 160, stride=2), :] + tmp[pl.ds(1, 160, stride=2), :]
        pooled = pooled * (0.125 if x == 3 else 0.125 * inside[0 if x == 1 else 1])
        pool_ref[x // 2, 3:7] = pooled[48:112].astype(BF16).reshape(4, 16, 64)
        pool_ref[x // 2, 0:3] = (pooled[0:48] * inside[2]).astype(BF16).reshape(3, 16, 64)
        pool_ref[x // 2, 7:10] = (pooled[112:160] * inside[3]).astype(BF16).reshape(3, 16, 64)


def joined_grad_kernel(
    c_ref, ylo, yhi, xlo, xhi, w_ref, lift_ref, cx_ref, jg_ref, kids_ref, adj_ref, tmp
):
    cx_ref[1:3, 5:13] = c_ref[...]
    cx_ref[0, 5:13] = xlo[0:8, :, 64:]
    cx_ref[3, 5:13] = xhi[0:8, :, 64:]
    cx_ref[:, 0:5] = ylo[0:4, 2:7, :, 64:]
    cx_ref[:, 13:18] = yhi[0:4, 0:5, :, 64:]
    weight = w_ref[...]
    for x in range(2):
        grad = combined(nn(stacked(cx_ref, x, 1, 16, True), weight), 32, True)
        grad = grad.astype(BF16)
        jg_ref[x] = grad[96:416, :64]
        tmp[pl.ds(x * 512, 512), :] = grad.astype(F32)
    kids = []
    for p in range(2):
        for q in range(2):
            for r in range(2):
                rows = [
                    tmp[pl.ds(p * 512 + (2 * j + q) * 32 + r, 16, stride=2), :] for j in range(8)
                ]
                kids.append(jnp.concatenate(rows, 0)[:, 64:])
    kids = jnp.concatenate(kids, -1).astype(BF16)
    kids_ref[...] = kids[32:96]
    adj_ref[...] = nn(kids, lift_ref[...].reshape(512, 128))


def halver(halves):
    chunk = halves.shape[2]

    def put(row, block):
        at = pl.ds(row % chunk, block.shape[0])
        halves[row // chunk % 2, row // (2 * chunk), at, :] = block.astype(LINK)

    return put


def lower_kernel(px, inside, w_ref, adj_ref, la_ref, lg_ref, msg_ref):
    def masked(value):
        first, last = value[0:32] * inside[2], value[96:128] * inside[3]
        return jnp.concatenate([first, value[32:96], last], 0).astype(BF16)

    pre = combined(nn(stacked(px, 0, 1, 8, False), w_ref[...]), 16, False)
    sigma = jax.nn.sigmoid(pre)
    la = masked(pre * sigma)
    lg = masked(adj_ref[...] * (sigma * (1.0 + pre * (1.0 - sigma))))
    la_ref[...] = la[16:112]
    lg_ref[...] = lg
    msg_ref[0:96] = la[16:112]
    msg_ref[96:224] = lg


def doubled(coarse, tmp):
    rows = coarse.shape[0]
    tmp[pl.ds(0, rows, stride=2), :] = coarse
    tmp[pl.ds(1, rows, stride=2), :] = coarse
    wide = tmp[...].reshape(rows // 16, 1, 32, 64)
    return jnp.broadcast_to(wide, (rows // 16, 2, 32, 64)).reshape(4 * rows, 64)


def grads_kernel(px, la_ref, lg_ref, core, lift_ref, kids_ref, cx_ref, enc_ref, *refs):
    (w_ref, slope_ref, jg_ref, fx_ref), refs = refs[:4], refs[4:]
    lifted_ref, keep_ref, send_ref, tmp, halves, enc_halves, wide = refs
    put, put_enc = halver(halves), halver(enc_halves)
    la, lg = la_ref[...], lg_ref[...]
    fine = nt(la, lift_ref[...].reshape(512, 128)).astype(BF16).astype(F32)
    for p in range(2):
        for q in range(2):
            for r in range(2):
                k = 4 * p + 2 * q + r
                for j in range(6):
                    y = 2 * j + q - 1
                    if 0 <= y < 10:
                        tmp[pl.ds((p * 10 + y) * 32 + r, 16, stride=2), :] = fine[
                            16 * j : 16 * j + 16, 64 * k : 64 * k + 64
                        ]
    lifted_ref[...] = tmp[...].astype(BF16).reshape(2, 10, 32, 64)
    lifted = jnp.concatenate([tmp[32:288], tmp[352:608]], 0)
    la, lg = la[16:80], lg[32:96]
    enc = enc_ref[1:3, 1:9].reshape(512, 64).astype(F32)
    joined = ztaps(jnp.concatenate([enc, lifted], -1), 32, False)
    dec = tn(stacked(cx_ref, 0, 2, 8, True, 4), joined)
    for ab in range(9):
        for c in range(3):
            block = dec[64 * ab : 64 * ab + 64, 128 * c : 128 * c + 128]
            put((3 * ab + c) * 64, block)
    low = tn(stacked(px, 0, 1, 4, False, 2), ztaps(lg.astype(F32), 16, True))
    for ab in range(9):
        for c in range(3):
            block = low[64 * ab : 64 * ab + 64, 128 * c : 128 * c + 128]
            put(1728 + (3 * ab + c) * 64, block)
    lift = tn(kids_ref[...], la)
    for k in range(8):
        put(3456 + 64 * k, lift[64 * k : 64 * k + 64])
    for row in (3968, 4032):
        put(row, jnp.zeros((64, 128), F32))
    lg = lg_ref[...].reshape(8, 16, 128)
    source = jnp.concatenate([lg[3 - b : 7 - b].reshape(64, 128) for b in range(3)], -1)
    grad = jnp.zeros((192, 576), F32)
    for a in range(3):
        pg = combined(nt(source, w_ref[:, 384 * a : 384 * a + 384]), 16, True)
        fine = doubled(pg * 0.125, wide)
        parts = []
        for x in (2 * a, 2 * a + 1):
            own = fine if a != 1 else fine + jg_ref[x - 2, 32:288].astype(F32)
            parts.append(own * slope_ref[x, 32:288])
        eg = ztaps(jnp.concatenate(parts, 0), 32, True)
        grad = grad + tn(eg, stacked(fx_ref, 2 * a, 2, 8, False, 6))
    for ab in range(9):
        for c in range(3):
            block = grad[64 * c : 64 * c + 64, 64 * ab : 64 * ab + 64]
            block = jnp.concatenate([block[:32], block[32:]], -1)
            put_enc((3 * ab + c) * 32, block[:16])
            put_enc((3 * ab + c) * 32 + 16, block[16:])
    for row in range(864, 1024, 16):
        put_enc(row, jnp.zeros((16, 128), F32))
    mine, chunk = core[0], halves.shape[2]
    keep_ref[:, :chunk, :] = halves[mine]
    send_ref[:, :chunk, :] = halves[1 - mine]
    keep_ref[:, chunk:, :] = enc_halves[mine]
    send_ref[:, chunk:, :] = enc_halves[1 - mine]


def middle_kernel(f_ref, c_ref, *refs):
    (ylo, yhi, xlo, xhi, xlo2, xhi2, inside, core), refs = refs[:8], refs[8:]
    (enc_w, dec_w, low_w, low_wt, lift), refs = refs[:5], refs[5:]
    (enc, slope, jg, lg, msg, lifted, keep, send), refs = refs[:8], refs[8:]
    (fx, cx, pool, kids, adj, la, tmp, kid_tmp, lift_tmp, halves, enc_halves, wide) = refs
    joined_grad_kernel(c_ref, ylo, yhi, xlo, xhi, dec_w, lift, cx, jg, kids, adj, kid_tmp)
    encode_kernel(
        f_ref, ylo, yhi, xlo, xhi, xlo2, xhi2, inside, enc_w, fx, enc, slope, pool, tmp
    )
    lower_kernel(pool, inside, low_w, adj, la, lg, msg)
    grads_kernel(
        *(pool, la, lg, core, lift, kids, cx, enc, low_wt, slope, jg, fx),
        *(lifted, keep, send, lift_tmp, halves, enc_halves, wide),
    )


def add_kernel(a_ref, b_ref, out_ref):
    out_ref[...] = (a_ref[...].astype(F32) + b_ref[...].astype(F32)).astype(LINK)


def plane(rows):
    return jnp.concatenate([rows[:, :64], rows[:, 64:]], 0).reshape(1, 10, 32, 64)


def encoder_grad_kernel(
    lg_ref, xlo, xhi, w_ref, slope_ref, jg_ref, eg_ref, lo_ref, hi_ref, lx, tmp
):
    lx[0] = xlo[96:224].reshape(8, 16, 128)
    lx[1] = lg_ref[...].reshape(8, 16, 128)
    lx[2] = xhi[96:224].reshape(8, 16, 128)
    pg = combined(nt(stacked(lx, 0, 1, 6, True), w_ref[...]), 16, True)
    fine = doubled(pg.astype(BF16).astype(F32) * 0.125, tmp)[32:352]
    for x, msg in ((0, lo_ref), (1, hi_ref)):
        eg = ((jg_ref[x].astype(F32) + fine) * slope_ref[2 + x]).astype(BF16)
        eg_ref[x] = eg.reshape(10, 32, 64)
        msg[...] = jnp.concatenate([eg[:160], eg[160:]], -1)


def decode_kernel(enc_ref, lifted_ref, xlo, xhi, lift_ref, w_ref, out_ref, jx, tx):
    jx[1:3] = jnp.concatenate([enc_ref[1:3], lifted_ref[...]], -1)
    for p, h in ((1, xlo), (0, xhi)):
        for q in range(2):
            for r in range(2):
                fine = nt(h[0:96], lift_ref[4 * p + 2 * q + r]).astype(BF16).astype(F32)
                for j in range(6):
                    y = 2 * j + q - 1
                    if 0 <= y < 10:
                        tx[pl.ds(32 * y + r, 16, stride=2), :] = fine[16 * j : 16 * j + 16]
        lifted = tx[...].astype(BF16).reshape(1, 10, 32, 64)
        x = 0 if p == 1 else 3
        jx[x : x + 1] = jnp.concatenate([enc_ref[x : x + 1], lifted], -1)
    weight = w_ref[...]
    for x in range(2):
        out = combined(nt(stacked(jx, x, 1, 8, False), weight), 32, False)
        out_ref[x] = out.astype(BF16).reshape(8, 32, 64)


def input_grad_kernel(eg_ref, xlo, xhi, w_ref, out_ref, ex):
    ex[0:1] = plane(xlo[...])
    ex[1:3] = eg_ref[...]
    ex[3:4] = plane(xhi[...])
    weight = w_ref[...]
    for x in range(2):
        out = combined(nn(stacked(ex, x, 1, 8, True), weight), 32, True)
        out_ref[x] = out.astype(BF16).reshape(8, 32, 64)


def sum_kernel(parts_ref, out_ref):
    total = parts_ref[0].astype(F32)
    for k in range(1, parts_ref.shape[0]):
        total = total + parts_ref[k].astype(F32)
    total = total.astype(LINK)
    for k in range(out_ref.shape[0]):
        out_ref[k] = total


def widen_kernel(core, own_ref, other_ref, encoder_ref, decoder_ref, lower_ref, lift_ref):
    own, other = own_ref[...].astype(F32), other_ref[...].astype(F32)
    first = core[0] == 0
    both = jnp.stack([jnp.where(first, own, other), jnp.where(first, other, own)], 1)
    chunk = own.shape[1] // 5 * 4
    sums = both[:, :, :chunk].reshape(4096, 128)
    decoder_ref[...] = sums[0:1728].reshape(27, 64, 128)
    lower_ref[...] = sums[1728:3456].reshape(27, 64, 128)
    lift_ref[...] = sums[3456:3968].reshape(8, 64, 128)
    wide = both[:, :, chunk:].reshape(1024, 128)[:864].reshape(27, 32, 128)
    encoder_ref[:, 0:32, :] = wide[..., :64]
    encoder_ref[:, 32:64, :] = wide[..., 64:]


def per_device(features, encoder_weight, lower_weight, lift_weight, decoder_weight, cotangent):
    f = jnp.transpose(features, (1, 2, 3, 0))
    c = jnp.transpose(cotangent, (1, 2, 3, 0))
    lower_t = jnp.transpose(lower_weight, (0, 2, 1))
    brick, tall = (2, 8, 32, 64), (2, 10, 32, 64)

    size_x, size_z = lax.axis_size("gx"), lax.axis_size("gz")
    at_x, at_y = lax.axis_index("gx"), lax.axis_index(GY)
    inside = jnp.stack([at_x > 0, at_x < size_x - 1, at_y > 0, at_y < 2 * size_z - 1]).astype(F32)
    core = lax.axis_index("gc").reshape(1)

    f, c, lo, hi, lo2, hi2 = call(
        pack_x_kernel,
        [(brick, BF16)] * 2 + [((12, 32, 128), BF16)] * 2 + [((4, 32, 128), BF16)] * 2,
        [],
        [f, c],
    )
    x_halo = swapped(lo, hi, GX)
    far_halo = [shifted(hi2, GX, 2), shifted(lo2, GX, -2)]
    edges = call(
        pack_y_kernel,
        [((6, 7, 32, 128), BF16)] * 2,
        [],
        [f, c, *x_halo, *far_halo],
    )
    y_halo = swapped(*edges, GY)
    enc_fwd, enc_bwd, low_fwd, low_bwd, dec_fwd, dec_bwd, lift = call(
        stack_kernel,
        [
            ((192, 576), BF16),
            ((576, 192), BF16),
            ((576, 384), BF16),
            ((192, 1152), BF16),
            ((192, 1152), BF16),
            ((576, 384), BF16),
            ((8, 64, 128), BF16),
        ],
        [],
        [edges[0], encoder_weight, lower_t, decoder_weight, lift_weight],
        flops=2 * 10**9,
    )
    half = (size_x, 2560 // size_x, 128)
    encoded, slope, jg, lg, edge, lifted, keep, send = call(
        middle_kernel,
        [((4, 10, 32, 64), BF16), ((6, 320, 64), F32), ((2, 320, 64), BF16)]
        + [((128, 128), BF16), ((224, 128), BF16), (tall, BF16), (half, LINK), (half, LINK)],
        [
            ((8, 22, 32, 64), BF16),
            ((4, 18, 32, 64), BF16),
            ((3, 10, 16, 64), BF16),
            ((64, 512), BF16),
            ((128, 128), F32),
            ((96, 128), BF16),
            ((320, 64), F32),
            ((1024, 128), F32),
            ((640, 64), F32),
            ((2, size_x, 2048 // size_x, 128), LINK),
            ((2, size_x, 512 // size_x, 128), LINK),
            ((128, 64), F32),
        ],
        [f, c, *y_halo, *x_halo, *far_halo, inside, core]
        + [enc_fwd, dec_bwd, low_fwd, low_bwd, lift],
        spaces={8: pltpu.SMEM, 9: pltpu.SMEM},
    )
    (sums,) = call(add_kernel, [(half, LINK)], [], [keep, partner(send)])
    sums, edge = lax.optimization_barrier((sums, edge))
    sums = exchanged(sums, True)
    halo = swapped(edge, edge, GX)
    (sums,) = call(sum_kernel, [((size_z,) + half[1:], LINK)], [], [sums])
    sums, halo = lax.optimization_barrier((sums, halo))
    sums = exchanged(sums, False)
    eg, *edges = call(
        encoder_grad_kernel,
        [(tall, BF16)] + [((160, 128), BF16)] * 2,
        [((3, 8, 16, 128), BF16), ((192, 64), F32)],
        [lg, *halo, low_bwd, slope, jg],
    )
    eg_halo = swapped(*edges, GX)
    (sums,) = call(sum_kernel, [(half, LINK)], [], [sums])
    sums, eg_halo = lax.optimization_barrier((sums, eg_halo))
    sums = exchanged(sums, True)
    (decoded,) = call(
        decode_kernel,
        [(brick, BF16)],
        [((4, 10, 32, 128), BF16), ((320, 64), F32)],
        [encoded, lifted, *halo, lift, dec_fwd],
    )
    (input_grad,) = call(
        input_grad_kernel,
        [(brick, BF16)],
        [((4, 10, 32, 64), BF16)],
        [eg, *eg_halo, enc_bwd],
    )
    sums, decoded, input_grad = lax.optimization_barrier((sums, decoded, input_grad))
    encoder_gradient, decoder_gradient, lower_gradient, lift_gradient = call(
        widen_kernel,
        [((27, 64, 64), F32), ((27, 64, 128), F32), ((27, 64, 128), F32), ((8, 64, 128), F32)],
        [],
        [core, sums, partner(sums)],
        spaces={0: pltpu.SMEM},
    )
    return (
        jnp.transpose(decoded, (3, 0, 1, 2)),
        jnp.transpose(input_grad, (3, 0, 1, 2)),
        encoder_gradient,
        jnp.transpose(lower_gradient, (0, 2, 1)),
        lift_gradient,
        decoder_gradient,
    )


def solution(mesh):
    size_x, size_y = mesh.devices.shape
    chips = Mesh(mesh.devices.reshape(size_x, size_y // 2, 2), ("gx", "gz", "gc"))
    field = P(None, "gx", ("gz", "gc"), None)
    return jax.shard_map(
        per_device,
        mesh=chips,
        in_specs=(field, P(), P(), P(), P(), field),
        out_specs=(field, field, P(), P(), P(), P()),
        check_vma=False,
    )
```

```python
import math

import jax
import jax.numpy as jnp
from jax import lax
from jax.experimental import pallas as pl
from jax.experimental.pallas import tpu as pltpu
from jax.sharding import Mesh, PartitionSpec as P

F32, BF16 = jnp.float32, jnp.bfloat16
LINK = BF16
GX, GY = ("gx",), ("gz", "gc")
TAPS9 = tuple((a, b) for a in range(3) for b in range(3))


def shifted(piece, axes, step):
    size = math.prod(lax.axis_size(axis) for axis in axes)
    pairs = [(i, i + step) for i in range(size) if 0 <= i + step < size]
    return lax.ppermute(piece, axes, pairs)


def swapped(low, high, axes):
    return shifted(high, axes, 1), shifted(low, axes, -1)


def partner(piece):
    return lax.ppermute(piece, "gc", [(0, 1), (1, 0)])


def exchanged(blocks, wide):
    size_x, size_z = lax.axis_size("gx"), lax.axis_size("gz")
    size_y = size_z
    assert size_x % size_y == 0

    def place(x, y, z, core):
        return ((x * size_y + y) * size_z + z) * 2 + core

    xs, ys, zs = range(size_x // size_y), range(size_y), range(size_z)
    if wide:
        groups = [[place(x, y, z, 0) for x in xs for y in ys] for z in zs]
        groups += [[place(x, y, z, 1) for x in xs for z in zs] for y in ys]
    else:
        groups = [[place(x, y, z, 0) for z in zs] for x in xs for y in ys]
        groups += [[place(x, y, z, 1) for y in ys] for x in xs for z in zs]
    return lax.all_to_all(blocks, ("gx", "gz", "gc"), 0, 0, axis_index_groups=groups)


def call(kernel, outs, scratch, operands, spaces=(), flops=10**6):
    return pl.pallas_call(
        kernel,
        out_shape=[jax.ShapeDtypeStruct(s, d) for s, d in outs],
        in_specs=[
            pl.BlockSpec(memory_space=dict(spaces).get(i, pltpu.VMEM)) for i in range(len(operands))
        ],
        out_specs=[pl.BlockSpec(memory_space=pltpu.VMEM)] * len(outs),
        scratch_shapes=[s if d is None else pltpu.VMEM(s, d) for s, d in scratch],
        compiler_params=pltpu.CompilerParams(vmem_limit_bytes=40 * 2**20),
        cost_estimate=pl.CostEstimate(flops=flops, bytes_accessed=10**4, transcendentals=0),
    )(*operands)


def nn(a, b):
    return lax.dot_general(a, b, (((1,), (0,)), ((), ())), preferred_element_type=F32)


def nt(a, b):
    return lax.dot_general(a, b, (((1,), (1,)), ((), ())), preferred_element_type=F32)


def tn(a, b):
    return lax.dot_general(a, b, (((0,), (0,)), ((), ())), preferred_element_type=F32)


def nn_weight(ref):
    rows = [jnp.concatenate([ref[3 * ab + c] for c in range(3)], -1) for ab in range(9)]
    return jnp.concatenate(rows, 0)


def nt_weight(ref):
    rows = [jnp.concatenate([ref[3 * ab + c] for ab in range(9)], -1) for c in range(3)]
    return jnp.concatenate(rows, 0)


def stacked(ref, x, nx, ny, adjoint, y=0):
    pieces = []
    for a, b in TAPS9:
        i, j = (x + 2 - a, y + 2 - b) if adjoint else (x + a, y + b)
        piece = ref[i : i + nx, j : j + ny]
        pieces.append(piece.reshape(nx * ny * piece.shape[2], piece.shape[3]))
    return jnp.concatenate(pieces, -1)


def zshift(value, step, depth):
    rows = value.shape[0]
    z = lax.broadcasted_iota(jnp.int32, value.shape, 0) & (depth - 1)
    moved = pltpu.roll(value, step % rows, 0)
    return jnp.where(z == (0 if step > 0 else depth - 1), 0.0, moved)


def combined(parts, depth, adjoint):
    ch = parts.shape[1] // 3
    step = -1 if adjoint else 1
    return (
        zshift(parts[:, :ch], step, depth)
        + parts[:, ch : 2 * ch]
        + zshift(parts[:, 2 * ch :], -step, depth)
    )


def ztaps(value, depth, adjoint):
    step = -1 if adjoint else 1
    return jnp.concatenate(
        [
            zshift(value, step, depth).astype(BF16),
            value.astype(BF16),
            zshift(value, -step, depth).astype(BF16),
        ],
        -1,
    )


def stack_kernel(first_ref, enc_ref, low_ref, dec_ref, lift_ref, *outs):
    for ref, forward, backward in (
        (enc_ref, nt_weight, nn_weight),
        (low_ref, nn_weight, nt_weight),
        (dec_ref, nt_weight, nn_weight),
    ):
        outs[0][...] = forward(ref)
        outs[1][...] = backward(ref)
        outs = outs[2:]
    outs[0][...] = lift_ref[...]


def pack_x_kernel(f_in, c_in, f_ref, c_ref, lo_ref, hi_ref, lo2_ref, hi2_ref):
    f_ref[...] = f_in[...]
    c_ref[...] = c_in[...]
    paired = [jnp.concatenate([f_in[x, 0:4], f_in[x, 4:8]], -1) for x in range(2)]
    for x, out, out2 in ((0, lo_ref, lo2_ref), (1, hi_ref, hi2_ref)):
        out[0:8] = jnp.concatenate([f_in[x], c_in[x]], -1)
        out[8:12] = paired[1 - x]
        out2[...] = paired[x]


def pack_y_kernel(f_ref, c_ref, xlo, xhi, xlo2, xhi2, lo_ref, hi_ref):
    for first, out in ((0, lo_ref), (1, hi_ref)):
        at = slice(first, first + 7)
        out[0] = xlo[at]
        for x in range(2):
            out[1 + x] = jnp.concatenate([f_ref[x, at], c_ref[x, at]], -1)
        out[3] = xhi[at]
        for k, far, near in ((4, xlo2[...], xlo[8:12]), (5, xhi[8:12], xhi2[...])):
            pair = [jnp.concatenate([v[..., :64], v[..., 64:]], 0)[at] for v in (far, near)]
            out[k] = jnp.concatenate(pair, -1)


def encode_kernel(
    f_ref, ylo, yhi, xlo, xhi, xlo2, xhi2, inside, w_ref, fx_ref, enc_ref, slope_ref, pool_ref, tmp
):
    fx_ref[3:5, 7:15] = f_ref[...]
    fx_ref[2, 7:15] = xlo[0:8, :, :64]
    fx_ref[5, 7:15] = xhi[0:8, :, :64]
    for x, ref, first in ((1, xlo, 8), (6, xhi, 8), (0, xlo2, 0), (7, xhi2, 0)):
        fx_ref[x, 7:11] = ref[first : first + 4, :, :64]
        fx_ref[x, 11:15] = ref[first : first + 4, :, 64:]
    for y, ref in ((0, ylo), (15, yhi)):
        at = slice(y, y + 7)
        fx_ref[2:6, at] = ref[0:4, :, :, :64]
        for x, k in ((0, 4), (6, 5)):
            fx_ref[x, at] = ref[k, :, :, :64]
            fx_ref[x + 1, at] = ref[k, :, :, 64:]
    weight = w_ref[...]

    def edged(value, x):
        if x < 2 or x > 3:
            value = value * inside[0 if x < 2 else 1]
        return jnp.concatenate(
            [value[0:32] * inside[2], value[32:288], value[288:320] * inside[3]], 0
        )

    for x in range(6):
        pre = combined(nt(stacked(fx_ref, x, 1, 20, False), weight), 32, False)
        sigma = jax.nn.sigmoid(pre)
        enc = (pre * sigma).astype(BF16).astype(F32)
        near, slope = pre[160:480], sigma[160:480]
        slope_ref[x] = edged(slope * (1.0 + near * (1.0 - slope)), x)
        if 0 < x < 5:
            enc_ref[x - 1] = edged(enc[160:480], x).astype(BF16).reshape(10, 32, 64)
        wide = enc.reshape(10, 2, 32, 64)
        part = wide[:, 0] + wide[:, 1]
        if x % 2 == 0:
            held = part
            continue
        tmp[...] = (held + part).reshape(320, 64)
        pooled = tmp[pl.ds(0, 160, stride=2), :] + tmp[pl.ds(1, 160, stride=2), :]
        pooled = pooled * (0.125 if x == 3 else 0.125 * inside[0 if x == 1 else 1])
        pool_ref[x // 2, 3:7] = pooled[48:112].astype(BF16).reshape(4, 16, 64)
        pool_ref[x // 2, 0:3] = (pooled[0:48] * inside[2]).astype(BF16).reshape(3, 16, 64)
        pool_ref[x // 2, 7:10] = (pooled[112:160] * inside[3]).astype(BF16).reshape(3, 16, 64)


def joined_grad_kernel(c_ref, *refs):
    (ylo, yhi, xlo, xhi), (w_ref, lift_ref) = refs[:4], refs[4:6]
    cx_ref, jg_ref, kids_ref, adj_ref, tmp = refs[6:]
    cx_ref[1:3, 5:13] = c_ref[...]
    cx_ref[0, 5:13] = xlo[0:8, :, 64:]
    cx_ref[3, 5:13] = xhi[0:8, :, 64:]
    cx_ref[:, 0:5] = ylo[0:4, 2:7, :, 64:]
    cx_ref[:, 13:18] = yhi[0:4, 0:5, :, 64:]
    weight = w_ref[...]
    for x in range(2):
        grad = combined(nn(stacked(cx_ref, x, 1, 16, True), weight), 32, True)
        grad = grad.astype(BF16)
        jg_ref[x] = grad[96:416, :64]
        tmp[pl.ds(x * 512, 512), :] = grad.astype(F32)
    kids = []
    for p in range(2):
        for q in range(2):
            for r in range(2):
                rows = [
                    tmp[pl.ds(p * 512 + (2 * j + q) * 32 + r, 16, stride=2), :] for j in range(8)
                ]
                kids.append(jnp.concatenate(rows, 0)[:, 64:])
    kids = jnp.concatenate(kids, -1).astype(BF16)
    kids_ref[...] = kids[32:96]
    adj_ref[...] = nn(kids, lift_ref[...].reshape(512, 128))


def halver(halves):
    chunk = halves.shape[2]

    def put(row, block):
        at = pl.ds(row % chunk, block.shape[0])
        halves[row // chunk % 2, row // (2 * chunk), at, :] = block.astype(LINK)

    return put


def lower_kernel(px, inside, w_ref, adj_ref, la_ref, lg_ref, msg_ref):
    def masked(value):
        first, last = value[0:32] * inside[2], value[96:128] * inside[3]
        return jnp.concatenate([first, value[32:96], last], 0).astype(BF16)

    pre = combined(nn(stacked(px, 0, 1, 8, False), w_ref[...]), 16, False)
    sigma = jax.nn.sigmoid(pre)
    la = masked(pre * sigma)
    lg = masked(adj_ref[...] * (sigma * (1.0 + pre * (1.0 - sigma))))
    la_ref[...] = la[16:112]
    lg_ref[...] = lg
    msg_ref[0:96] = la[16:112]
    msg_ref[96:224] = lg


def doubled(coarse, tmp):
    rows = coarse.shape[0]
    tmp[pl.ds(0, rows, stride=2), :] = coarse
    tmp[pl.ds(1, rows, stride=2), :] = coarse
    wide = tmp[...].reshape(rows // 16, 1, 32, 64)
    return jnp.broadcast_to(wide, (rows // 16, 2, 32, 64)).reshape(4 * rows, 64)


def grads_kernel(px, la_ref, lg_ref, core, lift_ref, kids_ref, cx_ref, enc_ref, *refs):
    (w_ref, slope_ref, jg_ref, fx_ref), refs = refs[:4], refs[4:]
    lifted_ref, keep_ref, send_ref, tmp, halves, enc_halves, wide = refs
    put, put_enc = halver(halves), halver(enc_halves)
    la, lg = la_ref[...], lg_ref[...]
    fine = nt(la, lift_ref[...].reshape(512, 128)).astype(BF16).astype(F32)
    for p in range(2):
        for q in range(2):
            for r in range(2):
                k = 4 * p + 2 * q + r
                for j in range(6):
                    y = 2 * j + q - 1
                    if 0 <= y < 10:
                        tmp[pl.ds((p * 10 + y) * 32 + r, 16, stride=2), :] = fine[
                            16 * j : 16 * j + 16, 64 * k : 64 * k + 64
                        ]
    lifted_ref[...] = tmp[...].astype(BF16).reshape(2, 10, 32, 64)
    lifted = jnp.concatenate([tmp[32:288], tmp[352:608]], 0)
    la, lg = la[16:80], lg[32:96]
    enc = enc_ref[1:3, 1:9].reshape(512, 64).astype(F32)
    joined = ztaps(jnp.concatenate([enc, lifted], -1), 32, False)
    dec = tn(stacked(cx_ref, 0, 2, 8, True, 4), joined)
    for ab in range(9):
        for c in range(3):
            block = dec[64 * ab : 64 * ab + 64, 128 * c : 128 * c + 128]
            put((3 * ab + c) * 64, block)
    low = tn(stacked(px, 0, 1, 4, False, 2), ztaps(lg.astype(F32), 16, True))
    for ab in range(9):
        for c in range(3):
            block = low[64 * ab : 64 * ab + 64, 128 * c : 128 * c + 128]
            put(1728 + (3 * ab + c) * 64, block)
    lift = tn(kids_ref[...], la)
    for k in range(8):
        put(3456 + 64 * k, lift[64 * k : 64 * k + 64])
    for row in (3968, 4032):
        put(row, jnp.zeros((64, 128), F32))
    lg = lg_ref[...].reshape(8, 16, 128)
    source = jnp.concatenate([lg[3 - b : 7 - b].reshape(64, 128) for b in range(3)], -1)
    grad = jnp.zeros((192, 576), F32)
    for a in range(3):
        pg = combined(nt(source, w_ref[:, 384 * a : 384 * a + 384]), 16, True)
        fine = doubled(pg * 0.125, wide)
        parts = []
        for x in (2 * a, 2 * a + 1):
            own = fine if a != 1 else fine + jg_ref[x - 2, 32:288].astype(F32)
            parts.append(own * slope_ref[x, 32:288])
        eg = ztaps(jnp.concatenate(parts, 0), 32, True)
        grad = grad + tn(eg, stacked(fx_ref, 2 * a, 2, 8, False, 6))
    for ab in range(9):
        for c in range(3):
            block = grad[64 * c : 64 * c + 64, 64 * ab : 64 * ab + 64]
            block = jnp.concatenate([block[:32], block[32:]], -1)
            put_enc((3 * ab + c) * 32, block[:16])
            put_enc((3 * ab + c) * 32 + 16, block[16:])
    for row in range(864, 1024, 16):
        put_enc(row, jnp.zeros((16, 128), F32))
    mine, chunk = core[0], halves.shape[2]
    keep_ref[:, :chunk, :] = halves[mine]
    send_ref[:, :chunk, :] = halves[1 - mine]
    keep_ref[:, chunk:, :] = enc_halves[mine]
    send_ref[:, chunk:, :] = enc_halves[1 - mine]


def add_kernel(a_ref, b_ref, out_ref):
    out_ref[...] = (a_ref[...].astype(F32) + b_ref[...].astype(F32)).astype(LINK)


def plane(rows):
    return jnp.concatenate([rows[:, :64], rows[:, 64:]], 0).reshape(1, 10, 32, 64)


def encoder_grad_kernel(
    lg_ref, xlo, xhi, w_ref, slope_ref, jg_ref, eg_ref, lo_ref, hi_ref, lx, tmp
):
    lx[0] = xlo[96:224].reshape(8, 16, 128)
    lx[1] = lg_ref[...].reshape(8, 16, 128)
    lx[2] = xhi[96:224].reshape(8, 16, 128)
    pg = combined(nt(stacked(lx, 0, 1, 6, True), w_ref[...]), 16, True)
    fine = doubled(pg.astype(BF16).astype(F32) * 0.125, tmp)[32:352]
    for x, msg in ((0, lo_ref), (1, hi_ref)):
        eg = ((jg_ref[x].astype(F32) + fine) * slope_ref[2 + x]).astype(BF16)
        eg_ref[x] = eg.reshape(10, 32, 64)
        msg[...] = jnp.concatenate([eg[:160], eg[160:]], -1)


def decode_kernel(enc_ref, lifted_ref, xlo, xhi, lift_ref, w_ref, out_ref, jx, tx):
    jx[1:3] = jnp.concatenate([enc_ref[1:3], lifted_ref[...]], -1)
    for p, h in ((1, xlo), (0, xhi)):
        for q in range(2):
            for r in range(2):
                fine = nt(h[0:96], lift_ref[4 * p + 2 * q + r]).astype(BF16).astype(F32)
                for j in range(6):
                    y = 2 * j + q - 1
                    if 0 <= y < 10:
                        tx[pl.ds(32 * y + r, 16, stride=2), :] = fine[16 * j : 16 * j + 16]
        lifted = tx[...].astype(BF16).reshape(1, 10, 32, 64)
        x = 0 if p == 1 else 3
        jx[x : x + 1] = jnp.concatenate([enc_ref[x : x + 1], lifted], -1)
    weight = w_ref[...]
    for x in range(2):
        out = combined(nt(stacked(jx, x, 1, 8, False), weight), 32, False)
        out_ref[x] = out.astype(BF16).reshape(8, 32, 64)


def input_grad_kernel(eg_ref, xlo, xhi, w_ref, out_ref, ex):
    ex[0:1] = plane(xlo[...])
    ex[1:3] = eg_ref[...]
    ex[3:4] = plane(xhi[...])
    weight = w_ref[...]
    for x in range(2):
        out = combined(nn(stacked(ex, x, 1, 8, True), weight), 32, True)
        out_ref[x] = out.astype(BF16).reshape(8, 32, 64)


def sum_kernel(parts_ref, out_ref):
    total = parts_ref[0].astype(F32)
    for k in range(1, parts_ref.shape[0]):
        total = total + parts_ref[k].astype(F32)
    total = total.astype(LINK)
    for k in range(out_ref.shape[0]):
        out_ref[k] = total


def widen_kernel(core, own_ref, other_ref, encoder_ref, decoder_ref, lower_ref, lift_ref):
    own, other = own_ref[...].astype(F32), other_ref[...].astype(F32)
    first = core[0] == 0
    both = jnp.stack([jnp.where(first, own, other), jnp.where(first, other, own)], 1)
    chunk = own.shape[1] // 5 * 4
    sums = both[:, :, :chunk].reshape(4096, 128)
    decoder_ref[...] = sums[0:1728].reshape(27, 64, 128)
    lower_ref[...] = sums[1728:3456].reshape(27, 64, 128)
    lift_ref[...] = sums[3456:3968].reshape(8, 64, 128)
    wide = both[:, :, chunk:].reshape(1024, 128)[:864].reshape(27, 32, 128)
    encoder_ref[:, 0:32, :] = wide[..., :64]
    encoder_ref[:, 32:64, :] = wide[..., 64:]


def per_device(features, encoder_weight, lower_weight, lift_weight, decoder_weight, cotangent):
    f = jnp.transpose(features, (1, 2, 3, 0))
    c = jnp.transpose(cotangent, (1, 2, 3, 0))
    lower_t = jnp.transpose(lower_weight, (0, 2, 1))
    brick, tall = (2, 8, 32, 64), (2, 10, 32, 64)

    size_x, size_z = lax.axis_size("gx"), lax.axis_size("gz")
    at_x, at_y = lax.axis_index("gx"), lax.axis_index(GY)
    inside = jnp.stack([at_x > 0, at_x < size_x - 1, at_y > 0, at_y < 2 * size_z - 1]).astype(F32)
    core = lax.axis_index("gc").reshape(1)

    f, c, lo, hi, lo2, hi2 = call(
        pack_x_kernel,
        [(brick, BF16)] * 2 + [((12, 32, 128), BF16)] * 2 + [((4, 32, 128), BF16)] * 2,
        [],
        [f, c],
    )
    x_halo = swapped(lo, hi, GX)
    far_halo = [shifted(hi2, GX, 2), shifted(lo2, GX, -2)]
    edges = call(
        pack_y_kernel,
        [((6, 7, 32, 128), BF16)] * 2,
        [],
        [f, c, *x_halo, *far_halo],
    )
    y_halo = swapped(*edges, GY)
    enc_fwd, enc_bwd, low_fwd, low_bwd, dec_fwd, dec_bwd, lift = call(
        stack_kernel,
        [
            ((192, 576), BF16),
            ((576, 192), BF16),
            ((576, 384), BF16),
            ((192, 1152), BF16),
            ((192, 1152), BF16),
            ((576, 384), BF16),
            ((8, 64, 128), BF16),
        ],
        [],
        [edges[0], encoder_weight, lower_t, decoder_weight, lift_weight],
        spaces={0: pltpu.HBM},
        flops=2 * 10**9,
    )
    fx, encoded, slope, pooled = call(
        encode_kernel,
        [((8, 22, 32, 64), BF16), ((4, 10, 32, 64), BF16)]
        + [((6, 320, 64), F32), ((3, 10, 16, 64), BF16)],
        [((320, 64), F32)],
        [f, *y_halo, *x_halo, *far_halo, inside, enc_fwd],
        spaces={7: pltpu.SMEM},
    )
    cx, jg, kids, adj = call(
        joined_grad_kernel,
        [
            ((4, 18, 32, 64), BF16),
            ((2, 320, 64), BF16),
            ((64, 512), BF16),
            ((128, 128), F32),
        ],
        [((1024, 128), F32)],
        [c, *y_halo, *x_halo, dec_bwd, lift],
    )
    half = (size_x, 2560 // size_x, 128)
    la, lg, edge = call(
        lower_kernel,
        [((96, 128), BF16), ((128, 128), BF16), ((224, 128), BF16)],
        [],
        [pooled, inside, low_fwd, adj],
        spaces={1: pltpu.SMEM},
    )
    lifted, keep, send = call(
        grads_kernel,
        [(tall, BF16), (half, LINK), (half, LINK)],
        [
            ((640, 64), F32),
            ((2, size_x, 2048 // size_x, 128), LINK),
            ((2, size_x, 512 // size_x, 128), LINK),
            ((128, 64), F32),
        ],
        [pooled, la, lg, core, lift, kids, cx, encoded, low_bwd, slope, jg, fx],
        spaces={3: pltpu.SMEM},
    )
    (sums,) = call(add_kernel, [(half, LINK)], [], [keep, partner(send)])
    sums, edge = lax.optimization_barrier((sums, edge))
    sums = exchanged(sums, True)
    halo = swapped(edge, edge, GX)
    (sums,) = call(sum_kernel, [((size_z,) + half[1:], LINK)], [], [sums])
    sums, halo = lax.optimization_barrier((sums, halo))
    sums = exchanged(sums, False)
    eg, *edges = call(
        encoder_grad_kernel,
        [(tall, BF16)] + [((160, 128), BF16)] * 2,
        [((3, 8, 16, 128), BF16), ((192, 64), F32)],
        [lg, *halo, low_bwd, slope, jg],
    )
    eg_halo = swapped(*edges, GX)
    (sums,) = call(sum_kernel, [(half, LINK)], [], [sums])
    sums, eg_halo = lax.optimization_barrier((sums, eg_halo))
    sums = exchanged(sums, True)
    (decoded,) = call(
        decode_kernel,
        [(brick, BF16)],
        [((4, 10, 32, 128), BF16), ((320, 64), F32)],
        [encoded, lifted, *halo, lift, dec_fwd],
    )
    (input_grad,) = call(
        input_grad_kernel,
        [(brick, BF16)],
        [((4, 10, 32, 64), BF16)],
        [eg, *eg_halo, enc_bwd],
    )
    sums, decoded, input_grad = lax.optimization_barrier((sums, decoded, input_grad))
    encoder_gradient, decoder_gradient, lower_gradient, lift_gradient = call(
        widen_kernel,
        [((27, 64, 64), F32), ((27, 64, 128), F32), ((27, 64, 128), F32), ((8, 64, 128), F32)],
        [],
        [core, sums, partner(sums)],
        spaces={0: pltpu.SMEM},
    )
    return (
        jnp.transpose(decoded, (3, 0, 1, 2)),
        jnp.transpose(input_grad, (3, 0, 1, 2)),
        encoder_gradient,
        jnp.transpose(lower_gradient, (0, 2, 1)),
        lift_gradient,
        decoder_gradient,
    )


def solution(mesh):
    size_x, size_y = mesh.devices.shape
    chips = Mesh(mesh.devices.reshape(size_x, size_y // 2, 2), ("gx", "gz", "gc"))
    field = P(None, "gx", ("gz", "gc"), None)
    return jax.shard_map(
        per_device,
        mesh=chips,
        in_specs=(field, P(), P(), P(), P(), field),
        out_specs=(field, field, P(), P(), P(), P()),
        check_vma=False,
    )
```
